256 devices in a mesh: az: 8 (over x, y_lo), rng: 32 (over z, y_hi, core).
Axes of the slice: x: 4, y: 4 (y_hi: 2, y_lo: 2; y = y_hi * 2 + y_lo), z: 8, core: 2. Of those that a mesh axis runs over, the one named last changes fastest.
Arguments:
- echoes: bfloat16 [2, 256, 32, 4096], P(None, 'az', None, 'rng'), may hold values from -12 to 12
- arc_start: int32 [64], replicated, may hold values from 0 to 255, as said below
- arc_offsets: int32 [64, 16], replicated, may hold values from 0 to 63, as said below
- doppler_bins: int32 [64, 16], replicated, may hold values from 0 to 31
- steer_angles: float32 [64, 16], replicated, may hold values from -3.140625 to 3.140625
- train_mask: int32 [64, 32], P('az', 'rng'), may hold values from 0 to 1, as said below
Outputs:
- smoothed: float32 [64, 16, 4096], P('az', None, 'rng')
The draws below stay inside these ranges and needn't reach their ends.
Inputs may be any that keep to these rules, and one draw needn't show every extreme that they name: `arc_start`: beam b's arc begins at column (b * 4 - 64 / 2 + j) mod 256 for some j with 0 <= j < 4. `arc_offsets`: each row holds 16 distinct offsets, ascending. `train_mask`: the last block of every beam is a training block.
All inputs are finite; a program needn't handle non-finite values.
Results may differ from the reference program's by a relative error of at most 0.0035.
Values may be sent and summed in bfloat16 or wider, within the bound.
No kernel may reach another device: no remote copies, remote signals or barrier semaphores. Data moves between devices by JAX's collectives and lax.ppermute only.
A program may use at most 64 MiB of HBM per device.

```python
import jax
import jax.numpy as jnp
from jax import lax

COLS = 256
PULSES = 32
ARC = 64
SEL = 16
BINS = 3
BEAMS = 64
DBINS = 16
BLK = 128
RANGE = 4096
NBLK = 32


PATCHES = 128


CLUTTER_LEVEL = 2.0


def clutter_steering(patch_key):
    jitter = jax.random.uniform(patch_key, (PATCHES,), jnp.float32, 0.0, 1.0)
    azimuth = 2.0 * jnp.pi * (jnp.arange(PATCHES, dtype=jnp.float32) + jitter) / PATCHES
    col_angle = 2.0 * jnp.pi * jnp.arange(COLS, dtype=jnp.float32) / COLS
    pulse_ids = jnp.arange(PULSES, dtype=jnp.float32)
    spatial = COLS / 2.0 * jnp.cos(col_angle[:, None, None] - azimuth[None, None, :])
    temporal = jnp.pi * jnp.cos(azimuth)[None, None, :] * pulse_ids[None, :, None]
    phase = (spatial + temporal).reshape(COLS * PULSES, PATCHES)
    return (jnp.cos(phase), jnp.sin(phase))


def clutter_field(steer_re, steer_im, amp_re, amp_im):
    real_part = jnp.dot(steer_re, amp_re, precision=lax.Precision.HIGHEST) - jnp.dot(steer_im, amp_im, precision=lax.Precision.HIGHEST)
    imag_part = jnp.dot(steer_re, amp_im, precision=lax.Precision.HIGHEST) + jnp.dot(steer_im, amp_re, precision=lax.Precision.HIGHEST)
    return jnp.stack([real_part, imag_part], 0).reshape(2, COLS, PULSES, RANGE)


def draw_echoes(key, part):
    base_key = jax.random.fold_in(key, 11)
    noise_key = jax.random.fold_in(base_key, 0)
    patch_key = jax.random.fold_in(base_key, 2)
    amp_key = jax.random.fold_in(base_key, 3)
    array_shape = (2, COLS, PULSES, RANGE)
    position = jnp.arange(RANGE, dtype=jnp.float32) / RANGE
    steer_re, steer_im = clutter_steering(patch_key)
    amp_scale = CLUTTER_LEVEL / PATCHES ** 0.5
    amplitudes = jax.random.normal(amp_key, (2, PATCHES, RANGE), jnp.float32) * amp_scale
    noise = jnp.clip(jax.random.normal(noise_key, array_shape, jnp.float32), -5.0, 5.0)
    values = noise + clutter_field(steer_re, steer_im, amplitudes[0], amplitudes[1])
    values = values * jnp.exp(0.6 * position)
    return jnp.clip(values, -12.0, 12.0).astype(jnp.bfloat16)


def draw_arc_start(key, part):
    spacing = COLS // BEAMS
    jitter = jax.random.randint(jax.random.fold_in(key, 12), (BEAMS,), 0, spacing)
    centre = jnp.arange(BEAMS, dtype=jnp.int32) * spacing
    return ((centre - ARC // 2 + jitter) % COLS).astype(jnp.int32)


def draw_arc_offsets(key, part):
    beam_keys = jax.random.split(jax.random.fold_in(key, 13), BEAMS)
    orders = jax.vmap(lambda single: jax.random.permutation(single, ARC))(beam_keys)
    return jnp.sort(orders[:, :SEL], axis=1).astype(jnp.int32)


def draw_train_mask(key, part):
    block_ids = jnp.arange(NBLK, dtype=jnp.int32)
    chance = 25 + 70 * block_ids // max(NBLK - 1, 1)
    rolls = jax.random.randint(jax.random.fold_in(key, 14), (BEAMS, NBLK), 0, 100)
    kept = jnp.where(block_ids[None, :] == NBLK - 1, 1, (rolls < chance[None, :]).astype(jnp.int32))
    return kept.astype(jnp.int32)


def plant(drawn, own_key, low, high):
    extent = drawn.shape
    spot = [jax.random.randint(jax.random.fold_in(own_key, axis), (), 0, extent[axis]) for axis in range(len(extent))]
    drawn = drawn.at[tuple(spot)].set(low)
    longest = extent.index(max(extent))
    spot[longest] = (spot[longest] + 1) % extent[longest]
    return drawn.at[tuple(spot)].set(high)


def setup_inputs(seed: int = 0) -> dict:
    arg_keys = jax.random.split(jax.random.key(seed), 7)
    return {
        "echoes": draw_echoes(jax.random.fold_in(arg_keys[6], 71), 0),
        "arc_start": draw_arc_start(jax.random.fold_in(arg_keys[6], 71), 0),
        "arc_offsets": draw_arc_offsets(jax.random.fold_in(arg_keys[6], 71), 0),
        "doppler_bins": plant(jax.random.randint(arg_keys[3], (BEAMS, DBINS), 0, PULSES), jax.random.fold_in(arg_keys[3], 1), 0, PULSES - 1).astype(jnp.int32),
        "steer_angles": jnp.clip(jax.random.uniform(arg_keys[4], (BEAMS, SEL), jnp.float32, -3.140625, 3.140625), -3.140625, 3.140625),
        "train_mask": draw_train_mask(jax.random.fold_in(arg_keys[6], 71), 0),
    }


LOADING = 0.1

def doppler_table():
    freq_ids = jnp.arange(PULSES, dtype=jnp.int32)
    phase_steps = freq_ids[:, None] * freq_ids[None, :] % PULSES
    phase_angle = -2.0 * jnp.pi / PULSES * phase_steps.astype(jnp.float32)
    return (jnp.cos(phase_angle).astype(jnp.bfloat16), jnp.sin(phase_angle).astype(jnp.bfloat16))

def snapshot(beam_cols, centers, beam_angle, table_re, table_im):
    num_sel = beam_cols.shape[1]
    num_pulses = beam_cols.shape[2]
    num_cells = beam_cols.shape[3]
    num_chan = centers.shape[0]
    bin_ids = ((centers[:, None] + jnp.arange(BINS, dtype=jnp.int32)[None, :] - BINS // 2) % num_pulses).reshape(-1)
    bin_pick = (jnp.arange(num_pulses, dtype=jnp.int32)[None, :] == bin_ids[:, None]).astype(jnp.bfloat16)
    wt_real = jnp.dot(bin_pick.astype(jnp.float32), table_re.astype(jnp.float32), preferred_element_type=jnp.float32).astype(jnp.bfloat16)
    wt_imag = jnp.dot(bin_pick.astype(jnp.float32), table_im.astype(jnp.float32), preferred_element_type=jnp.float32).astype(jnp.bfloat16)
    stacked_table = jnp.concatenate([jnp.concatenate([wt_real, -wt_imag], 1), jnp.concatenate([wt_imag, wt_real], 1)], 0)
    flat_cols = jnp.transpose(beam_cols, (0, 2, 1, 3)).reshape(2 * num_pulses, num_sel * num_cells)
    spectrum = jnp.dot(stacked_table.astype(jnp.float32), flat_cols.astype(jnp.float32), preferred_element_type=jnp.float32).reshape(2, num_chan, BINS, num_sel, num_cells)
    cosine = jnp.cos(beam_angle)[None, None, :, None]
    sine_part = jnp.sin(beam_angle)[None, None, :, None]
    part_real = cosine * spectrum[0] - sine_part * spectrum[1]
    part_imag = sine_part * spectrum[0] + cosine * spectrum[1]
    joined = jnp.concatenate([part_real.reshape(num_chan, BINS * num_sel, num_cells), part_imag.reshape(num_chan, BINS * num_sel, num_cells)], 1)
    return joined.astype(jnp.bfloat16)

def weights_from_blocks(block_a, block_b, train_count):
    dof_size = block_a.shape[0]
    embedded = jnp.concatenate([jnp.concatenate([block_a, -block_b], 1), jnp.concatenate([block_b, block_a], 1)], 0) / train_count
    loading_level = LOADING * jnp.trace(block_a) / (train_count * dof_size)
    embedded = embedded + loading_level * jnp.eye(2 * dof_size, dtype=jnp.float32)
    factor = jnp.linalg.cholesky(embedded)
    steering = (jnp.arange(2 * dof_size, dtype=jnp.int32)[:, None] // dof_size == jnp.arange(2, dtype=jnp.int32)[None, :]).astype(jnp.float32)
    solved = jax.scipy.linalg.cho_solve((factor, True), steering)
    quiescent = jnp.sum(solved[:dof_size, 0])
    return (solved.T.astype(jnp.bfloat16), quiescent)

def reference(echoes, arc_start, arc_offsets, doppler_bins, steer_angles, train_mask):
    table_re, table_im = doppler_table()

    def per_beam(packed):
        start, offsets, centers, beam_angle, mask_row = packed
        col_index = ((start + offsets) % COLS).astype(jnp.int32)
        beam_cols = jnp.take(echoes, col_index, axis=1)
        snapshots = snapshot(beam_cols, centers, beam_angle, table_re, table_im)
        cell_mask = jnp.repeat(mask_row, BLK).astype(jnp.bfloat16)
        train_count = (BLK * jnp.sum(mask_row)).astype(jnp.float32)

        def per_channel(single):
            gram_sum = jnp.dot((single * cell_mask[None, :]).astype(jnp.float32), single.T.astype(jnp.float32), preferred_element_type=jnp.float32)
            dof_size = gram_sum.shape[0] // 2
            block_a = gram_sum[:dof_size, :dof_size] + gram_sum[dof_size:, dof_size:]
            block_b = gram_sum[dof_size:, :dof_size] - gram_sum[:dof_size, dof_size:]
            adapted, quiescent = weights_from_blocks(block_a, block_b, train_count)
            projected = jnp.dot(adapted.astype(jnp.float32), single.astype(jnp.float32), preferred_element_type=jnp.float32)
            return (projected[0] * projected[0] + projected[1] * projected[1]) / quiescent
        return lax.map(per_channel, snapshots)
    power_map = lax.map(per_beam, (arc_start, arc_offsets, doppler_bins, steer_angles, train_mask))
    padded = jnp.pad(power_map, ((0, 0), (0, 0), (1, 1)))
    row_sums = padded[:, :, :-2] + padded[:, :, 1:-1] + padded[:, :, 2:]
    return (jnp.roll(row_sums, 1, 0) + row_sums + jnp.roll(row_sums, -1, 0)) / 9.0
```

```python
import functools

import jax
import jax.numpy as jnp
import numpy as np
from jax import lax
from jax.experimental import pallas as pl
from jax.experimental.pallas import tpu as pltpu
from jax.sharding import PartitionSpec as P

COLS = 256
ARC = 64
BINS = 3
BEAMS = 64
BLK = 128
PULSES = 32
SEL = 16
DBINS = 16
DOF = BINS * SEL
OWN_COLS = 32
OWN_BEAMS = 8
CELLS = 128
GROUPS = 16
LANES = 128
SLOTS = PULSES + 3
LOADING = 0.1
F32 = jnp.float32
BF16 = jnp.bfloat16
TRANSPOSED = (((1,), (1,)), ((), ()))


def table_array():
    ids = np.arange(PULSES)
    steps = (ids[:, None] * ids[None, :] % PULSES).astype(np.float32)
    angle = np.float32(-2.0 * np.pi / PULSES) * steps
    real, imag = np.cos(angle), np.sin(angle)
    return np.concatenate(
        [np.concatenate([real, -imag], 1), np.concatenate([imag, real], 1)], 0
    ).astype(jnp.bfloat16)


def lane_ids(rows):
    return lax.broadcasted_iota(jnp.int32, (rows, LANES), 1)


def own_group():
    place = lax.axis_index("rng")
    bits = [lax.rem(lax.div(place, 1 << bit), 2) for bit in range(4)]
    return bits[0] * 8 + bits[1] * 4 + bits[2] * 2 + bits[3]


def exclusive(left, right):
    return lax.bitwise_xor(left, right)


def gram_kernel(
    start_ref, offset_ref, bins_ref, mask_ref, cos_ref, sin_ref,
    table_ref, low_ref, own_ref, high_ref,
    snap_ref, keep_ref, send_ref,
    spec_ref, wide_ref, minus_ref,
):
    az = lax.axis_index("az")
    mine = own_group()
    table = table_ref[...]

    def transform(pair, carry):
        for part, ref in enumerate((low_ref, own_ref, high_ref)):
            blocks = [
                jnp.concatenate([ref[0, 2 * pair + one], ref[1, 2 * pair + one]], 0)
                for one in range(2)
            ]
            both = jnp.dot(
                table, jnp.concatenate(blocks, 1), preferred_element_type=F32
            )
            spec_ref[part * OWN_COLS + 2 * pair] = both[:, :CELLS]
            spec_ref[part * OWN_COLS + 2 * pair + 1] = both[:, CELLS:]
        return carry

    lax.fori_loop(0, OWN_COLS // 2, transform, 0)

    lane = lane_ids(DOF)
    row = lax.broadcasted_iota(jnp.int32, (DOF, LANES), 0)
    blank = jnp.zeros((LANES - 2 * DOF, 2 * CELLS), BF16)

    def one_beam(beam, carry):
        glob = az * OWN_BEAMS + beam
        first = lax.bitwise_and(start_ref[glob] - az * OWN_COLS + ARC // 2, COLS - 1)
        for sel in range(SEL):
            column = first + offset_ref[glob, sel]
            real = spec_ref[column, :PULSES]
            imag = spec_ref[column, PULSES:]
            cosine = cos_ref[glob, sel]
            sine = sin_ref[glob, sel]
            rows = pl.ds(SEL + sel, PULSES, stride=SEL)
            wide_ref[0, rows, :] = cosine * real - sine * imag
            wide_ref[1, rows, :] = sine * real + cosine * imag
        last = PULSES * SEL
        for part in range(2):
            for low, high, place in (
                (SEL, SEL + last, SEL),
                (last, last + SEL, 0),
                (SEL, 3 * SEL, SEL + last),
            ):
                value = wide_ref[part, low:high, :]
                snap_ref[beam, part, place : place + high - low, :] = value.astype(BF16)
                if part == 0:
                    minus_ref[place : place + high - low, :] = (-value).astype(BF16)
        weight = mask_ref[beam, 0].astype(F32)
        for half in range(2):
            out = [None, None, None]
            for pair in range(4):
                same, turned = [], []
                for one in range(2):
                    centre = bins_ref[glob, half * 8 + pair * 2 + one]
                    rows = pl.ds(pl.multiple_of(centre * SEL, SEL), DOF)
                    real = snap_ref[beam, 0, rows, :]
                    imag = snap_ref[beam, 1, rows, :]
                    minus = minus_ref[rows, :]
                    same.append(jnp.concatenate([real, imag], 1))
                    turned.append(jnp.concatenate([imag, minus], 1))
                left = jnp.concatenate([same[0], turned[0], same[1], turned[1]], 0)
                right = jnp.concatenate([same[0], same[1], blank], 0)
                gram = lax.dot_general(
                    left, right, TRANSPOSED, preferred_element_type=F32
                )
                packed = jnp.where(
                    lane < DOF,
                    jnp.where(row >= lane, gram[:DOF], gram[DOF : 2 * DOF]),
                    jnp.where(
                        row >= lane - DOF, gram[2 * DOF : 3 * DOF], gram[3 * DOF :]
                    ),
                )
                shift = 2 * DOF * pair % LANES
                if shift:
                    packed = pltpu.roll(packed, shift, 1)
                if pair == 0:
                    out[0] = packed
                elif pair == 1:
                    out[0] = jnp.where(lane >= 96, packed, out[0])
                    out[1] = packed
                elif pair == 2:
                    out[1] = jnp.where(lane >= 64, packed, out[1])
                    out[2] = packed
                else:
                    out[2] = jnp.where(lane >= 32, packed, out[2])
            place = exclusive(beam * 2 + half, mine)
            whole = jnp.concatenate(out, 1) * weight

            @pl.when(place < 8)
            def _():
                keep_ref[lax.rem(place, 8)] = whole

            @pl.when(place >= 8)
            def _():
                send_ref[lax.rem(place, 8)] = whole

        return carry

    lax.fori_loop(0, OWN_BEAMS, one_beam, 0)


def spread(value, index):
    return jnp.take_along_axis(
        value, jnp.full(value.shape, index, jnp.int32), axis=1
    )


def solve_kernel(first_ref, second_ref, marks_ref, out_ref, rows_ref):
    lane = lane_ids(DOF)
    row = lax.broadcasted_iota(jnp.int32, (DOF, LANES), 0)
    total = first_ref[...] + second_ref[...]
    parts = [total[:, LANES * i : LANES * (i + 1)] for i in range(3)]
    for pair in range(4):
        if pair == 0:
            packed = parts[0]
        elif pair == 1:
            packed = jnp.where(
                lane < 32, pltpu.roll(parts[0], 32, 1), pltpu.roll(parts[1], 32, 1)
            )
        elif pair == 2:
            packed = jnp.where(
                lane < 64, pltpu.roll(parts[1], 64, 1), pltpu.roll(parts[2], 64, 1)
            )
        else:
            packed = pltpu.roll(parts[2], 96, 1)
        square = jnp.concatenate([packed, jnp.zeros((LANES - DOF, LANES), F32)], 0)
        turned = jnp.transpose(square)
        for one in range(2):
            here = packed if one == 0 else pltpu.roll(packed, LANES - DOF, 1)
            there = turned[one * DOF : (one + 1) * DOF]
            block_a = jnp.where(row >= lane, here, there)
            block_b = jnp.where(
                row < lane, here, jnp.where(row == lane, 0.0, -there)
            )
            block_b = pltpu.roll(block_b, 64, 1)
            joined = jnp.where(
                lane < DOF,
                block_a,
                jnp.where(
                    lane == DOF,
                    1.0,
                    jnp.where(
                        jnp.logical_and(lane >= 64, lane < 64 + DOF), block_b, 0.0
                    ),
                ),
            )
            rows_ref[pl.ds(pair * 2 + one, DOF, stride=8), :] = joined
    small = lane_ids(8)
    lines = [rows_ref[8 * i : 8 * i + 8, :] for i in range(DOF)]
    diagonal = jnp.zeros((8, LANES), F32)
    for i in range(DOF):
        diagonal = jnp.where(small == i, lines[i], diagonal)
    level = LOADING / DOF * jnp.sum(diagonal, axis=1, keepdims=True)
    level = jnp.broadcast_to(level, (8, LANES))
    for i in range(DOF):
        lines[i] = jnp.where(small == i, lines[i] + level, lines[i])
    for k in range(DOF):
        pivot = lines[k]
        pivot = pivot / spread(pivot, k)
        swapped = pltpu.roll(pivot, 64, 1)
        swapped = jnp.where(small < 64, -swapped, swapped)
        for i in range(DOF):
            if i != k:
                lines[i] = (
                    lines[i]
                    - spread(lines[i], k) * pivot
                    - spread(lines[i], 64 + k) * swapped
                )
        lines[k] = pivot
    found = jnp.zeros((8, LANES), F32)
    for i in range(DOF):
        found = jnp.where(small == i, spread(lines[i], DOF), found)
        found = jnp.where(small == 64 + i, spread(lines[i], 64 + DOF), found)
    quiet = jnp.sum(jnp.where(small < DOF, found, 0.0), axis=1, keepdims=True)
    found = jnp.where(small == 56, jnp.broadcast_to(quiet, (8, LANES)), found)
    out_ref[...] = jnp.where(small == 120, marks_ref[...], found)


def power_kernel(bins_ref, weights_ref, snap_ref, power_ref):
    az = lax.axis_index("az")
    mine = own_group()
    small = lane_ids(8)
    counts = jnp.zeros((8, LANES), F32)
    for place in range(GROUPS):
        counts = counts + weights_ref[place]
    counts = spread(counts, 120) * BLK
    used = jnp.logical_or(
        small < DOF, jnp.logical_and(small >= 64, small < 64 + DOF)
    )
    row = lax.broadcasted_iota(jnp.int32, (2 * 8, LANES), 0)
    for group in range(GROUPS):
        beam = group // 2
        scaled = weights_ref[exclusive(mine, group)] * counts[beam : beam + 1, :]
        quiet = spread(scaled, 56)
        direct = jnp.where(used, scaled, 0.0)
        turned = pltpu.roll(direct, 64, 1)
        turned = jnp.where(small < 64, -turned, turned)
        left = jnp.concatenate([direct, turned], 0).astype(BF16)
        found = jnp.zeros((16, LANES), F32)
        for one in range(8):
            centre = bins_ref[az * OWN_BEAMS + beam, (group % 2) * 8 + one]
            rows = pl.ds(pl.multiple_of(centre * SEL, SEL), 64)
            right = jnp.concatenate(
                [snap_ref[beam, 0, rows, :], snap_ref[beam, 1, rows, :]], 0
            )
            product = jnp.dot(left, right, preferred_element_type=F32)
            found = jnp.where(lax.rem(row, 8) == one, product, found)
        power_ref[group] = (found[:8] * found[:8] + found[8:] * found[8:]) / quiet


def with_halo(block, sides, width, periodic):
    for axis, dim in sides:
        count = lax.axis_size(axis)
        forward = [(i, i + 1) for i in range(count - 1)]
        if periodic:
            forward.append((count - 1, 0))
        backward = [(target, source) for source, target in forward]
        low = lax.ppermute(
            lax.slice_in_dim(block, block.shape[dim] - width, None, axis=dim), axis, forward
        )
        high = lax.ppermute(lax.slice_in_dim(block, 0, width, axis=dim), axis, backward)
        block = jnp.concatenate([low, block, high], axis=dim)
    return block


def swap(value, bit):
    return lax.ppermute(value, "rng", [(i, i ^ (1 << bit)) for i in range(32)])


def halo_columns(echoes):
    ring = [(i, (i + 1) % 8) for i in range(8)]
    low = lax.ppermute(echoes, "az", ring)
    high = lax.ppermute(echoes, "az", [(b, a) for a, b in ring])
    return low, high


SMEM = pl.BlockSpec(memory_space=pltpu.SMEM)
VMEM = pl.BlockSpec(memory_space=pltpu.VMEM)


def body(echoes, arc_start, arc_offsets, doppler_bins, steer_angles, train_mask):
    low, high = halo_columns(echoes)
    marks = jnp.broadcast_to(train_mask.astype(F32), (OWN_BEAMS, LANES))
    marks = marks + swap(marks, 4)
    half = jax.ShapeDtypeStruct((8, DOF, 8 * DOF), F32)
    snaps, keep, send = pl.pallas_call(
        gram_kernel,
        out_shape=(
            jax.ShapeDtypeStruct((OWN_BEAMS, 2, SLOTS * SEL, CELLS), BF16),
            half,
            half,
        ),
        in_specs=[SMEM] * 6 + [VMEM] * 4,
        out_specs=(VMEM, VMEM, VMEM),
        scratch_shapes=[
            pltpu.VMEM((3 * OWN_COLS, 2 * PULSES, CELLS), F32),
            pltpu.VMEM((2, SLOTS * SEL, CELLS), F32),
            pltpu.VMEM((SLOTS * SEL, CELLS), BF16),
        ],
        compiler_params=pltpu.CompilerParams(vmem_limit_bytes=40 * 2**20),
        name="grams",
    )(
        arc_start, arc_offsets, doppler_bins, train_mask,
        jnp.cos(steer_angles), jnp.sin(steer_angles),
        jnp.asarray(table_array()), low, echoes, high,
    )
    part = keep + swap(send, 0)
    for bit, size in ((1, 4), (2, 2), (3, 1)):
        part = part[:size] + swap(part[size:], bit)
    part = part.reshape(DOF, 8 * DOF)
    other = swap(part, 4)
    weights = pl.pallas_call(
        solve_kernel,
        out_shape=jax.ShapeDtypeStruct((8, LANES), F32),
        in_specs=[VMEM] * 3,
        out_specs=VMEM,
        scratch_shapes=[pltpu.VMEM((DOF * 8, LANES), F32)],
        compiler_params=pltpu.CompilerParams(vmem_limit_bytes=32 * 2**20),
        name="solve",
    )(part, other, marks)
    weights = weights[None]
    for bit in (3, 2, 1, 0):
        weights = jnp.concatenate([weights, swap(weights, bit)], 0)
    power = pl.pallas_call(
        power_kernel,
        out_shape=jax.ShapeDtypeStruct((GROUPS, 8, CELLS), F32),
        in_specs=[SMEM, VMEM, VMEM],
        out_specs=VMEM,
        compiler_params=pltpu.CompilerParams(vmem_limit_bytes=32 * 2**20),
        name="power",
    )(doppler_bins, weights, snaps)
    power_map = power.reshape(OWN_BEAMS, DBINS, CELLS)
    beam_ext = with_halo(power_map, (("az", 0),), 1, True)
    full_ext = with_halo(beam_ext, (("rng", 2),), 1, False)
    row_sums = full_ext[:, :, :-2] + full_ext[:, :, 1:-1] + full_ext[:, :, 2:]
    return (row_sums[:-2] + row_sums[1:-1] + row_sums[2:]) / 9.0


def solution(mesh):
    return jax.shard_map(
        body,
        mesh=mesh,
        in_specs=(P(None, "az", None, "rng"), P(), P(), P(), P(), P("az", "rng")),
        out_specs=P("az", None, "rng"),
        check_vma=False,
    )
```

```python
import functools

import jax
import jax.numpy as jnp
import numpy as np
from jax import lax
from jax.experimental import pallas as pl
from jax.experimental.pallas import tpu as pltpu
from jax.sharding import PartitionSpec as P

COLS = 256
ARC = 64
BINS = 3
BEAMS = 64
BLK = 128
PULSES = 32
SEL = 16
DBINS = 16
DOF = BINS * SEL
OWN_COLS = 32
OWN_BEAMS = 8
CELLS = 128
GROUPS = 16
LANES = 128
SLOTS = PULSES + 3
LOADING = 0.1
F32 = jnp.float32
BF16 = jnp.bfloat16
TRANSPOSED = (((1,), (1,)), ((), ()))


def table_array():
    ids = np.arange(PULSES)
    steps = (ids[:, None] * ids[None, :] % PULSES).astype(np.float32)
    angle = np.float32(-2.0 * np.pi / PULSES) * steps
    real, imag = np.cos(angle), np.sin(angle)
    return np.concatenate(
        [np.concatenate([real, -imag], 1), np.concatenate([imag, real], 1)], 0
    ).astype(jnp.bfloat16)


def lane_ids(rows):
    return lax.broadcasted_iota(jnp.int32, (rows, LANES), 1)


def own_group():
    place = lax.axis_index("rng")
    bits = [lax.rem(lax.div(place, 1 << bit), 2) for bit in range(4)]
    return bits[0] * 8 + bits[1] * 4 + bits[2] * 2 + bits[3]


def exclusive(left, right):
    return lax.bitwise_xor(left, right)


def spectra(table, ref, pair, out_ref, base):
    blocks = [
        jnp.concatenate([ref[0, 2 * pair + one], ref[1, 2 * pair + one]], 0)
        for one in range(2)
    ]
    both = jnp.dot(table, jnp.concatenate(blocks, 1), preferred_element_type=F32)
    out_ref[base + 2 * pair] = both[:, :CELLS]
    out_ref[base + 2 * pair + 1] = both[:, CELLS:]


def own_kernel(table_ref, own_ref, spec_ref, passed_ref):
    table = table_ref[...]
    passed_ref[...] = table

    def step(index, carry):
        for one in range(4):
            spectra(table, own_ref, 4 * index + one, spec_ref, 0)
        return carry

    lax.fori_loop(0, OWN_COLS // 8, step, 0)


def gram_kernel(
    column_ref, bins_ref, mask_ref, cos_ref, sin_ref,
    table_ref, low_ref, own_ref, high_ref, marks_ref,
    snap_ref, keep_ref, send_ref, passed_ref,
    spec_ref, wide_ref, minus_ref,
):
    az = lax.axis_index("az")
    mine = own_group()
    table = table_ref[...]
    passed_ref[...] = marks_ref[...]

    def transform(index, carry):
        for one in range(2):
            spectra(table, low_ref, 2 * index + one, spec_ref, 0)
            spectra(table, high_ref, 2 * index + one, spec_ref, 2 * OWN_COLS)
        for one in range(4):
            spec_ref[OWN_COLS + 4 * index + one] = own_ref[4 * index + one]
        return carry

    lax.fori_loop(0, OWN_COLS // 4, transform, 0)

    lane = lane_ids(DOF)
    row = lax.broadcasted_iota(jnp.int32, (DOF, LANES), 0)
    blank = jnp.zeros((LANES - 2 * DOF, 2 * CELLS), BF16)

    def one_beam(beam, carry):
        glob = az * OWN_BEAMS + beam
        for sel in range(SEL):
            column = column_ref[glob, sel]
            real = spec_ref[column, :PULSES]
            imag = spec_ref[column, PULSES:]
            cosine = cos_ref[glob, sel]
            sine = sin_ref[glob, sel]
            rows = pl.ds(SEL + sel, PULSES, stride=SEL)
            wide_ref[0, rows, :] = cosine * real - sine * imag
            wide_ref[1, rows, :] = sine * real + cosine * imag
        last = PULSES * SEL
        for part in range(2):
            for low, high, place in (
                (SEL, SEL + last, SEL),
                (last, last + SEL, 0),
                (SEL, 3 * SEL, SEL + last),
            ):
                value = wide_ref[part, low:high, :]
                snap_ref[beam, part, place : place + high - low, :] = value.astype(BF16)
                if part == 0:
                    minus_ref[place : place + high - low, :] = (-value).astype(BF16)
        weight = mask_ref[beam, 0].astype(F32)
        for half in range(2):
            out = [None, None, None]
            for pair in range(4):
                same, turned = [], []
                for one in range(2):
                    centre = bins_ref[glob, half * 8 + pair * 2 + one]
                    rows = pl.ds(pl.multiple_of(centre * SEL, SEL), DOF)
                    real = snap_ref[beam, 0, rows, :]
                    imag = snap_ref[beam, 1, rows, :]
                    minus = minus_ref[rows, :]
                    same.append(jnp.concatenate([real, imag], 1))
                    turned.append(jnp.concatenate([imag, minus], 1))
                left = jnp.concatenate([same[0], turned[0], same[1], turned[1]], 0)
                right = jnp.concatenate([same[0], same[1], blank], 0)
                gram = lax.dot_general(
                    left, right, TRANSPOSED, preferred_element_type=F32
                )
                packed = jnp.where(
                    lane < DOF,
                    jnp.where(row >= lane, gram[:DOF], gram[DOF : 2 * DOF]),
                    jnp.where(
                        row >= lane - DOF, gram[2 * DOF : 3 * DOF], gram[3 * DOF :]
                    ),
                )
                shift = 2 * DOF * pair % LANES
                if shift:
                    packed = pltpu.roll(packed, shift, 1)
                if pair == 0:
                    out[0] = packed
                elif pair == 1:
                    out[0] = jnp.where(lane >= 96, packed, out[0])
                    out[1] = packed
                elif pair == 2:
                    out[1] = jnp.where(lane >= 64, packed, out[1])
                    out[2] = packed
                else:
                    out[2] = jnp.where(lane >= 32, packed, out[2])
            place = exclusive(beam * 2 + half, mine)
            whole = jnp.concatenate(out, 1) * weight

            @pl.when(place < 8)
            def _():
                keep_ref[lax.rem(place, 8)] = whole

            @pl.when(place >= 8)
            def _():
                send_ref[lax.rem(place, 8)] = whole

        return carry

    lax.fori_loop(0, OWN_BEAMS, one_beam, 0)


def spread(value, index):
    return jnp.take_along_axis(
        value, jnp.full(value.shape, index, jnp.int32), axis=1
    )


def solve_kernel(first_ref, second_ref, marks_ref, out_ref, turn_ref):
    lane = lane_ids(DOF)
    row = lax.broadcasted_iota(jnp.int32, (DOF, LANES), 0)
    slot = lax.div(lane, SEL)
    lower = row >= lane
    same = row == lane
    total = first_ref[...] + second_ref[...]
    parts = [total[:, LANES * i : LANES * (i + 1)] for i in range(3)]
    block_a = [None] * BINS
    block_b = [None] * BINS
    for pair in range(4):
        if pair == 0:
            packed = parts[0]
        elif pair == 1:
            packed = jnp.where(
                lane < 32, pltpu.roll(parts[0], 32, 1), pltpu.roll(parts[1], 32, 1)
            )
        elif pair == 2:
            packed = jnp.where(
                lane < 64, pltpu.roll(parts[1], 64, 1), pltpu.roll(parts[2], 64, 1)
            )
        else:
            packed = pltpu.roll(parts[2], 96, 1)
        square = jnp.concatenate([packed, jnp.zeros((LANES - DOF, LANES), F32)], 0)
        turned = jnp.transpose(square)
        for one in range(2):
            item = pair * 2 + one
            here = packed if one == 0 else pltpu.roll(packed, LANES - DOF, 1)
            there = turned[one * DOF : (one + 1) * DOF]
            value_a = jnp.where(lower, here, there)
            value_b = jnp.where(lower, jnp.where(same, 0.0, -there), here)
            if item:
                value_a = pltpu.roll(value_a, SEL * item, 1)
                value_b = pltpu.roll(value_b, SEL * item, 1)
            for part in range(BINS):
                if item == 0:
                    block_a[part] = value_a
                    block_b[part] = value_b
                else:
                    chosen = slot == (item + part) % 8
                    block_a[part] = jnp.where(chosen, value_a, block_a[part])
                    block_b[part] = jnp.where(chosen, value_b, block_b[part])
    for part in range(1, BINS):
        block_a[part] = pltpu.roll(block_a[part], LANES - SEL * part, 1)
        block_b[part] = pltpu.roll(block_b[part], LANES - SEL * part, 1)
    small = lane_ids(8)
    line = lax.broadcasted_iota(jnp.int32, (8, LANES), 0)
    place = lax.rem(small, SEL)
    base = small - place
    diagonal = jnp.zeros((8, LANES), F32)
    masks = []
    for group in range(DOF // 8):
        masks.append(place == line + group % 2 * 8)
        diagonal = diagonal + jnp.where(
            masks[group], block_a[group // 2][8 * group : 8 * group + 8], 0.0
        )
    level = jnp.sum(diagonal, axis=0, keepdims=True)
    level = jnp.broadcast_to(level, (8, LANES))
    for step in (1, 2, 4, 8):
        partner = base + lax.rem(place + step, SEL)
        level = level + jnp.take_along_axis(level, partner, axis=1)
    level = LOADING / DOF * level
    real = [[None] * 4 for _ in range(6)]
    imag = [[None] * 4 for _ in range(6)]
    for group in range(6):
        for part in range(BINS):
            real[group][part] = block_a[part][8 * group : 8 * group + 8]
            imag[group][part] = block_b[part][8 * group : 8 * group + 8]
        real[group][group // 2] = jnp.where(
            masks[group], real[group][group // 2] + level, real[group][group // 2]
        )
        real[group][3] = jnp.ones((8, LANES), F32)
        imag[group][3] = jnp.zeros((8, LANES), F32)
    inverse = [jnp.ones((8, LANES), F32)] * 6
    for k in range(DOF):
        group, inner, part = k // 8, k % 8, k // SEL
        index = base + k % SEL
        mult_re = [jnp.take_along_axis(real[i][part], index, axis=1) for i in range(6)]
        mult_im = [jnp.take_along_axis(imag[i][part], index, axis=1) for i in range(6)]
        pivot = jnp.broadcast_to(mult_re[group][inner : inner + 1], (8, LANES))
        pivot = 1.0 / pivot
        here = line == inner
        mult_re[group] = jnp.where(here, 0.0, mult_re[group])
        mult_im[group] = jnp.where(here, 0.0, mult_im[group])
        inverse[group] = jnp.where(here, pivot, inverse[group])
        for block in (*range(part, BINS), 3):
            row_re = pivot * jnp.broadcast_to(
                real[group][block][inner : inner + 1], (8, LANES)
            )
            row_im = pivot * jnp.broadcast_to(
                imag[group][block][inner : inner + 1], (8, LANES)
            )
            for i in range(6):
                real[i][block] = (
                    real[i][block] - mult_re[i] * row_re + mult_im[i] * row_im
                )
                imag[i][block] = (
                    imag[i][block] - mult_re[i] * row_im - mult_im[i] * row_re
                )
    gap = jnp.zeros((SEL, LANES), F32)
    found_re = [real[i][3] * inverse[i] for i in range(6)]
    found_im = [imag[i][3] * inverse[i] for i in range(6)]
    quiet = found_re[0]
    for i in range(1, 6):
        quiet = quiet + found_re[i]
    quiet = jnp.broadcast_to(jnp.sum(quiet, axis=0, keepdims=True), (SEL, LANES))
    turn_ref[...] = jnp.transpose(
        jnp.concatenate([*found_re, quiet, *found_im, gap], 0)
    )
    found = turn_ref[pl.ds(0, 8, stride=SEL), :]
    out_ref[...] = jnp.where(small == 120, marks_ref[...], found)


def power_kernel(bins_ref, weights_ref, snap_ref, power_ref):
    az = lax.axis_index("az")
    mine = own_group()
    small = lane_ids(8)
    counts = jnp.zeros((8, LANES), F32)
    for place in range(GROUPS):
        counts = counts + weights_ref[place]
    counts = spread(counts, 120) * BLK
    used = jnp.logical_or(
        small < DOF, jnp.logical_and(small >= 64, small < 64 + DOF)
    )
    row = lax.broadcasted_iota(jnp.int32, (2 * 8, LANES), 0)
    for group in range(GROUPS):
        beam = group // 2
        scaled = weights_ref[exclusive(mine, group)] * counts[beam : beam + 1, :]
        quiet = spread(scaled, 56)
        direct = jnp.where(used, scaled, 0.0)
        turned = pltpu.roll(direct, 64, 1)
        turned = jnp.where(small < 64, -turned, turned)
        left = jnp.concatenate([direct, turned], 0).astype(BF16)
        found = jnp.zeros((16, LANES), F32)
        for one in range(8):
            centre = bins_ref[az * OWN_BEAMS + beam, (group % 2) * 8 + one]
            rows = pl.ds(pl.multiple_of(centre * SEL, SEL), 64)
            right = jnp.concatenate(
                [snap_ref[beam, 0, rows, :], snap_ref[beam, 1, rows, :]], 0
            )
            product = jnp.dot(left, right, preferred_element_type=F32)
            found = jnp.where(lax.rem(row, 8) == one, product, found)
        power_ref[group] = (found[:8] * found[:8] + found[8:] * found[8:]) / quiet


def with_halo(block, sides, width, periodic):
    for axis, dim in sides:
        count = lax.axis_size(axis)
        forward = [(i, i + 1) for i in range(count - 1)]
        if periodic:
            forward.append((count - 1, 0))
        backward = [(target, source) for source, target in forward]
        low = lax.ppermute(
            lax.slice_in_dim(block, block.shape[dim] - width, None, axis=dim), axis, forward
        )
        high = lax.ppermute(lax.slice_in_dim(block, 0, width, axis=dim), axis, backward)
        block = jnp.concatenate([low, block, high], axis=dim)
    return block


def swap(value, turn):
    return lax.ppermute(value, "rng", [(i, i ^ turn) for i in range(32)])


def halo_columns(echoes):
    ring = [(i, (i + 1) % 8) for i in range(8)]
    low = lax.ppermute(echoes, "az", ring)
    high = lax.ppermute(echoes, "az", [(b, a) for a, b in ring])
    return low, high


SMEM = pl.BlockSpec(memory_space=pltpu.SMEM)
VMEM = pl.BlockSpec(memory_space=pltpu.VMEM)


def body(echoes, arc_start, arc_offsets, doppler_bins, steer_angles, train_mask):
    low, high = halo_columns(echoes)
    marks = jnp.broadcast_to(train_mask.astype(F32), (OWN_BEAMS, LANES))
    marks = marks + swap(marks, 16)
    half = jax.ShapeDtypeStruct((8, DOF, 8 * DOF), F32)
    first = (arc_start - lax.axis_index("az") * OWN_COLS + ARC // 2) % COLS
    spec, table = pl.pallas_call(
        own_kernel,
        out_shape=(
            jax.ShapeDtypeStruct((OWN_COLS, 2 * PULSES, CELLS), F32),
            jax.ShapeDtypeStruct((2 * PULSES, 2 * PULSES), BF16),
        ),
        in_specs=[VMEM, VMEM],
        out_specs=(VMEM, VMEM),
        compiler_params=pltpu.CompilerParams(vmem_limit_bytes=32 * 2**20),
        name="spectra",
    )(jnp.asarray(table_array()), echoes)
    snaps, keep, send, marks = pl.pallas_call(
        gram_kernel,
        out_shape=(
            jax.ShapeDtypeStruct((OWN_BEAMS, 2, SLOTS * SEL, CELLS), BF16),
            half,
            half,
            jax.ShapeDtypeStruct((OWN_BEAMS, LANES), F32),
        ),
        in_specs=[SMEM] * 5 + [VMEM] * 5,
        out_specs=(VMEM, VMEM, VMEM, VMEM),
        scratch_shapes=[
            pltpu.VMEM((3 * OWN_COLS, 2 * PULSES, CELLS), F32),
            pltpu.VMEM((2, SLOTS * SEL, CELLS), F32),
            pltpu.VMEM((SLOTS * SEL, CELLS), BF16),
        ],
        compiler_params=pltpu.CompilerParams(vmem_limit_bytes=40 * 2**20),
        name="grams",
    )(
        first[:, None] + arc_offsets, doppler_bins, train_mask,
        jnp.cos(steer_angles), jnp.sin(steer_angles),
        table, low, spec, high, marks,
    )
    part = keep + swap(send, 1)
    part = part[:2] + swap(part[2:4], 4) + swap(part[4:6], 2) + swap(part[6:], 6)
    part = part[0] + swap(part[1], 8)
    other = swap(part, 16)
    weights = pl.pallas_call(
        solve_kernel,
        out_shape=jax.ShapeDtypeStruct((8, LANES), F32),
        in_specs=[VMEM] * 3,
        out_specs=VMEM,
        scratch_shapes=[pltpu.VMEM((LANES, LANES), F32)],
        compiler_params=pltpu.CompilerParams(vmem_limit_bytes=32 * 2**20),
        name="solve",
    )(part, other, marks)
    weights = weights[None]
    for turn in (8, 4, 2, 1):
        weights = jnp.concatenate([weights, swap(weights, turn)], 0)
    power = pl.pallas_call(
        power_kernel,
        out_shape=jax.ShapeDtypeStruct((GROUPS, 8, CELLS), F32),
        in_specs=[SMEM, VMEM, VMEM],
        out_specs=VMEM,
        compiler_params=pltpu.CompilerParams(vmem_limit_bytes=32 * 2**20),
        name="power",
    )(doppler_bins, weights, snaps)
    power_map = power.reshape(OWN_BEAMS, DBINS, CELLS)
    beam_ext = with_halo(power_map, (("az", 0),), 1, True)
    full_ext = with_halo(beam_ext, (("rng", 2),), 1, False)
    row_sums = full_ext[:, :, :-2] + full_ext[:, :, 1:-1] + full_ext[:, :, 2:]
    return (row_sums[:-2] + row_sums[1:-1] + row_sums[2:]) / 9.0


def solution(mesh):
    return jax.shard_map(
        body,
        mesh=mesh,
        in_specs=(P(None, "az", None, "rng"), P(), P(), P(), P(), P("az", "rng")),
        out_specs=P("az", None, "rng"),
        check_vma=False,
    )
```

```python
import functools

import jax
import jax.numpy as jnp
import numpy as np
from jax import lax
from jax.experimental import pallas as pl
from jax.experimental.pallas import tpu as pltpu
from jax.sharding import PartitionSpec as P

COLS = 256
ARC = 64
BINS = 3
BEAMS = 64
BLK = 128
PULSES = 32
SEL = 16
DBINS = 16
DOF = BINS * SEL
OWN_COLS = 32
OWN_BEAMS = 8
CELLS = 128
GROUPS = 16
LANES = 128
SLOTS = PULSES + 3
LOADING = 0.1
F32 = jnp.float32
BF16 = jnp.bfloat16
TRANSPOSED = (((1,), (1,)), ((), ()))


def table_array():
    ids = np.arange(PULSES)
    steps = (ids[:, None] * ids[None, :] % PULSES).astype(np.float32)
    angle = np.float32(-2.0 * np.pi / PULSES) * steps
    real, imag = np.cos(angle), np.sin(angle)
    return np.concatenate(
        [np.concatenate([real, -imag], 1), np.concatenate([imag, real], 1)], 0
    ).astype(jnp.bfloat16)


def lane_ids(rows):
    return lax.broadcasted_iota(jnp.int32, (rows, LANES), 1)


def own_group():
    place = lax.axis_index("rng")
    bits = [lax.rem(lax.div(place, 1 << bit), 2) for bit in range(4)]
    return bits[0] * 8 + bits[1] * 4 + bits[2] * 2 + bits[3]


def exclusive(left, right):
    return lax.bitwise_xor(left, right)


def spectra(table, ref, pair, out_ref, base):
    blocks = [
        jnp.concatenate([ref[0, 2 * pair + one], ref[1, 2 * pair + one]], 0)
        for one in range(2)
    ]
    both = jnp.dot(table, jnp.concatenate(blocks, 1), preferred_element_type=F32)
    out_ref[base + 2 * pair] = both[:, :CELLS]
    out_ref[base + 2 * pair + 1] = both[:, CELLS:]


def own_kernel(table_ref, own_ref, spec_ref, passed_ref):
    table = table_ref[...]
    passed_ref[...] = table

    def step(index, carry):
        for one in range(4):
            spectra(table, own_ref, 4 * index + one, spec_ref, 0)
        return carry

    lax.fori_loop(0, OWN_COLS // 8, step, 0)


def gram_kernel(
    ints_ref, floats_ref,
    table_ref, low_ref, own_ref, high_ref, marks_ref,
    snap_ref, keep_ref, send_ref, passed_ref,
    spec_ref, wide_ref,
):
    mine = own_group()
    table = table_ref[...]
    passed_ref[...] = marks_ref[...]

    def transform(index, carry):
        for one in range(2):
            spectra(table, low_ref, 2 * index + one, spec_ref, 0)
            spectra(table, high_ref, 2 * index + one, spec_ref, 2 * OWN_COLS)
        for one in range(4):
            spec_ref[OWN_COLS + 4 * index + one] = own_ref[4 * index + one]
        return carry

    lax.fori_loop(0, OWN_COLS // 4, transform, 0)

    lane = lane_ids(DOF)
    row = lax.broadcasted_iota(jnp.int32, (DOF, LANES), 0)
    lower = row >= lane - jnp.where(lane < DOF, 0, DOF)
    blank = jnp.zeros((LANES - 2 * DOF, 2 * CELLS), BF16)
    last = PULSES * SEL

    def first_group(step):
        return exclusive(exclusive(2 * step, 8), mine)

    def turn(step):
        beam = lax.div(first_group(step), 2)
        for sel in range(SEL):
            column = ints_ref[beam, sel]
            real = spec_ref[column, :PULSES]
            imag = spec_ref[column, PULSES:]
            cosine = floats_ref[beam, sel]
            sine = floats_ref[beam, SEL + sel]
            rows = pl.ds(SEL + sel, PULSES, stride=SEL)
            wide_ref[0, rows, :] = cosine * real - sine * imag
            wide_ref[1, rows, :] = sine * real + cosine * imag
        for part in range(2):
            for low, high, place in (
                (SEL, SEL + last, SEL),
                (last, last + SEL, 0),
                (SEL, 3 * SEL, SEL + last),
            ):
                snap_ref[beam, part, place : place + high - low, :] = wide_ref[
                    part, low:high, :
                ].astype(BF16)

    def multiply(step, out_ref):
        group = first_group(step)
        beam = lax.div(group, 2)
        weight = ints_ref[beam, 2 * SEL].astype(F32)
        for half in range(2):
            base = exclusive(lax.rem(group, 2), half) * 8
            out = [None, None, None]
            for pair in range(4):
                same, turned = [], []
                for one in range(2):
                    centre = ints_ref[beam, SEL + base + pair * 2 + one]
                    rows = pl.ds(pl.multiple_of(centre * SEL, SEL), DOF)
                    real = snap_ref[beam, 0, rows, :]
                    imag = snap_ref[beam, 1, rows, :]
                    same.append(jnp.concatenate([real, imag], 1))
                    turned.append(jnp.concatenate([imag, -real], 1))
                left = jnp.concatenate([same[0], turned[0], same[1], turned[1]], 0)
                right = jnp.concatenate([same[0], same[1], blank], 0)
                gram = lax.dot_general(
                    left, right, TRANSPOSED, preferred_element_type=F32
                )
                packed = jnp.where(
                    lower,
                    jnp.where(lane < DOF, gram[:DOF], gram[2 * DOF : 3 * DOF]),
                    jnp.where(lane < DOF, gram[DOF : 2 * DOF], gram[3 * DOF :]),
                )
                shift = 2 * DOF * pair % LANES
                if shift:
                    packed = pltpu.roll(packed, shift, 1)
                if pair == 0:
                    out[0] = packed
                elif pair == 1:
                    out[0] = jnp.where(lane >= 96, packed, out[0])
                    out[1] = packed
                elif pair == 2:
                    out[1] = jnp.where(lane >= 64, packed, out[1])
                    out[2] = packed
                else:
                    out[2] = jnp.where(lane >= 32, packed, out[2])
            place = lax.rem(2 * step, 8) + half
            for part in range(3):
                out_ref[place, :, LANES * part : LANES * (part + 1)] = (
                    out[part] * weight
                )

    def sending(step, carry):
        turn(step + 1)
        multiply(step, send_ref)
        return carry

    def keeping(step, carry):
        turn(step + 1)
        multiply(step, keep_ref)
        return carry

    turn(0)
    lax.fori_loop(0, 4, sending, 0)
    lax.fori_loop(4, 7, keeping, 0)
    multiply(7, keep_ref)


def edge_out_kernel(snap_ref, first_ref, second_ref):
    rows = 8 * 8
    lane = lane_ids(rows)
    ends = [jnp.zeros((rows, LANES), F32) for _ in range(2)]
    for beam in range(OWN_BEAMS):
        for part in range(2):
            for block in range(8):
                low = SEL + rows * block
                value = snap_ref[beam, part, low : low + rows, :].astype(F32)
                target = 16 * block + 8 * part + beam
                here = lane == target
                for end in range(2):
                    shift = (target + end) % LANES
                    moved = pltpu.roll(value, shift, 1) if shift else value
                    ends[end] = jnp.where(here, moved, ends[end])
    even = lax.rem(lax.axis_index("rng"), 2) == 0
    first_ref[...] = jnp.where(even, ends[1], ends[0]).astype(BF16)
    second_ref[...] = jnp.where(even, ends[0], ends[1]).astype(BF16)


def edge_in_kernel(first_ref, second_ref, direct_ref, turned_ref):
    rows = 8 * 8
    lane = lane_ids(rows)
    first = first_ref[...].astype(F32)
    second = second_ref[...].astype(F32)

    def rolled(value, shift):
        return pltpu.roll(value, shift % LANES, 1) if shift % LANES else value

    for block in range(8):
        both = jnp.where(
            lane < 16, rolled(first, -16 * block), rolled(second, 16 - 16 * block)
        )
        for ref, value in ((direct_ref, both), (turned_ref, rolled(both, -8))):
            value = value.astype(BF16)
            ref[SEL + rows * block : SEL + rows * (block + 1), :] = value
            if block == 0:
                ref[PULSES * SEL + SEL :, :] = value[: 2 * SEL]
            if block == 7:
                ref[:SEL, :] = value[rows - SEL :]


def spread(value, index):
    return jnp.take_along_axis(
        value, jnp.full(value.shape, index, jnp.int32), axis=1
    )


def solve_kernel(first_ref, second_ref, marks_ref, out_ref, turn_ref):
    lane = lane_ids(DOF)
    row = lax.broadcasted_iota(jnp.int32, (DOF, LANES), 0)
    slot = lax.div(lane, SEL)
    lower = row >= lane
    same = row == lane
    total = first_ref[...] + second_ref[...]
    parts = [total[:, LANES * i : LANES * (i + 1)] for i in range(3)]
    block_a = [None] * BINS
    block_b = [None] * BINS
    for pair in range(4):
        if pair == 0:
            packed = parts[0]
        elif pair == 1:
            packed = jnp.where(
                lane < 32, pltpu.roll(parts[0], 32, 1), pltpu.roll(parts[1], 32, 1)
            )
        elif pair == 2:
            packed = jnp.where(
                lane < 64, pltpu.roll(parts[1], 64, 1), pltpu.roll(parts[2], 64, 1)
            )
        else:
            packed = pltpu.roll(parts[2], 96, 1)
        square = jnp.concatenate([packed, jnp.zeros((LANES - DOF, LANES), F32)], 0)
        turned = jnp.transpose(square)
        for one in range(2):
            item = pair * 2 + one
            here = packed if one == 0 else pltpu.roll(packed, LANES - DOF, 1)
            there = turned[one * DOF : (one + 1) * DOF]
            value_a = jnp.where(lower, here, there)
            value_b = jnp.where(lower, jnp.where(same, 0.0, -there), here)
            if item:
                value_a = pltpu.roll(value_a, SEL * item, 1)
                value_b = pltpu.roll(value_b, SEL * item, 1)
            for part in range(BINS):
                if item == 0:
                    block_a[part] = value_a
                    block_b[part] = value_b
                else:
                    chosen = slot == (item + part) % 8
                    block_a[part] = jnp.where(chosen, value_a, block_a[part])
                    block_b[part] = jnp.where(chosen, value_b, block_b[part])
    for part in range(1, BINS):
        block_a[part] = pltpu.roll(block_a[part], LANES - SEL * part, 1)
        block_b[part] = pltpu.roll(block_b[part], LANES - SEL * part, 1)
    small = lane_ids(8)
    line = lax.broadcasted_iota(jnp.int32, (8, LANES), 0)
    place = lax.rem(small, SEL)
    base = small - place
    diagonal = jnp.zeros((8, LANES), F32)
    masks = []
    for group in range(DOF // 8):
        masks.append(place == line + group % 2 * 8)
        diagonal = diagonal + jnp.where(
            masks[group], block_a[group // 2][8 * group : 8 * group + 8], 0.0
        )
    level = jnp.sum(diagonal, axis=0, keepdims=True)
    level = jnp.broadcast_to(level, (8, LANES))
    for step in (1, 2, 4, 8):
        partner = base + lax.rem(place + step, SEL)
        level = level + jnp.take_along_axis(level, partner, axis=1)
    level = LOADING / DOF * level
    real = [[None] * 4 for _ in range(6)]
    imag = [[None] * 4 for _ in range(6)]
    for group in range(6):
        for part in range(BINS):
            real[group][part] = block_a[part][8 * group : 8 * group + 8]
            imag[group][part] = block_b[part][8 * group : 8 * group + 8]
        real[group][group // 2] = jnp.where(
            masks[group], real[group][group // 2] + level, real[group][group // 2]
        )
        real[group][3] = jnp.ones((8, LANES), F32)
        imag[group][3] = jnp.zeros((8, LANES), F32)
    inverse = [jnp.ones((8, LANES), F32)] * 6
    for k in range(DOF):
        group, inner, part = k // 8, k % 8, k // SEL
        index = base + k % SEL
        mult_re = [jnp.take_along_axis(real[i][part], index, axis=1) for i in range(6)]
        mult_im = [jnp.take_along_axis(imag[i][part], index, axis=1) for i in range(6)]
        pivot = jnp.broadcast_to(mult_re[group][inner : inner + 1], (8, LANES))
        pivot = 1.0 / pivot
        here = line == inner
        mult_re[group] = jnp.where(here, 0.0, mult_re[group])
        mult_im[group] = jnp.where(here, 0.0, mult_im[group])
        inverse[group] = jnp.where(here, pivot, inverse[group])
        for block in (*range(part, BINS), 3):
            row_re = pivot * jnp.broadcast_to(
                real[group][block][inner : inner + 1], (8, LANES)
            )
            row_im = pivot * jnp.broadcast_to(
                imag[group][block][inner : inner + 1], (8, LANES)
            )
            for i in range(6):
                real[i][block] = (
                    real[i][block] - mult_re[i] * row_re + mult_im[i] * row_im
                )
                imag[i][block] = (
                    imag[i][block] - mult_re[i] * row_im - mult_im[i] * row_re
                )
    gap = jnp.zeros((SEL, LANES), F32)
    found_re = [real[i][3] * inverse[i] for i in range(6)]
    found_im = [imag[i][3] * inverse[i] for i in range(6)]
    quiet = found_re[0]
    for i in range(1, 6):
        quiet = quiet + found_re[i]
    quiet = jnp.broadcast_to(jnp.sum(quiet, axis=0, keepdims=True), (SEL, LANES))
    turn_ref[...] = jnp.transpose(
        jnp.concatenate([*found_re, quiet, *found_im, gap], 0)
    )
    found = turn_ref[pl.ds(0, 8, stride=SEL), :]
    out_ref[...] = jnp.where(small == 120, marks_ref[...], found)


def power_kernel(
    ints_ref, weights_ref, snap_ref, direct_ref, turned_ref,
    power_ref, first_ref, second_ref,
):
    mine = own_group()
    even = lax.rem(lax.axis_index("rng"), 2) == 0
    small = lane_ids(8)
    counts = jnp.zeros((8, LANES), F32)
    for place in range(GROUPS):
        counts = counts + weights_ref[place]
    counts = spread(counts, 120) * BLK
    used = jnp.logical_or(
        small < DOF, jnp.logical_and(small >= 64, small < 64 + DOF)
    )
    row = lax.broadcasted_iota(jnp.int32, (2 * 8, 2 * LANES), 0)
    low_lane = jnp.where(even, 16, 0)
    for group in range(GROUPS):
        beam = group // 2
        scaled = weights_ref[exclusive(mine, group)] * counts[beam : beam + 1, :]
        quiet = spread(scaled, 56)
        direct = jnp.where(used, scaled, 0.0)
        turned = pltpu.roll(direct, 64, 1)
        turned = jnp.where(small < 64, -turned, turned)
        left = jnp.concatenate([direct, turned], 0).astype(BF16)
        found = jnp.zeros((16, 2 * LANES), F32)
        for one in range(8):
            centre = ints_ref[beam, SEL + (group % 2) * 8 + one]
            rows = pl.ds(pl.multiple_of(centre * SEL, SEL), 64)
            right = jnp.concatenate(
                [
                    jnp.concatenate([snap_ref[beam, 0, rows, :], direct_ref[rows, :]], 1),
                    jnp.concatenate([snap_ref[beam, 1, rows, :], turned_ref[rows, :]], 1),
                ],
                0,
            )
            product = jnp.dot(left, right, preferred_element_type=F32)
            found = jnp.where(lax.rem(row, 8) == one, product, found)
        power = found[:8] * found[:8] + found[8:] * found[8:]
        inner = power[:, :LANES] / quiet
        outer = power[:, LANES:] / quiet
        low = spread(outer, beam + low_lane)
        high = spread(outer, beam + 16 - low_lane)
        below = jnp.where(small == 0, low, pltpu.roll(inner, 1, 1))
        above = jnp.where(small == LANES - 1, high, pltpu.roll(inner, LANES - 1, 1))
        power_ref[group] = below + inner + above
    even = lax.rem(lax.axis_index("az"), 2) == 0
    for half in range(2):
        bottom, top = power_ref[half], power_ref[GROUPS - 2 + half]
        first_ref[half] = jnp.where(even, top, bottom)
        second_ref[half] = jnp.where(even, bottom, top)


def smooth_kernel(power_ref, first_ref, second_ref, out_ref):
    even = lax.rem(lax.axis_index("az"), 2) == 0
    first, second = first_ref[...], second_ref[...]
    low = jnp.where(even, second, first)
    high = jnp.where(even, first, second)
    for beam in range(OWN_BEAMS):
        below = low if beam == 0 else power_ref[2 * beam - 2 : 2 * beam]
        above = (
            high if beam == OWN_BEAMS - 1 else power_ref[2 * beam + 2 : 2 * beam + 4]
        )
        here = power_ref[2 * beam : 2 * beam + 2]
        out_ref[2 * beam : 2 * beam + 2] = (below + here + above) / 9.0


def swap(value, turn):
    return lax.ppermute(value, "rng", [(i, i ^ turn) for i in range(32)])


def halo_columns(echoes):
    ring = [(i, (i + 1) % 8) for i in range(8)]
    low = lax.ppermute(echoes, "az", ring)
    high = lax.ppermute(echoes, "az", [(b, a) for a, b in ring])
    return low, high


SMEM = pl.BlockSpec(memory_space=pltpu.SMEM)
VMEM = pl.BlockSpec(memory_space=pltpu.VMEM)


def limit(mebibytes):
    return pltpu.CompilerParams(vmem_limit_bytes=mebibytes * 2**20)


def shape(*dims, dtype=F32):
    return jax.ShapeDtypeStruct(dims, dtype)


def neighbours(count, closed):
    nearest = [(i, i ^ 1) for i in range(count)]
    across = [(i, i + 1) if i % 2 else (i, i - 1) for i in range(count)]
    if closed:
        across = [(a, b % count) for a, b in across]
    else:
        across = [(a, b) for a, b in across if 0 <= b < count]
    return nearest, across


def body(echoes, arc_start, arc_offsets, doppler_bins, steer_angles, train_mask):
    low, high = halo_columns(echoes)
    az = lax.axis_index("az")

    def own(value):
        return lax.dynamic_slice_in_dim(value, az * OWN_BEAMS, OWN_BEAMS, 0)

    marks = jnp.broadcast_to(train_mask.astype(F32), (OWN_BEAMS, LANES))
    marks = marks + swap(marks, 16)
    first = (own(arc_start) - az * OWN_COLS + ARC // 2) % COLS
    ints = jnp.concatenate(
        [first[:, None] + own(arc_offsets), own(doppler_bins), train_mask], 1
    )
    angles = own(steer_angles)
    floats = jnp.concatenate([jnp.cos(angles), jnp.sin(angles)], 1)
    spec, table = pl.pallas_call(
        own_kernel,
        out_shape=(
            shape(OWN_COLS, 2 * PULSES, CELLS),
            shape(2 * PULSES, 2 * PULSES, dtype=BF16),
        ),
        in_specs=[VMEM, VMEM],
        out_specs=(VMEM, VMEM),
        compiler_params=limit(8),
        name="spectra",
    )(jnp.asarray(table_array()), echoes)
    half = shape(8, DOF, 8 * DOF)
    snaps, keep, send, marks = pl.pallas_call(
        gram_kernel,
        out_shape=(
            shape(OWN_BEAMS, 2, SLOTS * SEL, CELLS, dtype=BF16),
            half,
            half,
            shape(OWN_BEAMS, LANES),
        ),
        in_specs=[SMEM] * 2 + [VMEM] * 5,
        out_specs=(VMEM,) * 4,
        scratch_shapes=[
            pltpu.VMEM((3 * OWN_COLS, 2 * PULSES, CELLS), F32),
            pltpu.VMEM((2, SLOTS * SEL, CELLS), F32),
        ],
        compiler_params=limit(16),
        name="grams",
    )(ints, floats, table, low, spec, high, marks)
    edge = shape(64, LANES, dtype=BF16)
    edges = pl.pallas_call(
        edge_out_kernel,
        out_shape=(edge, edge),
        in_specs=[VMEM],
        out_specs=(VMEM, VMEM),
        compiler_params=limit(8),
        name="edges_out",
    )(snaps)
    part = keep + swap(send, 1)
    moved = [swap(part[2:4], 4), swap(part[4:6], 2), swap(part[6:], 6)]
    moved, edges = lax.optimization_barrier((moved, edges))
    part = part[:2] + moved[0] + moved[1] + moved[2]
    moved = swap(part[1], 8)
    edges = [
        lax.ppermute(value, "rng", pairs)
        for value, pairs in zip(edges, neighbours(32, False))
    ]
    moved, edges = lax.optimization_barrier((moved, edges))
    part = part[0] + moved
    other = swap(part, 16)
    edge = shape(SLOTS * SEL, LANES, dtype=BF16)
    edges = pl.pallas_call(
        edge_in_kernel,
        out_shape=(edge, edge),
        in_specs=[VMEM, VMEM],
        out_specs=(VMEM, VMEM),
        compiler_params=limit(8),
        name="edges_in",
    )(*edges)
    other, edges = lax.optimization_barrier((other, edges))
    weights = pl.pallas_call(
        solve_kernel,
        out_shape=shape(8, LANES),
        in_specs=[VMEM] * 3,
        out_specs=VMEM,
        scratch_shapes=[pltpu.VMEM((LANES, LANES), F32)],
        compiler_params=limit(8),
        name="solve",
    )(part, other, marks)
    weights = weights[None]
    for turn in (8, 4, 2, 1):
        weights = jnp.concatenate([weights, swap(weights, turn)], 0)
    rim = shape(2, 8, CELLS)
    power, *rims = pl.pallas_call(
        power_kernel,
        out_shape=(shape(GROUPS, 8, CELLS), rim, rim),
        in_specs=[SMEM] + [VMEM] * 4,
        out_specs=(VMEM,) * 3,
        compiler_params=limit(8),
        name="power",
    )(ints, weights, snaps, *edges)
    rims = [
        lax.ppermute(value, "az", pairs)
        for value, pairs in zip(rims, neighbours(8, True))
    ]
    smoothed = pl.pallas_call(
        smooth_kernel,
        out_shape=shape(GROUPS, 8, CELLS),
        in_specs=[VMEM] * 3,
        out_specs=VMEM,
        compiler_params=limit(8),
        name="smooth",
    )(power, *rims)
    return smoothed.reshape(OWN_BEAMS, DBINS, CELLS)


def solution(mesh):
    return jax.shard_map(
        body,
        mesh=mesh,
        in_specs=(P(None, "az", None, "rng"), P(), P(), P(), P(), P("az", "rng")),
        out_specs=P("az", None, "rng"),
        check_vma=False,
    )
```

```python
import functools

import jax
import jax.numpy as jnp
import numpy as np
from jax import lax
from jax.experimental import pallas as pl
from jax.experimental.pallas import tpu as pltpu
from jax.sharding import PartitionSpec as P

COLS = 256
ARC = 64
BINS = 3
BEAMS = 64
BLK = 128
PULSES = 32
SEL = 16
DBINS = 16
DOF = BINS * SEL
OWN_COLS = 32
OWN_BEAMS = 8
CELLS = 128
GROUPS = 16
LANES = 128
SLOTS = PULSES + 3
LOADING = 0.1
F32 = jnp.float32
BF16 = jnp.bfloat16
TRANSPOSED = (((1,), (1,)), ((), ()))


def table_array():
    ids = np.arange(PULSES)
    steps = (ids[:, None] * ids[None, :] % PULSES).astype(np.float32)
    angle = np.float32(-2.0 * np.pi / PULSES) * steps
    real, imag = np.cos(angle), np.sin(angle)
    return np.concatenate(
        [np.concatenate([real, -imag], 1), np.concatenate([imag, real], 1)], 0
    ).astype(jnp.bfloat16)


def lane_ids(rows):
    return lax.broadcasted_iota(jnp.int32, (rows, LANES), 1)


def own_group():
    place = lax.axis_index("rng")
    bits = [lax.rem(lax.div(place, 1 << bit), 2) for bit in range(5)]
    along = exclusive(bits[2], bits[4]) * 2 + exclusive(bits[3], bits[4])
    return bits[0] * 8 + bits[1] * 4 + along


def exclusive(left, right):
    return lax.bitwise_xor(left, right)


def spectra(table, ref, pair, out_ref, base):
    blocks = [
        jnp.concatenate([ref[0, 2 * pair + one], ref[1, 2 * pair + one]], 0)
        for one in range(2)
    ]
    both = jnp.dot(table, jnp.concatenate(blocks, 1), preferred_element_type=F32)
    out_ref[base + 2 * pair] = both[:, :CELLS]
    out_ref[base + 2 * pair + 1] = both[:, CELLS:]


def own_kernel(table_ref, own_ref, spec_ref, passed_ref):
    table = table_ref[...]
    passed_ref[...] = table

    def step(index, carry):
        for one in range(4):
            spectra(table, own_ref, 4 * index + one, spec_ref, 0)
        return carry

    lax.fori_loop(0, OWN_COLS // 8, step, 0)


def gram_kernel(
    ints_ref, floats_ref,
    table_ref, low_ref, own_ref, high_ref, marks_ref,
    snap_ref, keep_ref, send_ref, passed_ref,
    spec_ref, wide_ref,
):
    mine = own_group()
    table = table_ref[...]
    passed_ref[...] = marks_ref[...]

    def transform(index, carry):
        for one in range(2):
            spectra(table, low_ref, 2 * index + one, spec_ref, 0)
            spectra(table, high_ref, 2 * index + one, spec_ref, 2 * OWN_COLS)
        for one in range(4):
            spec_ref[OWN_COLS + 4 * index + one] = own_ref[4 * index + one]
        return carry

    lax.fori_loop(0, OWN_COLS // 4, transform, 0)

    lane = lane_ids(DOF)
    row = lax.broadcasted_iota(jnp.int32, (DOF, LANES), 0)
    lower = row >= lane - jnp.where(lane < DOF, 0, DOF)
    blank = jnp.zeros((LANES - 2 * DOF, 2 * CELLS), BF16)
    last = PULSES * SEL

    def first_group(step):
        return exclusive(exclusive(2 * step, 8), mine)

    def turn(step):
        beam = lax.div(first_group(step), 2)
        for sel in range(SEL):
            column = ints_ref[beam, sel]
            real = spec_ref[column, :PULSES]
            imag = spec_ref[column, PULSES:]
            cosine = floats_ref[beam, sel]
            sine = floats_ref[beam, SEL + sel]
            rows = pl.ds(SEL + sel, PULSES, stride=SEL)
            wide_ref[0, rows, :] = cosine * real - sine * imag
            wide_ref[1, rows, :] = sine * real + cosine * imag
        for part in range(2):
            for low, high, place in (
                (SEL, SEL + last, SEL),
                (last, last + SEL, 0),
                (SEL, 3 * SEL, SEL + last),
            ):
                snap_ref[beam, part, place : place + high - low, :] = wide_ref[
                    part, low:high, :
                ].astype(BF16)

    def multiply(step, out_ref):
        group = first_group(step)
        beam = lax.div(group, 2)
        weight = ints_ref[beam, 2 * SEL].astype(F32)
        for half in range(2):
            base = exclusive(lax.rem(group, 2), half) * 8
            out = [None, None, None]
            for pair in range(4):
                same, turned = [], []
                for one in range(2):
                    centre = ints_ref[beam, SEL + base + pair * 2 + one]
                    rows = pl.ds(pl.multiple_of(centre * SEL, SEL), DOF)
                    real = snap_ref[beam, 0, rows, :]
                    imag = snap_ref[beam, 1, rows, :]
                    same.append(jnp.concatenate([real, imag], 1))
                    turned.append(jnp.concatenate([imag, -real], 1))
                left = jnp.concatenate([same[0], turned[0], same[1], turned[1]], 0)
                right = jnp.concatenate([same[0], same[1], blank], 0)
                gram = lax.dot_general(
                    left, right, TRANSPOSED, preferred_element_type=F32
                )
                packed = jnp.where(
                    lower,
                    jnp.where(lane < DOF, gram[:DOF], gram[2 * DOF : 3 * DOF]),
                    jnp.where(lane < DOF, gram[DOF : 2 * DOF], gram[3 * DOF :]),
                )
                shift = 2 * DOF * pair % LANES
                if shift:
                    packed = pltpu.roll(packed, shift, 1)
                if pair == 0:
                    out[0] = packed
                elif pair == 1:
                    out[0] = jnp.where(lane >= 96, packed, out[0])
                    out[1] = packed
                elif pair == 2:
                    out[1] = jnp.where(lane >= 64, packed, out[1])
                    out[2] = packed
                else:
                    out[2] = jnp.where(lane >= 32, packed, out[2])
            place = lax.rem(2 * step, 8) + half
            for part in range(3):
                out_ref[place, :, LANES * part : LANES * (part + 1)] = (
                    out[part] * weight
                )

    def sending(step, carry):
        turn(step + 1)
        multiply(step, send_ref)
        return carry

    def keeping(step, carry):
        turn(step + 1)
        multiply(step, keep_ref)
        return carry

    turn(0)
    lax.fori_loop(0, 4, sending, 0)
    lax.fori_loop(4, 7, keeping, 0)
    multiply(7, keep_ref)


def edge_out_kernel(snap_ref, first_ref, second_ref):
    rows = 8 * 8
    lane = lane_ids(rows)
    ends = [jnp.zeros((rows, LANES), F32) for _ in range(2)]
    for beam in range(OWN_BEAMS):
        for part in range(2):
            for block in range(8):
                low = SEL + rows * block
                value = snap_ref[beam, part, low : low + rows, :].astype(F32)
                target = 16 * block + 8 * part + beam
                here = lane == target
                for end in range(2):
                    shift = (target + end) % LANES
                    moved = pltpu.roll(value, shift, 1) if shift else value
                    ends[end] = jnp.where(here, moved, ends[end])
    even = lax.rem(lax.axis_index("rng"), 2) == 0
    first_ref[...] = jnp.where(even, ends[1], ends[0]).astype(BF16)
    second_ref[...] = jnp.where(even, ends[0], ends[1]).astype(BF16)


def edge_in_kernel(first_ref, second_ref, direct_ref, turned_ref):
    rows = 8 * 8
    lane = lane_ids(rows)
    first = first_ref[...].astype(F32)
    second = second_ref[...].astype(F32)

    def rolled(value, shift):
        return pltpu.roll(value, shift % LANES, 1) if shift % LANES else value

    for block in range(8):
        both = jnp.where(
            lane < 16, rolled(first, -16 * block), rolled(second, 16 - 16 * block)
        )
        for ref, value in ((direct_ref, both), (turned_ref, rolled(both, -8))):
            value = value.astype(BF16)
            ref[SEL + rows * block : SEL + rows * (block + 1), :] = value
            if block == 0:
                ref[PULSES * SEL + SEL :, :] = value[: 2 * SEL]
            if block == 7:
                ref[:SEL, :] = value[rows - SEL :]


def spread(value, index):
    return jnp.take_along_axis(
        value, jnp.full(value.shape, index, jnp.int32), axis=1
    )


def solve_kernel(first_ref, second_ref, marks_ref, out_ref, turn_ref):
    lane = lane_ids(DOF)
    row = lax.broadcasted_iota(jnp.int32, (DOF, LANES), 0)
    slot = lax.div(lane, SEL)
    lower = row >= lane
    same = row == lane
    total = first_ref[...] + second_ref[...]
    parts = [total[:, LANES * i : LANES * (i + 1)] for i in range(3)]
    block_a = [None] * BINS
    block_b = [None] * BINS
    for pair in range(4):
        if pair == 0:
            packed = parts[0]
        elif pair == 1:
            packed = jnp.where(
                lane < 32, pltpu.roll(parts[0], 32, 1), pltpu.roll(parts[1], 32, 1)
            )
        elif pair == 2:
            packed = jnp.where(
                lane < 64, pltpu.roll(parts[1], 64, 1), pltpu.roll(parts[2], 64, 1)
            )
        else:
            packed = pltpu.roll(parts[2], 96, 1)
        square = jnp.concatenate([packed, jnp.zeros((LANES - DOF, LANES), F32)], 0)
        turned = jnp.transpose(square)
        for one in range(2):
            item = pair * 2 + one
            here = packed if one == 0 else pltpu.roll(packed, LANES - DOF, 1)
            there = turned[one * DOF : (one + 1) * DOF]
            value_a = jnp.where(lower, here, there)
            value_b = jnp.where(lower, jnp.where(same, 0.0, -there), here)
            if item:
                value_a = pltpu.roll(value_a, SEL * item, 1)
                value_b = pltpu.roll(value_b, SEL * item, 1)
            for part in range(BINS):
                if item == 0:
                    block_a[part] = value_a
                    block_b[part] = value_b
                else:
                    chosen = slot == (item + part) % 8
                    block_a[part] = jnp.where(chosen, value_a, block_a[part])
                    block_b[part] = jnp.where(chosen, value_b, block_b[part])
    for part in range(1, BINS):
        block_a[part] = pltpu.roll(block_a[part], LANES - SEL * part, 1)
        block_b[part] = pltpu.roll(block_b[part], LANES - SEL * part, 1)
    small = lane_ids(8)
    line = lax.broadcasted_iota(jnp.int32, (8, LANES), 0)
    place = lax.rem(small, SEL)
    base = small - place
    diagonal = jnp.zeros((8, LANES), F32)
    masks = []
    for group in range(DOF // 8):
        masks.append(place == line + group % 2 * 8)
        diagonal = diagonal + jnp.where(
            masks[group], block_a[group // 2][8 * group : 8 * group + 8], 0.0
        )
    level = jnp.sum(diagonal, axis=0, keepdims=True)
    level = jnp.broadcast_to(level, (8, LANES))
    for step in (1, 2, 4, 8):
        partner = base + lax.rem(place + step, SEL)
        level = level + jnp.take_along_axis(level, partner, axis=1)
    level = LOADING / DOF * level
    real = [[None] * 4 for _ in range(6)]
    imag = [[None] * 4 for _ in range(6)]
    for group in range(6):
        for part in range(BINS):
            real[group][part] = block_a[part][8 * group : 8 * group + 8]
            imag[group][part] = block_b[part][8 * group : 8 * group + 8]
        real[group][group // 2] = jnp.where(
            masks[group], real[group][group // 2] + level, real[group][group // 2]
        )
        real[group][3] = jnp.ones((8, LANES), F32)
        imag[group][3] = jnp.zeros((8, LANES), F32)
    inverse = [jnp.ones((8, LANES), F32)] * 6
    for k in range(DOF):
        group, inner, part = k // 8, k % 8, k // SEL
        index = base + k % SEL
        mult_re = [jnp.take_along_axis(real[i][part], index, axis=1) for i in range(6)]
        mult_im = [jnp.take_along_axis(imag[i][part], index, axis=1) for i in range(6)]
        pivot = jnp.broadcast_to(mult_re[group][inner : inner + 1], (8, LANES))
        pivot = 1.0 / pivot
        here = line == inner
        mult_re[group] = jnp.where(here, 0.0, mult_re[group])
        mult_im[group] = jnp.where(here, 0.0, mult_im[group])
        inverse[group] = jnp.where(here, pivot, inverse[group])
        for block in (*range(part, BINS), 3):
            row_re = pivot * jnp.broadcast_to(
                real[group][block][inner : inner + 1], (8, LANES)
            )
            row_im = pivot * jnp.broadcast_to(
                imag[group][block][inner : inner + 1], (8, LANES)
            )
            for i in range(6):
                real[i][block] = (
                    real[i][block] - mult_re[i] * row_re + mult_im[i] * row_im
                )
                imag[i][block] = (
                    imag[i][block] - mult_re[i] * row_im - mult_im[i] * row_re
                )
    gap = jnp.zeros((SEL, LANES), F32)
    found_re = [real[i][3] * inverse[i] for i in range(6)]
    found_im = [imag[i][3] * inverse[i] for i in range(6)]
    quiet = found_re[0]
    for i in range(1, 6):
        quiet = quiet + found_re[i]
    quiet = jnp.broadcast_to(jnp.sum(quiet, axis=0, keepdims=True), (SEL, LANES))
    turn_ref[...] = jnp.transpose(
        jnp.concatenate([*found_re, quiet, *found_im, gap], 0)
    )
    found = turn_ref[pl.ds(0, 8, stride=SEL), :]
    out_ref[...] = jnp.where(small == 120, marks_ref[...], found)


def power_kernel(
    ints_ref, weights_ref, snap_ref, direct_ref, turned_ref,
    power_ref, first_ref, second_ref,
):
    mine = own_group()
    even = lax.rem(lax.axis_index("rng"), 2) == 0
    small = lane_ids(8)
    counts = jnp.zeros((8, LANES), F32)
    for place in range(GROUPS):
        counts = counts + weights_ref[place]
    counts = spread(counts, 120) * BLK
    used = jnp.logical_or(
        small < DOF, jnp.logical_and(small >= 64, small < 64 + DOF)
    )
    row = lax.broadcasted_iota(jnp.int32, (2 * 8, 2 * LANES), 0)
    low_lane = jnp.where(even, 16, 0)
    for group in range(GROUPS):
        beam = group // 2
        scaled = weights_ref[exclusive(mine, group)] * counts[beam : beam + 1, :]
        quiet = spread(scaled, 56)
        direct = jnp.where(used, scaled, 0.0)
        turned = pltpu.roll(direct, 64, 1)
        turned = jnp.where(small < 64, -turned, turned)
        left = jnp.concatenate([direct, turned], 0).astype(BF16)
        found = jnp.zeros((16, 2 * LANES), F32)
        for one in range(8):
            centre = ints_ref[beam, SEL + (group % 2) * 8 + one]
            rows = pl.ds(pl.multiple_of(centre * SEL, SEL), 64)
            right = jnp.concatenate(
                [
                    jnp.concatenate([snap_ref[beam, 0, rows, :], direct_ref[rows, :]], 1),
                    jnp.concatenate([snap_ref[beam, 1, rows, :], turned_ref[rows, :]], 1),
                ],
                0,
            )
            product = jnp.dot(left, right, preferred_element_type=F32)
            found = jnp.where(lax.rem(row, 8) == one, product, found)
        power = found[:8] * found[:8] + found[8:] * found[8:]
        inner = power[:, :LANES] / quiet
        outer = power[:, LANES:] / quiet
        low = spread(outer, beam + low_lane)
        high = spread(outer, beam + 16 - low_lane)
        below = jnp.where(small == 0, low, pltpu.roll(inner, 1, 1))
        above = jnp.where(small == LANES - 1, high, pltpu.roll(inner, LANES - 1, 1))
        power_ref[group] = below + inner + above
    even = lax.rem(lax.axis_index("az"), 2) == 0
    for half in range(2):
        bottom, top = power_ref[half], power_ref[GROUPS - 2 + half]
        first_ref[half] = jnp.where(even, top, bottom)
        second_ref[half] = jnp.where(even, bottom, top)


def smooth_kernel(power_ref, first_ref, second_ref, out_ref):
    even = lax.rem(lax.axis_index("az"), 2) == 0
    first, second = first_ref[...], second_ref[...]
    low = jnp.where(even, second, first)
    high = jnp.where(even, first, second)
    for beam in range(OWN_BEAMS):
        below = low if beam == 0 else power_ref[2 * beam - 2 : 2 * beam]
        above = (
            high if beam == OWN_BEAMS - 1 else power_ref[2 * beam + 2 : 2 * beam + 4]
        )
        here = power_ref[2 * beam : 2 * beam + 2]
        out_ref[2 * beam : 2 * beam + 2] = (below + here + above) / 9.0


def swap(value, turn):
    return lax.ppermute(value, "rng", [(i, i ^ turn) for i in range(32)])


def halo_columns(echoes):
    ring = [(i, (i + 1) % 8) for i in range(8)]
    low = lax.ppermute(echoes, "az", ring)
    high = lax.ppermute(echoes, "az", [(b, a) for a, b in ring])
    return low, high


SMEM = pl.BlockSpec(memory_space=pltpu.SMEM)
VMEM = pl.BlockSpec(memory_space=pltpu.VMEM)


def limit(mebibytes):
    return pltpu.CompilerParams(vmem_limit_bytes=mebibytes * 2**20)


def shape(*dims, dtype=F32):
    return jax.ShapeDtypeStruct(dims, dtype)


def neighbours(count, closed):
    nearest = [(i, i ^ 1) for i in range(count)]
    across = [(i, i + 1) if i % 2 else (i, i - 1) for i in range(count)]
    if closed:
        across = [(a, b % count) for a, b in across]
    else:
        across = [(a, b) for a, b in across if 0 <= b < count]
    return nearest, across


def body(echoes, arc_start, arc_offsets, doppler_bins, steer_angles, train_mask):
    low, high = halo_columns(echoes)
    az = lax.axis_index("az")

    def own(value):
        return lax.dynamic_slice_in_dim(value, az * OWN_BEAMS, OWN_BEAMS, 0)

    marks = jnp.broadcast_to(train_mask.astype(F32), (OWN_BEAMS, LANES))
    marks = marks + swap(marks, 28)
    first = (own(arc_start) - az * OWN_COLS + ARC // 2) % COLS
    ints = jnp.concatenate(
        [first[:, None] + own(arc_offsets), own(doppler_bins), train_mask], 1
    )
    angles = own(steer_angles)
    floats = jnp.concatenate([jnp.cos(angles), jnp.sin(angles)], 1)
    spec, table = pl.pallas_call(
        own_kernel,
        out_shape=(
            shape(OWN_COLS, 2 * PULSES, CELLS),
            shape(2 * PULSES, 2 * PULSES, dtype=BF16),
        ),
        in_specs=[VMEM, VMEM],
        out_specs=(VMEM, VMEM),
        compiler_params=limit(8),
        name="spectra",
    )(jnp.asarray(table_array()), echoes)
    half = shape(8, DOF, 8 * DOF)
    snaps, keep, send, marks = pl.pallas_call(
        gram_kernel,
        out_shape=(
            shape(OWN_BEAMS, 2, SLOTS * SEL, CELLS, dtype=BF16),
            half,
            half,
            shape(OWN_BEAMS, LANES),
        ),
        in_specs=[SMEM] * 2 + [VMEM] * 5,
        out_specs=(VMEM,) * 4,
        scratch_shapes=[
            pltpu.VMEM((3 * OWN_COLS, 2 * PULSES, CELLS), F32),
            pltpu.VMEM((2, SLOTS * SEL, CELLS), F32),
        ],
        compiler_params=limit(16),
        name="grams",
    )(ints, floats, table, low, spec, high, marks)
    edge = shape(64, LANES, dtype=BF16)
    edges = pl.pallas_call(
        edge_out_kernel,
        out_shape=(edge, edge),
        in_specs=[VMEM],
        out_specs=(VMEM, VMEM),
        compiler_params=limit(8),
        name="edges_out",
    )(snaps)
    moved, edges = lax.optimization_barrier((swap(send, 1), edges))
    part = keep + moved
    moved = [swap(part[2:4], 4), swap(part[4:6], 2), swap(part[6:], 6)]
    edges = [
        lax.ppermute(value, "rng", pairs)
        for value, pairs in zip(edges, neighbours(32, False))
    ]
    moved, edges = lax.optimization_barrier((moved, edges))
    part = part[:2] + moved[0] + moved[1] + moved[2]
    part = part[0] + swap(part[1], 8)
    other = swap(part, 28)
    edge = shape(SLOTS * SEL, LANES, dtype=BF16)
    edges = pl.pallas_call(
        edge_in_kernel,
        out_shape=(edge, edge),
        in_specs=[VMEM, VMEM],
        out_specs=(VMEM, VMEM),
        compiler_params=limit(8),
        name="edges_in",
    )(*edges)
    other, edges = lax.optimization_barrier((other, edges))
    weights = pl.pallas_call(
        solve_kernel,
        out_shape=shape(8, LANES),
        in_specs=[VMEM] * 3,
        out_specs=VMEM,
        scratch_shapes=[pltpu.VMEM((LANES, LANES), F32)],
        compiler_params=limit(8),
        name="solve",
    )(part, other, marks)
    weights = weights[None]
    for turn in (8, 4, 2, 1):
        weights = jnp.concatenate([weights, swap(weights, turn)], 0)
    rim = shape(2, 8, CELLS)
    power, *rims = pl.pallas_call(
        power_kernel,
        out_shape=(shape(GROUPS, 8, CELLS), rim, rim),
        in_specs=[SMEM] + [VMEM] * 4,
        out_specs=(VMEM,) * 3,
        compiler_params=limit(8),
        name="power",
    )(ints, weights, snaps, *edges)
    rims = [
        lax.ppermute(value, "az", pairs)
        for value, pairs in zip(rims, neighbours(8, True))
    ]
    smoothed = pl.pallas_call(
        smooth_kernel,
        out_shape=shape(GROUPS, 8, CELLS),
        in_specs=[VMEM] * 3,
        out_specs=VMEM,
        compiler_params=limit(8),
        name="smooth",
    )(power, *rims)
    return smoothed.reshape(OWN_BEAMS, DBINS, CELLS)


def solution(mesh):
    return jax.shard_map(
        body,
        mesh=mesh,
        in_specs=(P(None, "az", None, "rng"), P(), P(), P(), P(), P("az", "rng")),
        out_specs=P("az", None, "rng"),
        check_vma=False,
    )
```

```python
import functools

import jax
import jax.numpy as jnp
import numpy as np
from jax import lax
from jax.experimental import pallas as pl
from jax.experimental.pallas import tpu as pltpu
from jax.sharding import PartitionSpec as P

COLS = 256
ARC = 64
BINS = 3
BEAMS = 64
BLK = 128
PULSES = 32
SEL = 16
DBINS = 16
DOF = BINS * SEL
OWN_COLS = 32
OWN_BEAMS = 8
CELLS = 128
GROUPS = 16
LANES = 128
SLOTS = PULSES + 8
LOADING = 0.1
F32 = jnp.float32
BF16 = jnp.bfloat16
TRANSPOSED = (((1,), (1,)), ((), ()))


def table_array():
    ids = np.arange(PULSES)
    steps = (ids[:, None] * ids[None, :] % PULSES).astype(np.float32)
    angle = np.float32(-2.0 * np.pi / PULSES) * steps
    real, imag = np.cos(angle), np.sin(angle)
    return np.concatenate(
        [np.concatenate([real, -imag], 1), np.concatenate([imag, real], 1)], 0
    ).astype(jnp.bfloat16)


def lane_ids(rows):
    return lax.broadcasted_iota(jnp.int32, (rows, LANES), 1)


def own_group():
    place = lax.axis_index("rng")
    bits = [lax.rem(lax.div(place, 1 << bit), 2) for bit in range(5)]
    along = exclusive(bits[2], bits[4]) * 2 + exclusive(bits[3], bits[4])
    return bits[0] * 8 + bits[1] * 4 + along


def exclusive(left, right):
    return lax.bitwise_xor(left, right)


def spectra(table, ref, pair, out_ref, base):
    blocks = [
        jnp.concatenate([ref[0, 2 * pair + one], ref[1, 2 * pair + one]], 0)
        for one in range(2)
    ]
    both = jnp.dot(table, jnp.concatenate(blocks, 1), preferred_element_type=F32)
    out_ref[base + 2 * pair] = both[:, :CELLS]
    out_ref[base + 2 * pair + 1] = both[:, CELLS:]


def own_kernel(table_ref, own_ref, spec_ref, passed_ref):
    table = table_ref[...]
    passed_ref[...] = table

    def step(index, carry):
        for one in range(4):
            spectra(table, own_ref, 4 * index + one, spec_ref, 0)
        return carry

    lax.fori_loop(0, OWN_COLS // 8, step, 0)


def gram_kernel(
    ints_ref, floats_ref,
    table_ref, low_ref, own_ref, high_ref, marks_ref,
    snap_ref, keep_ref, send_ref, passed_ref,
    spec_ref, wide_ref, even_ref, odd_ref,
):
    mine = own_group()
    table = table_ref[...]
    passed_ref[...] = marks_ref[...]

    def transform(index, carry):
        for one in range(2):
            spectra(table, low_ref, 2 * index + one, spec_ref, 0)
        for one in range(4):
            spec_ref[OWN_COLS + 4 * index + one] = own_ref[4 * index + one]
            spec_ref[2 * OWN_COLS + 4 * index + one] = high_ref[4 * index + one]
        return carry

    lax.fori_loop(0, OWN_COLS // 4, transform, 0)

    lane = lane_ids(DOF)
    row = lax.broadcasted_iota(jnp.int32, (DOF, LANES), 0)
    lower = row >= lane - jnp.where(lane < DOF, 0, DOF)
    blank = jnp.zeros((LANES - 2 * DOF, 2 * CELLS), BF16)
    last = PULSES * SEL

    def first_group(step):
        return exclusive(exclusive(2 * step, 8), mine)

    def turn(step, work_ref):
        beam = lax.div(first_group(step), 2)
        for sel in range(SEL):
            column = ints_ref[beam, sel]
            real = spec_ref[column, :PULSES]
            imag = spec_ref[column, PULSES:]
            cosine = floats_ref[beam, sel]
            sine = floats_ref[beam, SEL + sel]
            rows = pl.ds(SEL + sel, PULSES, stride=SEL)
            wide_ref[0, rows, :] = cosine * real - sine * imag
            wide_ref[1, rows, :] = sine * real + cosine * imag
        for part in range(2):
            for low, high, place in (
                (SEL, SEL + last, SEL),
                (last, last + SEL, 0),
                (SEL, 2 * SEL, SEL + last),
            ):
                value = wide_ref[part, low:high, :].astype(BF16)
                work_ref[part, place : place + high - low, :] = value
                snap_ref[beam, part, place : place + high - low, :] = value
            snap_ref[beam, part, last + 2 * SEL :, :] = jnp.zeros(
                (SLOTS * SEL - last - 2 * SEL, CELLS), BF16
            )

    def multiply(step, work_ref, out_ref):
        group = first_group(step)
        beam = lax.div(group, 2)
        weight = ints_ref[beam, 2 * SEL].astype(F32)
        for half in range(2):
            base = exclusive(lax.rem(group, 2), half) * 8
            out = [None, None, None]
            for pair in range(4):
                same, turned = [], []
                for one in range(2):
                    centre = ints_ref[beam, SEL + base + pair * 2 + one]
                    rows = pl.ds(pl.multiple_of(centre * SEL, SEL), DOF)
                    real = work_ref[0, rows, :]
                    imag = work_ref[1, rows, :]
                    same.append(jnp.concatenate([real, imag], 1))
                    turned.append(jnp.concatenate([imag, -real], 1))
                left = jnp.concatenate([same[0], turned[0], same[1], turned[1]], 0)
                right = jnp.concatenate([same[0], same[1], blank], 0)
                gram = lax.dot_general(
                    left, right, TRANSPOSED, preferred_element_type=F32
                )
                packed = jnp.where(
                    lower,
                    jnp.where(lane < DOF, gram[:DOF], gram[2 * DOF : 3 * DOF]),
                    jnp.where(lane < DOF, gram[DOF : 2 * DOF], gram[3 * DOF :]),
                )
                shift = 2 * DOF * pair % LANES
                if shift:
                    packed = pltpu.roll(packed, shift, 1)
                if pair == 0:
                    out[0] = packed
                elif pair == 1:
                    out[0] = jnp.where(lane >= 96, packed, out[0])
                    out[1] = packed
                elif pair == 2:
                    out[1] = jnp.where(lane >= 64, packed, out[1])
                    out[2] = packed
                else:
                    out[2] = jnp.where(lane >= 32, packed, out[2])
            place = lax.rem(2 * step, 8) + half
            for part in range(3):
                out_ref[place, :, LANES * part : LANES * (part + 1)] = (
                    out[part] * weight
                )

    def sending(index, carry):
        turn(2 * index + 1, odd_ref)
        multiply(2 * index, even_ref, send_ref)
        turn(2 * index + 2, even_ref)
        multiply(2 * index + 1, odd_ref, send_ref)
        return carry

    turn(0, even_ref)
    lax.fori_loop(0, 2, sending, 0)
    turn(5, odd_ref)
    multiply(4, even_ref, keep_ref)
    turn(6, even_ref)
    multiply(5, odd_ref, keep_ref)
    turn(7, odd_ref)
    multiply(6, even_ref, keep_ref)
    multiply(7, odd_ref, keep_ref)


def edge_out_kernel(snap_ref, first_ref, second_ref):
    rows = 8 * 8
    lane = lane_ids(rows)
    ends = [jnp.zeros((rows, LANES), F32) for _ in range(2)]
    for beam in range(OWN_BEAMS):
        for part in range(2):
            for block in range(8):
                low = SEL + rows * block
                value = snap_ref[beam, part, low : low + rows, :].astype(F32)
                target = 16 * block + 8 * part + beam
                here = lane == target
                for end in range(2):
                    shift = (target + end) % LANES
                    moved = pltpu.roll(value, shift, 1) if shift else value
                    ends[end] = jnp.where(here, moved, ends[end])
    even = lax.rem(lax.axis_index("rng"), 2) == 0
    first_ref[...] = jnp.where(even, ends[1], ends[0]).astype(BF16)
    second_ref[...] = jnp.where(even, ends[0], ends[1]).astype(BF16)


def edge_in_kernel(first_ref, second_ref, out_ref):
    rows = 8 * 8
    last = PULSES * SEL
    lane = lane_ids(rows)
    first = first_ref[...].astype(F32)
    second = second_ref[...].astype(F32)

    def rolled(value, shift):
        return pltpu.roll(value, shift % LANES, 1) if shift % LANES else value

    for block in range(8):
        both = jnp.where(
            lane < 16, rolled(first, -16 * block), rolled(second, 16 - 16 * block)
        )
        for part, value in enumerate((both, rolled(both, -8))):
            value = value.astype(BF16)
            out_ref[part, SEL + rows * block : SEL + rows * (block + 1), :] = value
            if block == 0:
                out_ref[part, last + SEL : last + 2 * SEL, :] = value[:SEL]
            if block == 7:
                out_ref[part, :SEL, :] = value[rows - SEL :]
    for part in range(2):
        out_ref[part, last + 2 * SEL :, :] = jnp.zeros(
            (SLOTS * SEL - last - 2 * SEL, CELLS), BF16
        )


def spread(value, index):
    return jnp.take_along_axis(
        value, jnp.full(value.shape, index, jnp.int32), axis=1
    )


def solve_kernel(first_ref, second_ref, marks_ref, out_ref, turn_ref):
    lane = lane_ids(DOF)
    row = lax.broadcasted_iota(jnp.int32, (DOF, LANES), 0)
    slot = lax.div(lane, SEL)
    lower = row >= lane
    same = row == lane
    total = first_ref[...] + second_ref[...]
    parts = [total[:, LANES * i : LANES * (i + 1)] for i in range(3)]
    block_a = [None] * BINS
    block_b = [None] * BINS
    for pair in range(4):
        if pair == 0:
            packed = parts[0]
        elif pair == 1:
            packed = jnp.where(
                lane < 32, pltpu.roll(parts[0], 32, 1), pltpu.roll(parts[1], 32, 1)
            )
        elif pair == 2:
            packed = jnp.where(
                lane < 64, pltpu.roll(parts[1], 64, 1), pltpu.roll(parts[2], 64, 1)
            )
        else:
            packed = pltpu.roll(parts[2], 96, 1)
        square = jnp.concatenate([packed, jnp.zeros((LANES - DOF, LANES), F32)], 0)
        turned = jnp.transpose(square)
        for one in range(2):
            item = pair * 2 + one
            here = packed if one == 0 else pltpu.roll(packed, LANES - DOF, 1)
            there = turned[one * DOF : (one + 1) * DOF]
            value_a = jnp.where(lower, here, there)
            value_b = jnp.where(lower, jnp.where(same, 0.0, -there), here)
            if item:
                value_a = pltpu.roll(value_a, SEL * item, 1)
                value_b = pltpu.roll(value_b, SEL * item, 1)
            for part in range(BINS):
                if item == 0:
                    block_a[part] = value_a
                    block_b[part] = value_b
                else:
                    chosen = slot == (item + part) % 8
                    block_a[part] = jnp.where(chosen, value_a, block_a[part])
                    block_b[part] = jnp.where(chosen, value_b, block_b[part])
    for part in range(1, BINS):
        block_a[part] = pltpu.roll(block_a[part], LANES - SEL * part, 1)
        block_b[part] = pltpu.roll(block_b[part], LANES - SEL * part, 1)
    small = lane_ids(8)
    line = lax.broadcasted_iota(jnp.int32, (8, LANES), 0)
    place = lax.rem(small, SEL)
    base = small - place
    diagonal = jnp.zeros((8, LANES), F32)
    masks = []
    for group in range(DOF // 8):
        masks.append(place == line + group % 2 * 8)
        diagonal = diagonal + jnp.where(
            masks[group], block_a[group // 2][8 * group : 8 * group + 8], 0.0
        )
    level = jnp.sum(diagonal, axis=0, keepdims=True)
    level = jnp.broadcast_to(level, (8, LANES))
    for step in (1, 2, 4, 8):
        partner = base + lax.rem(place + step, SEL)
        level = level + jnp.take_along_axis(level, partner, axis=1)
    level = LOADING / DOF * level
    real = [[None] * 4 for _ in range(6)]
    imag = [[None] * 4 for _ in range(6)]
    for group in range(6):
        for part in range(BINS):
            real[group][part] = block_a[part][8 * group : 8 * group + 8]
            imag[group][part] = block_b[part][8 * group : 8 * group + 8]
        real[group][group // 2] = jnp.where(
            masks[group], real[group][group // 2] + level, real[group][group // 2]
        )
        real[group][3] = jnp.ones((8, LANES), F32)
        imag[group][3] = jnp.zeros((8, LANES), F32)
    inverse = [jnp.ones((8, LANES), F32)] * 6
    for k in range(0, DOF, 2):
        group, inner, part = k // 8, k % 8, k // SEL
        columns = []
        for step in range(2):
            index = base + k % SEL + step
            columns.append(
                [
                    [
                        jnp.take_along_axis(half[i][part], index, axis=1)
                        for i in range(6)
                    ]
                    for half in (real, imag)
                ]
            )
        (zero_re, zero_im), (one_re, one_im) = columns

        def line_of(value, offset):
            return jnp.broadcast_to(
                value[inner + offset : inner + offset + 1], (8, LANES)
            )

        side_re, side_im = line_of(one_re[group], 0), line_of(one_im[group], 0)
        below_re, below_im = line_of(zero_re[group], 1), line_of(zero_im[group], 1)
        first = 1.0 / line_of(zero_re[group], 0)
        below_re, below_im = below_re * first, below_im * first
        second = 1.0 / (
            line_of(one_re[group], 1) - below_re * side_re + below_im * side_im
        )
        upper, under = line == inner, line == inner + 1
        inverse[group] = jnp.where(
            upper, first, jnp.where(under, second, inverse[group])
        )
        zero_re[group] = jnp.where(upper, 0.0, zero_re[group])
        zero_im[group] = jnp.where(upper, 0.0, zero_im[group])
        alpha_re = [value * first for value in zero_re]
        alpha_im = [value * first for value in zero_im]
        beta_re = [
            (one_re[i] - alpha_re[i] * side_re + alpha_im[i] * side_im) * second
            for i in range(6)
        ]
        beta_im = [
            (one_im[i] - alpha_re[i] * side_im - alpha_im[i] * side_re) * second
            for i in range(6)
        ]
        beta_re[group] = jnp.where(under, 0.0, beta_re[group])
        beta_im[group] = jnp.where(under, 0.0, beta_im[group])
        for block in (*range(part, BINS), 3):
            row_re = line_of(real[group][block], 0)
            row_im = line_of(imag[group][block], 0)
            next_re = (
                line_of(real[group][block], 1) - below_re * row_re + below_im * row_im
            )
            next_im = (
                line_of(imag[group][block], 1) - below_re * row_im - below_im * row_re
            )
            for i in range(6):
                real[i][block] = (
                    real[i][block]
                    - alpha_re[i] * row_re
                    + alpha_im[i] * row_im
                    - beta_re[i] * next_re
                    + beta_im[i] * next_im
                )
                imag[i][block] = (
                    imag[i][block]
                    - alpha_re[i] * row_im
                    - alpha_im[i] * row_re
                    - beta_re[i] * next_im
                    - beta_im[i] * next_re
                )
    gap = jnp.zeros((SEL, LANES), F32)
    found_re = [real[i][3] * inverse[i] for i in range(6)]
    found_im = [imag[i][3] * inverse[i] for i in range(6)]
    quiet = found_re[0]
    for i in range(1, 6):
        quiet = quiet + found_re[i]
    quiet = jnp.broadcast_to(jnp.sum(quiet, axis=0, keepdims=True), (SEL, LANES))
    turn_ref[...] = jnp.transpose(
        jnp.concatenate([*found_re, quiet, *found_im, gap], 0)
    )
    found = turn_ref[pl.ds(0, 8, stride=SEL), :]
    out_ref[...] = jnp.where(small == 120, marks_ref[...], found)


def power_kernel(
    bins_ref, weights_ref, snap_ref, edge_ref,
    power_ref, first_ref, second_ref,
):
    mine = own_group()
    even = lax.rem(lax.axis_index("rng"), 2) == 0
    small = lane_ids(8)
    counts = jnp.zeros((8, LANES), F32)
    for place in range(GROUPS):
        counts = counts + weights_ref[place]
    counts = spread(counts, 120) * BLK
    low_lane = jnp.where(even, 16, 0)
    rows = SLOTS * SEL
    edge = edge_ref[...].reshape(2 * rows, LANES)
    for beam in range(OWN_BEAMS):
        lefts, quiets = [], []
        for group in (2 * beam, 2 * beam + 1):
            scaled = weights_ref[exclusive(mine, group)] * counts[beam : beam + 1, :]
            quiets.append(spread(scaled, 56))
            away = small - bins_ref[group] * SEL
            left = [[], []]
            for tile in range(rows // LANES):
                index = away + LANES * tile
                inside = jnp.logical_and(index >= 0, index < DOF)
                direct = jnp.take_along_axis(
                    scaled, lax.bitwise_and(index, LANES - 1), axis=1
                )
                crossed = jnp.take_along_axis(
                    scaled, lax.bitwise_and(index + 64, LANES - 1), axis=1
                )
                direct = jnp.where(inside, direct, 0.0)
                crossed = jnp.where(inside, crossed, 0.0)
                left[0].append(jnp.concatenate([direct, -crossed], 0).astype(BF16))
                left[1].append(jnp.concatenate([crossed, direct], 0).astype(BF16))
            lefts.append(jnp.concatenate(left[0] + left[1], 1))
        right = jnp.concatenate([snap_ref[beam].reshape(2 * rows, LANES), edge], 1)
        found = jnp.dot(
            jnp.concatenate(lefts, 0), right, preferred_element_type=F32
        )
        found = found * found
        for half in range(2):
            power = found[16 * half : 16 * half + 8] + found[16 * half + 8 : 16 * half + 16]
            inner = power[:, :LANES] / quiets[half]
            outer = power[:, LANES:] / quiets[half]
            low = spread(outer, beam + low_lane)
            high = spread(outer, beam + 16 - low_lane)
            below = jnp.where(small == 0, low, pltpu.roll(inner, 1, 1))
            above = jnp.where(
                small == LANES - 1, high, pltpu.roll(inner, LANES - 1, 1)
            )
            power_ref[2 * beam + half] = below + inner + above
    even = lax.rem(lax.axis_index("az"), 2) == 0
    for half in range(2):
        bottom, top = power_ref[half], power_ref[GROUPS - 2 + half]
        first_ref[half] = jnp.where(even, top, bottom)
        second_ref[half] = jnp.where(even, bottom, top)


def smooth_kernel(power_ref, first_ref, second_ref, out_ref):
    even = lax.rem(lax.axis_index("az"), 2) == 0
    first, second = first_ref[...], second_ref[...]
    low = jnp.where(even, second, first)
    high = jnp.where(even, first, second)
    for beam in range(OWN_BEAMS):
        below = low if beam == 0 else power_ref[2 * beam - 2 : 2 * beam]
        above = (
            high if beam == OWN_BEAMS - 1 else power_ref[2 * beam + 2 : 2 * beam + 4]
        )
        here = power_ref[2 * beam : 2 * beam + 2]
        out_ref[2 * beam : 2 * beam + 2] = (below + here + above) / 9.0


def swap(value, turn):
    return lax.ppermute(value, "rng", [(i, i ^ turn) for i in range(32)])


def halo_columns(echoes):
    ring = [(i, (i + 1) % 8) for i in range(8)]
    low = lax.ppermute(echoes, "az", ring)
    high = lax.ppermute(echoes, "az", [(b, a) for a, b in ring])
    return low, high


SMEM = pl.BlockSpec(memory_space=pltpu.SMEM)
VMEM = pl.BlockSpec(memory_space=pltpu.VMEM)


def limit(mebibytes):
    return pltpu.CompilerParams(vmem_limit_bytes=mebibytes * 2**20)


def shape(*dims, dtype=F32):
    return jax.ShapeDtypeStruct(dims, dtype)


def neighbours(count, closed):
    nearest = [(i, i ^ 1) for i in range(count)]
    across = [(i, i + 1) if i % 2 else (i, i - 1) for i in range(count)]
    if closed:
        across = [(a, b % count) for a, b in across]
    else:
        across = [(a, b) for a, b in across if 0 <= b < count]
    return nearest, across


def body(echoes, arc_start, arc_offsets, doppler_bins, steer_angles, train_mask):
    low, high = halo_columns(echoes)
    az = lax.axis_index("az")

    def own(value):
        return lax.dynamic_slice_in_dim(value, az * OWN_BEAMS, OWN_BEAMS, 0)

    marks = jnp.broadcast_to(train_mask.astype(F32), (OWN_BEAMS, LANES))
    marks = marks + swap(marks, 28)
    first = (own(arc_start) - az * OWN_COLS + ARC // 2) % COLS
    ints = jnp.concatenate(
        [first[:, None] + own(arc_offsets), own(doppler_bins), train_mask], 1
    )
    angles = own(steer_angles)
    floats = jnp.concatenate([jnp.cos(angles), jnp.sin(angles)], 1)
    centres = jnp.broadcast_to(
        own(doppler_bins).reshape(GROUPS, 8, 1), (GROUPS, 8, LANES)
    )
    transform = pl.pallas_call(
        own_kernel,
        out_shape=(
            shape(OWN_COLS, 2 * PULSES, CELLS),
            shape(2 * PULSES, 2 * PULSES, dtype=BF16),
        ),
        in_specs=[VMEM, VMEM],
        out_specs=(VMEM, VMEM),
        compiler_params=limit(8),
        name="spectra",
    )
    spec, table = transform(jnp.asarray(table_array()), echoes)
    high, table = transform(table, high)
    half = shape(8, DOF, 8 * DOF)
    snaps, keep, send, marks = pl.pallas_call(
        gram_kernel,
        out_shape=(
            shape(OWN_BEAMS, 2, SLOTS * SEL, CELLS, dtype=BF16),
            half,
            half,
            shape(OWN_BEAMS, LANES),
        ),
        in_specs=[SMEM] * 2 + [VMEM] * 5,
        out_specs=(VMEM,) * 4,
        scratch_shapes=[
            pltpu.VMEM((3 * OWN_COLS, 2 * PULSES, CELLS), F32),
            pltpu.VMEM((2, (PULSES + 1) * SEL, CELLS), F32),
            pltpu.VMEM((2, (PULSES + 2) * SEL, CELLS), BF16),
            pltpu.VMEM((2, (PULSES + 2) * SEL, CELLS), BF16),
        ],
        compiler_params=limit(16),
        name="grams",
    )(ints, floats, table, low, spec, high, marks)
    edge = shape(64, LANES, dtype=BF16)
    edges = pl.pallas_call(
        edge_out_kernel,
        out_shape=(edge, edge),
        in_specs=[VMEM],
        out_specs=(VMEM, VMEM),
        compiler_params=limit(8),
        name="edges_out",
    )(snaps)
    moved, edges = lax.optimization_barrier((swap(send, 1), edges))
    part = keep + moved
    moved = [swap(part[2:4], 4), swap(part[4:6], 2), swap(part[6:], 6)]
    edges = [
        lax.ppermute(value, "rng", pairs)
        for value, pairs in zip(edges, neighbours(32, False))
    ]
    moved, edges = lax.optimization_barrier((moved, edges))
    part = part[:2] + moved[0] + moved[1] + moved[2]
    part = part[0] + swap(part[1], 8)
    other = swap(part, 28)
    edges = pl.pallas_call(
        edge_in_kernel,
        out_shape=shape(2, SLOTS * SEL, LANES, dtype=BF16),
        in_specs=[VMEM, VMEM],
        out_specs=VMEM,
        compiler_params=limit(8),
        name="edges_in",
    )(*edges)
    other, edges = lax.optimization_barrier((other, edges))
    weights = pl.pallas_call(
        solve_kernel,
        out_shape=shape(8, LANES),
        in_specs=[VMEM] * 3,
        out_specs=VMEM,
        scratch_shapes=[pltpu.VMEM((LANES, LANES), F32)],
        compiler_params=limit(8),
        name="solve",
    )(part, other, marks)
    weights = weights[None]
    for turn in (8, 4, 2, 1):
        weights = jnp.concatenate([weights, swap(weights, turn)], 0)
    rim = shape(2, 8, CELLS)
    power, *rims = pl.pallas_call(
        power_kernel,
        out_shape=(shape(GROUPS, 8, CELLS), rim, rim),
        in_specs=[VMEM] * 4,
        out_specs=(VMEM,) * 3,
        compiler_params=limit(12),
        name="power",
    )(centres, weights, snaps, edges)
    rims = [
        lax.ppermute(value, "az", pairs)
        for value, pairs in zip(rims, neighbours(8, True))
    ]
    smoothed = pl.pallas_call(
        smooth_kernel,
        out_shape=shape(GROUPS, 8, CELLS),
        in_specs=[VMEM] * 3,
        out_specs=VMEM,
        compiler_params=limit(8),
        name="smooth",
    )(power, *rims)
    return smoothed.reshape(OWN_BEAMS, DBINS, CELLS)


def solution(mesh):
    return jax.shard_map(
        body,
        mesh=mesh,
        in_specs=(P(None, "az", None, "rng"), P(), P(), P(), P(), P("az", "rng")),
        out_specs=P("az", None, "rng"),
        check_vma=False,
    )
```

```python
import itertools

import jax
import jax.numpy as jnp
import numpy as np
from jax import lax
from jax.experimental import pallas as pl
from jax.experimental.pallas import tpu as pltpu
from jax.sharding import PartitionSpec as P

COLS = 256
ARC = 64
BINS = 3
BEAMS = 64
BLK = 128
PULSES = 32
SEL = 16
DBINS = 16
DOF = BINS * SEL
OWN_COLS = 32
OWN_BEAMS = 8
CELLS = 128
GROUPS = 16
LANES = 128
SLOTS = PULSES + 8
LOADING = 0.1
F32 = jnp.float32
BF16 = jnp.bfloat16
TRANSPOSED = (((1,), (1,)), ((), ()))


def table_array():
    ids = np.arange(PULSES)
    steps = (ids[:, None] * ids[None, :] % PULSES).astype(np.float32)
    angle = np.float32(-2.0 * np.pi / PULSES) * steps
    real, imag = np.cos(angle), np.sin(angle)
    return np.concatenate(
        [np.concatenate([real, -imag], 1), np.concatenate([imag, real], 1)], 0
    ).astype(jnp.bfloat16)


def lane_ids(rows):
    return lax.broadcasted_iota(jnp.int32, (rows, LANES), 1)


def own_group():
    place = lax.axis_index("rng")
    bits = [lax.rem(lax.div(place, 1 << bit), 2) for bit in range(5)]
    along = exclusive(bits[2], bits[4]) * 2 + exclusive(bits[3], bits[4])
    return bits[0] * 8 + bits[1] * 4 + along


def exclusive(left, right):
    return lax.bitwise_xor(left, right)


def spectra(table, ref, pair, out_ref, base):
    blocks = [
        jnp.concatenate([ref[0, 2 * pair + one], ref[1, 2 * pair + one]], 0)
        for one in range(2)
    ]
    both = jnp.dot(table, jnp.concatenate(blocks, 1), preferred_element_type=F32)
    out_ref[base + 2 * pair] = both[:, :CELLS]
    out_ref[base + 2 * pair + 1] = both[:, CELLS:]


def own_kernel(table_ref, own_ref, spec_ref, passed_ref):
    table = table_ref[...]
    passed_ref[...] = table

    def step(index, carry):
        for one in range(4):
            spectra(table, own_ref, 4 * index + one, spec_ref, 0)
        return carry

    lax.fori_loop(0, OWN_COLS // 8, step, 0)


def gram_kernel(
    ints_ref, floats_ref,
    table_ref, low_ref, own_ref, high_ref, marks_ref,
    snap_ref, keep_ref, send_ref, passed_ref,
    spec_ref, wide_ref, even_ref, odd_ref,
):
    mine = own_group()
    table = table_ref[...]
    passed_ref[...] = marks_ref[...]

    for pair in range(OWN_COLS // 2):
        spectra(table, low_ref, pair, spec_ref, 0)
        for column in (2 * pair, 2 * pair + 1):
            spec_ref[OWN_COLS + column] = own_ref[column]
            spec_ref[2 * OWN_COLS + column] = high_ref[column]

    lane = lane_ids(DOF)
    row = lax.broadcasted_iota(jnp.int32, (DOF, LANES), 0)
    lower = row >= lane - jnp.where(lane < DOF, 0, DOF)
    blank = jnp.zeros((LANES - 2 * DOF, 2 * CELLS), BF16)
    last = PULSES * SEL

    def first_group(step):
        return exclusive(exclusive(2 * step, 8), mine)

    def turn(step, work_ref):
        beam = lax.div(first_group(step), 2)
        for sel in range(SEL):
            column = ints_ref[beam, sel]
            real = spec_ref[column, :PULSES]
            imag = spec_ref[column, PULSES:]
            cosine = floats_ref[beam, sel]
            sine = floats_ref[beam, SEL + sel]
            rows = pl.ds(SEL + sel, PULSES, stride=SEL)
            wide_ref[0, rows, :] = cosine * real - sine * imag
            wide_ref[1, rows, :] = sine * real + cosine * imag
            if sel % 4 == 3:
                yield
        for part in range(2):
            for low, high, place in (
                (SEL, SEL + last // 2, SEL),
                (SEL + last // 2, SEL + last, SEL + last // 2),
                (last, last + SEL, 0),
                (SEL, 2 * SEL, SEL + last),
            ):
                value = wide_ref[part, low:high, :].astype(BF16)
                work_ref[part, place : place + high - low, :] = value
                snap_ref[beam, part, place : place + high - low, :] = value
                if place in (SEL, SEL + last // 2):
                    yield
            snap_ref[beam, part, last + 2 * SEL :, :] = jnp.zeros(
                (SLOTS * SEL - last - 2 * SEL, CELLS), BF16
            )

    def multiply(step, work_ref, out_ref):
        group = first_group(step)
        beam = lax.div(group, 2)
        weight = ints_ref[beam, 2 * SEL].astype(F32)
        for half in range(2):
            base = exclusive(lax.rem(group, 2), half) * 8
            out = [None, None, None]
            for pair in range(4):
                same, turned = [], []
                for one in range(2):
                    centre = ints_ref[beam, SEL + base + pair * 2 + one]
                    rows = pl.ds(pl.multiple_of(centre * SEL, SEL), DOF)
                    real = work_ref[0, rows, :]
                    imag = work_ref[1, rows, :]
                    same.append(jnp.concatenate([real, imag], 1))
                    turned.append(jnp.concatenate([imag, -real], 1))
                left = jnp.concatenate([same[0], turned[0], same[1], turned[1]], 0)
                right = jnp.concatenate([same[0], same[1], blank], 0)
                gram = lax.dot_general(
                    left, right, TRANSPOSED, preferred_element_type=F32
                )
                packed = jnp.where(
                    lower,
                    jnp.where(lane < DOF, gram[:DOF], gram[2 * DOF : 3 * DOF]),
                    jnp.where(lane < DOF, gram[DOF : 2 * DOF], gram[3 * DOF :]),
                )
                shift = 2 * DOF * pair % LANES
                if shift:
                    packed = pltpu.roll(packed, shift, 1)
                if pair == 0:
                    out[0] = packed
                elif pair == 1:
                    out[0] = jnp.where(lane >= 96, packed, out[0])
                    out[1] = packed
                elif pair == 2:
                    out[1] = jnp.where(lane >= 64, packed, out[1])
                    out[2] = packed
                else:
                    out[2] = jnp.where(lane >= 32, packed, out[2])
                yield
            place = lax.rem(2 * step, 8) + half
            for part in range(3):
                out_ref[place, :, LANES * part : LANES * (part + 1)] = (
                    out[part] * weight
                )

    def run(*works):
        for _ in itertools.zip_longest(*works):
            pass

    def sending(index, carry):
        run(turn(2 * index + 1, odd_ref), multiply(2 * index, even_ref, send_ref))
        run(turn(2 * index + 2, even_ref), multiply(2 * index + 1, odd_ref, send_ref))
        return carry

    run(turn(0, even_ref))
    lax.fori_loop(0, 2, sending, 0)
    run(turn(5, odd_ref), multiply(4, even_ref, keep_ref))
    run(turn(6, even_ref), multiply(5, odd_ref, keep_ref))
    run(turn(7, odd_ref), multiply(6, even_ref, keep_ref))
    run(multiply(7, odd_ref, keep_ref))


def edge_out_kernel(snap_ref, first_ref, second_ref):
    rows = 8 * 8
    lane = lane_ids(rows)
    ends = [jnp.zeros((rows, LANES), F32) for _ in range(2)]
    for beam in range(OWN_BEAMS):
        for part in range(2):
            for block in range(8):
                low = SEL + rows * block
                value = snap_ref[beam, part, low : low + rows, :].astype(F32)
                target = 16 * block + 8 * part + beam
                here = lane == target
                for end in range(2):
                    shift = (target + end) % LANES
                    moved = pltpu.roll(value, shift, 1) if shift else value
                    ends[end] = jnp.where(here, moved, ends[end])
    even = lax.rem(lax.axis_index("rng"), 2) == 0
    first_ref[...] = jnp.where(even, ends[1], ends[0]).astype(BF16)
    second_ref[...] = jnp.where(even, ends[0], ends[1]).astype(BF16)


def edge_in_kernel(first_ref, second_ref, out_ref):
    rows = 8 * 8
    last = PULSES * SEL
    lane = lane_ids(rows)
    first = first_ref[...].astype(F32)
    second = second_ref[...].astype(F32)

    def rolled(value, shift):
        return pltpu.roll(value, shift % LANES, 1) if shift % LANES else value

    for block in range(8):
        both = jnp.where(
            lane < 16, rolled(first, -16 * block), rolled(second, 16 - 16 * block)
        )
        for part, value in enumerate((both, rolled(both, -8))):
            value = value.astype(BF16)
            out_ref[part, SEL + rows * block : SEL + rows * (block + 1), :] = value
            if block == 0:
                out_ref[part, last + SEL : last + 2 * SEL, :] = value[:SEL]
            if block == 7:
                out_ref[part, :SEL, :] = value[rows - SEL :]
    for part in range(2):
        out_ref[part, last + 2 * SEL :, :] = jnp.zeros(
            (SLOTS * SEL - last - 2 * SEL, CELLS), BF16
        )


def spread(value, index):
    return jnp.take_along_axis(
        value, jnp.full(value.shape, index, jnp.int32), axis=1
    )


def solve_kernel(first_ref, second_ref, marks_ref, out_ref, turn_ref):
    lane = lane_ids(DOF)
    row = lax.broadcasted_iota(jnp.int32, (DOF, LANES), 0)
    slot = lax.div(lane, SEL)
    lower = row >= lane
    same = row == lane
    total = first_ref[...] + second_ref[...]
    parts = [total[:, LANES * i : LANES * (i + 1)] for i in range(3)]
    block_a = [None] * BINS
    block_b = [None] * BINS
    for pair in range(4):
        if pair == 0:
            packed = parts[0]
        elif pair == 1:
            packed = jnp.where(
                lane < 32, pltpu.roll(parts[0], 32, 1), pltpu.roll(parts[1], 32, 1)
            )
        elif pair == 2:
            packed = jnp.where(
                lane < 64, pltpu.roll(parts[1], 64, 1), pltpu.roll(parts[2], 64, 1)
            )
        else:
            packed = pltpu.roll(parts[2], 96, 1)
        square = jnp.concatenate([packed, jnp.zeros((LANES - DOF, LANES), F32)], 0)
        turned = jnp.transpose(square)
        for one in range(2):
            item = pair * 2 + one
            here = packed if one == 0 else pltpu.roll(packed, LANES - DOF, 1)
            there = turned[one * DOF : (one + 1) * DOF]
            value_a = jnp.where(lower, here, there)
            value_b = jnp.where(lower, jnp.where(same, 0.0, -there), here)
            if item:
                value_a = pltpu.roll(value_a, SEL * item, 1)
                value_b = pltpu.roll(value_b, SEL * item, 1)
            for part in range(BINS):
                if item == 0:
                    block_a[part] = value_a
                    block_b[part] = value_b
                else:
                    chosen = slot == (item + part) % 8
                    block_a[part] = jnp.where(chosen, value_a, block_a[part])
                    block_b[part] = jnp.where(chosen, value_b, block_b[part])
    for part in range(1, BINS):
        block_a[part] = pltpu.roll(block_a[part], LANES - SEL * part, 1)
        block_b[part] = pltpu.roll(block_b[part], LANES - SEL * part, 1)
    small = lane_ids(8)
    line = lax.broadcasted_iota(jnp.int32, (8, LANES), 0)
    place = lax.rem(small, SEL)
    base = small - place
    diagonal = jnp.zeros((8, LANES), F32)
    masks = []
    for group in range(DOF // 8):
        masks.append(place == line + group % 2 * 8)
        diagonal = diagonal + jnp.where(
            masks[group], block_a[group // 2][8 * group : 8 * group + 8], 0.0
        )
    level = jnp.sum(diagonal, axis=0, keepdims=True)
    level = jnp.broadcast_to(level, (8, LANES))
    for step in (1, 2, 4, 8):
        partner = base + lax.rem(place + step, SEL)
        level = level + jnp.take_along_axis(level, partner, axis=1)
    level = LOADING / DOF * level
    real = [[None] * 4 for _ in range(6)]
    imag = [[None] * 4 for _ in range(6)]
    for group in range(6):
        for part in range(BINS):
            real[group][part] = block_a[part][8 * group : 8 * group + 8]
            imag[group][part] = block_b[part][8 * group : 8 * group + 8]
        real[group][group // 2] = jnp.where(
            masks[group], real[group][group // 2] + level, real[group][group // 2]
        )
        real[group][3] = jnp.ones((8, LANES), F32)
        imag[group][3] = jnp.zeros((8, LANES), F32)
    inverse = [jnp.ones((8, LANES), F32)] * 6
    for k in range(0, DOF, 2):
        group, inner, part = k // 8, k % 8, k // SEL
        columns = []
        for step in range(2):
            index = base + k % SEL + step
            columns.append(
                [
                    [
                        jnp.take_along_axis(half[i][part], index, axis=1)
                        for i in range(6)
                    ]
                    for half in (real, imag)
                ]
            )
        (zero_re, zero_im), (one_re, one_im) = columns

        def line_of(value, offset):
            return jnp.broadcast_to(
                value[inner + offset : inner + offset + 1], (8, LANES)
            )

        side_re, side_im = line_of(one_re[group], 0), line_of(one_im[group], 0)
        below_re, below_im = line_of(zero_re[group], 1), line_of(zero_im[group], 1)
        first = 1.0 / line_of(zero_re[group], 0)
        below_re, below_im = below_re * first, below_im * first
        second = 1.0 / (
            line_of(one_re[group], 1) - below_re * side_re + below_im * side_im
        )
        upper, under = line == inner, line == inner + 1
        inverse[group] = jnp.where(
            upper, first, jnp.where(under, second, inverse[group])
        )
        zero_re[group] = jnp.where(upper, 0.0, zero_re[group])
        zero_im[group] = jnp.where(upper, 0.0, zero_im[group])
        alpha_re = [value * first for value in zero_re]
        alpha_im = [value * first for value in zero_im]
        beta_re = [
            (one_re[i] - alpha_re[i] * side_re + alpha_im[i] * side_im) * second
            for i in range(6)
        ]
        beta_im = [
            (one_im[i] - alpha_re[i] * side_im - alpha_im[i] * side_re) * second
            for i in range(6)
        ]
        beta_re[group] = jnp.where(under, 0.0, beta_re[group])
        beta_im[group] = jnp.where(under, 0.0, beta_im[group])
        for block in (*range(part, BINS), 3):
            row_re = line_of(real[group][block], 0)
            row_im = line_of(imag[group][block], 0)
            next_re = (
                line_of(real[group][block], 1) - below_re * row_re + below_im * row_im
            )
            next_im = (
                line_of(imag[group][block], 1) - below_re * row_im - below_im * row_re
            )
            for i in range(6):
                real[i][block] = (
                    real[i][block]
                    - alpha_re[i] * row_re
                    + alpha_im[i] * row_im
                    - beta_re[i] * next_re
                    + beta_im[i] * next_im
                )
                imag[i][block] = (
                    imag[i][block]
                    - alpha_re[i] * row_im
                    - alpha_im[i] * row_re
                    - beta_re[i] * next_im
                    - beta_im[i] * next_re
                )
    gap = jnp.zeros((SEL, LANES), F32)
    found_re = [real[i][3] * inverse[i] for i in range(6)]
    found_im = [imag[i][3] * inverse[i] for i in range(6)]
    quiet = found_re[0]
    for i in range(1, 6):
        quiet = quiet + found_re[i]
    quiet = jnp.broadcast_to(jnp.sum(quiet, axis=0, keepdims=True), (SEL, LANES))
    turn_ref[...] = jnp.transpose(
        jnp.concatenate([*found_re, quiet, *found_im, gap], 0)
    )
    found = turn_ref[pl.ds(0, 8, stride=SEL), :]
    out_ref[...] = jnp.where(small == 120, marks_ref[...], found)


def power_kernel(
    bins_ref, weights_ref, snap_ref, edge_ref,
    power_ref, first_ref, second_ref,
):
    mine = own_group()
    even = lax.rem(lax.axis_index("rng"), 2) == 0
    small = lane_ids(8)
    counts = jnp.zeros((8, LANES), F32)
    for place in range(GROUPS):
        counts = counts + weights_ref[place]
    counts = spread(counts, 120) * BLK
    low_lane = jnp.where(even, 16, 0)
    rows = SLOTS * SEL
    edge = edge_ref[...].reshape(2 * rows, LANES)
    for beam in range(OWN_BEAMS):
        lefts, quiets = [], []
        for group in (2 * beam, 2 * beam + 1):
            scaled = weights_ref[exclusive(mine, group)] * counts[beam : beam + 1, :]
            quiets.append(spread(scaled, 56))
            away = small - bins_ref[group] * SEL
            left = [[], []]
            for tile in range(rows // LANES):
                index = away + LANES * tile
                inside = jnp.logical_and(index >= 0, index < DOF)
                direct = jnp.take_along_axis(
                    scaled, lax.bitwise_and(index, LANES - 1), axis=1
                )
                crossed = jnp.take_along_axis(
                    scaled, lax.bitwise_and(index + 64, LANES - 1), axis=1
                )
                direct = jnp.where(inside, direct, 0.0)
                crossed = jnp.where(inside, crossed, 0.0)
                left[0].append(jnp.concatenate([direct, -crossed], 0).astype(BF16))
                left[1].append(jnp.concatenate([crossed, direct], 0).astype(BF16))
            lefts.append(jnp.concatenate(left[0] + left[1], 1))
        right = jnp.concatenate([snap_ref[beam].reshape(2 * rows, LANES), edge], 1)
        found = jnp.dot(
            jnp.concatenate(lefts, 0), right, preferred_element_type=F32
        )
        found = found * found
        for half in range(2):
            power = found[16 * half : 16 * half + 8] + found[16 * half + 8 : 16 * half + 16]
            inner = power[:, :LANES] / quiets[half]
            outer = power[:, LANES:] / quiets[half]
            low = spread(outer, beam + low_lane)
            high = spread(outer, beam + 16 - low_lane)
            below = jnp.where(small == 0, low, pltpu.roll(inner, 1, 1))
            above = jnp.where(
                small == LANES - 1, high, pltpu.roll(inner, LANES - 1, 1)
            )
            power_ref[2 * beam + half] = below + inner + above
    even = lax.rem(lax.axis_index("az"), 2) == 0
    for half in range(2):
        bottom, top = power_ref[half], power_ref[GROUPS - 2 + half]
        first_ref[half] = jnp.where(even, top, bottom)
        second_ref[half] = jnp.where(even, bottom, top)


def smooth_kernel(power_ref, first_ref, second_ref, out_ref):
    even = lax.rem(lax.axis_index("az"), 2) == 0
    first, second = first_ref[...], second_ref[...]
    low = jnp.where(even, second, first)
    high = jnp.where(even, first, second)
    for beam in range(OWN_BEAMS):
        below = low if beam == 0 else power_ref[2 * beam - 2 : 2 * beam]
        above = (
            high if beam == OWN_BEAMS - 1 else power_ref[2 * beam + 2 : 2 * beam + 4]
        )
        here = power_ref[2 * beam : 2 * beam + 2]
        out_ref[2 * beam : 2 * beam + 2] = (below + here + above) / 9.0


def swap(value, turn):
    return lax.ppermute(value, "rng", [(i, i ^ turn) for i in range(32)])


def halo_columns(echoes):
    ring = [(i, (i + 1) % 8) for i in range(8)]
    low = lax.ppermute(echoes, "az", ring)
    high = lax.ppermute(echoes, "az", [(b, a) for a, b in ring])
    return low, high


SMEM = pl.BlockSpec(memory_space=pltpu.SMEM)
VMEM = pl.BlockSpec(memory_space=pltpu.VMEM)


def limit(mebibytes):
    return pltpu.CompilerParams(vmem_limit_bytes=mebibytes * 2**20)


def shape(*dims, dtype=F32):
    return jax.ShapeDtypeStruct(dims, dtype)


def neighbours(count, closed):
    nearest = [(i, i ^ 1) for i in range(count)]
    across = [(i, i + 1) if i % 2 else (i, i - 1) for i in range(count)]
    if closed:
        across = [(a, b % count) for a, b in across]
    else:
        across = [(a, b) for a, b in across if 0 <= b < count]
    return nearest, across


def body(echoes, arc_start, arc_offsets, doppler_bins, steer_angles, train_mask):
    low, high = halo_columns(echoes)
    az = lax.axis_index("az")

    def own(value):
        return lax.dynamic_slice_in_dim(value, az * OWN_BEAMS, OWN_BEAMS, 0)

    marks = jnp.broadcast_to(train_mask.astype(F32), (OWN_BEAMS, LANES))
    marks = marks + swap(marks, 28)
    first = (own(arc_start) - az * OWN_COLS + ARC // 2) % COLS
    ints = jnp.concatenate(
        [first[:, None] + own(arc_offsets), own(doppler_bins), train_mask], 1
    )
    angles = own(steer_angles)
    floats = jnp.concatenate([jnp.cos(angles), jnp.sin(angles)], 1)
    centres = jnp.broadcast_to(
        own(doppler_bins).reshape(GROUPS, 8, 1), (GROUPS, 8, LANES)
    )
    transform = pl.pallas_call(
        own_kernel,
        out_shape=(
            shape(OWN_COLS, 2 * PULSES, CELLS),
            shape(2 * PULSES, 2 * PULSES, dtype=BF16),
        ),
        in_specs=[VMEM, VMEM],
        out_specs=(VMEM, VMEM),
        compiler_params=limit(8),
        name="spectra",
    )
    spec, table = transform(jnp.asarray(table_array()), echoes)
    high, table = transform(table, high)
    half = shape(8, DOF, 8 * DOF)
    snaps, keep, send, marks = pl.pallas_call(
        gram_kernel,
        out_shape=(
            shape(OWN_BEAMS, 2, SLOTS * SEL, CELLS, dtype=BF16),
            half,
            half,
            shape(OWN_BEAMS, LANES),
        ),
        in_specs=[SMEM] * 2 + [VMEM] * 5,
        out_specs=(VMEM,) * 4,
        scratch_shapes=[
            pltpu.VMEM((3 * OWN_COLS, 2 * PULSES, CELLS), F32),
            pltpu.VMEM((2, (PULSES + 1) * SEL, CELLS), F32),
            pltpu.VMEM((2, (PULSES + 2) * SEL, CELLS), BF16),
            pltpu.VMEM((2, (PULSES + 2) * SEL, CELLS), BF16),
        ],
        compiler_params=limit(16),
        name="grams",
    )(ints, floats, table, low, spec, high, marks)
    edge = shape(64, LANES, dtype=BF16)
    edges = pl.pallas_call(
        edge_out_kernel,
        out_shape=(edge, edge),
        in_specs=[VMEM],
        out_specs=(VMEM, VMEM),
        compiler_params=limit(8),
        name="edges_out",
    )(snaps)
    moved, edges = lax.optimization_barrier((swap(send, 1), edges))
    part = keep + moved
    moved = [swap(part[2:4], 4), swap(part[4:6], 2), swap(part[6:], 6)]
    edges = [
        lax.ppermute(value, "rng", pairs)
        for value, pairs in zip(edges, neighbours(32, False))
    ]
    moved, edges[0] = lax.optimization_barrier((moved, edges[0]))
    part = part[:2] + moved[0] + moved[1] + moved[2]
    part = part[0] + swap(part[1], 8)
    other = swap(part, 28)
    other, edges = lax.optimization_barrier((other, edges))
    edges = pl.pallas_call(
        edge_in_kernel,
        out_shape=shape(2, SLOTS * SEL, LANES, dtype=BF16),
        in_specs=[VMEM, VMEM],
        out_specs=VMEM,
        compiler_params=limit(8),
        name="edges_in",
    )(*edges)
    weights = pl.pallas_call(
        solve_kernel,
        out_shape=shape(8, LANES),
        in_specs=[VMEM] * 3,
        out_specs=VMEM,
        scratch_shapes=[pltpu.VMEM((LANES, LANES), F32)],
        compiler_params=limit(8),
        name="solve",
    )(part, other, marks)
    weights = weights[None]
    for turn in (8, 4, 2, 1):
        weights = jnp.concatenate([weights, swap(weights, turn)], 0)
    rim = shape(2, 8, CELLS)
    power, *rims = pl.pallas_call(
        power_kernel,
        out_shape=(shape(GROUPS, 8, CELLS), rim, rim),
        in_specs=[VMEM] * 4,
        out_specs=(VMEM,) * 3,
        compiler_params=limit(12),
        name="power",
    )(centres, weights, snaps, edges)
    rims = [
        lax.ppermute(value, "az", pairs)
        for value, pairs in zip(rims, neighbours(8, True))
    ]
    smoothed = pl.pallas_call(
        smooth_kernel,
        out_shape=shape(GROUPS, 8, CELLS),
        in_specs=[VMEM] * 3,
        out_specs=VMEM,
        compiler_params=limit(8),
        name="smooth",
    )(power, *rims)
    return smoothed.reshape(OWN_BEAMS, DBINS, CELLS)


def solution(mesh):
    return jax.shard_map(
        body,
        mesh=mesh,
        in_specs=(P(None, "az", None, "rng"), P(), P(), P(), P(), P("az", "rng")),
        out_specs=P("az", None, "rng"),
        check_vma=False,
    )
```

```python
import itertools

import jax
import jax.numpy as jnp
import numpy as np
from jax import lax
from jax.experimental import pallas as pl
from jax.experimental.pallas import tpu as pltpu
from jax.sharding import PartitionSpec as P

COLS = 256
ARC = 64
BINS = 3
BEAMS = 64
BLK = 128
PULSES = 32
SEL = 16
DBINS = 16
DOF = BINS * SEL
OWN_COLS = 32
OWN_BEAMS = 8
CELLS = 128
GROUPS = 16
LANES = 128
SLOTS = PULSES + 8
LOADING = 0.1
F32 = jnp.float32
BF16 = jnp.bfloat16
TRANSPOSED = (((1,), (1,)), ((), ()))


def table_array():
    ids = np.arange(PULSES)
    steps = (ids[:, None] * ids[None, :] % PULSES).astype(np.float32)
    angle = np.float32(-2.0 * np.pi / PULSES) * steps
    real, imag = np.cos(angle), np.sin(angle)
    return np.concatenate(
        [np.concatenate([real, -imag], 1), np.concatenate([imag, real], 1)], 0
    ).astype(jnp.bfloat16)


def lane_ids(rows):
    return lax.broadcasted_iota(jnp.int32, (rows, LANES), 1)


def own_group():
    place = lax.axis_index("rng")
    bits = [lax.rem(lax.div(place, 1 << bit), 2) for bit in range(5)]
    along = exclusive(bits[2], bits[4]) * 2 + exclusive(bits[3], bits[4])
    return bits[0] * 8 + bits[1] * 4 + along


def exclusive(left, right):
    return lax.bitwise_xor(left, right)


def spectra(table, ref, pair, out_ref, base):
    blocks = [
        jnp.concatenate([ref[0, 2 * pair + one], ref[1, 2 * pair + one]], 0)
        for one in range(2)
    ]
    both = jnp.dot(table, jnp.concatenate(blocks, 1), preferred_element_type=F32)
    out_ref[base + 2 * pair] = both[:, :CELLS]
    out_ref[base + 2 * pair + 1] = both[:, CELLS:]


def own_kernel(table_ref, own_ref, spec_ref, passed_ref):
    table = table_ref[...]
    passed_ref[...] = table

    def step(index, carry):
        for one in range(4):
            spectra(table, own_ref, 4 * index + one, spec_ref, 0)
        return carry

    lax.fori_loop(0, OWN_COLS // 8, step, 0)


def gram_kernel(
    ints_ref, floats_ref,
    table_ref, low_ref, own_ref, high_ref, marks_ref,
    snap_ref, keep_ref, send_ref, passed_ref,
    spec_ref, wide_ref, even_ref, odd_ref,
):
    mine = own_group()
    table = table_ref[...]
    passed_ref[...] = marks_ref[...]

    for pair in range(OWN_COLS // 2):
        spectra(table, low_ref, pair, spec_ref, 0)
        for column in (2 * pair, 2 * pair + 1):
            spec_ref[OWN_COLS + column] = own_ref[column]
            spec_ref[2 * OWN_COLS + column] = high_ref[column]

    lane = lane_ids(DOF)
    row = lax.broadcasted_iota(jnp.int32, (DOF, LANES), 0)
    lower = row >= lane - jnp.where(lane < DOF, 0, DOF)
    blank = jnp.zeros((LANES - 2 * DOF, 2 * CELLS), BF16)
    last = PULSES * SEL

    def first_group(step):
        return exclusive(exclusive(2 * step, 8), mine)

    def turn(step, work_ref):
        beam = lax.div(first_group(step), 2)
        for sel in range(SEL):
            column = ints_ref[beam, sel]
            real = spec_ref[column, :PULSES]
            imag = spec_ref[column, PULSES:]
            cosine = floats_ref[beam, sel]
            sine = floats_ref[beam, SEL + sel]
            rows = pl.ds(SEL + sel, PULSES, stride=SEL)
            wide_ref[0, rows, :] = cosine * real - sine * imag
            wide_ref[1, rows, :] = sine * real + cosine * imag
            if sel % 4 == 3:
                yield
        for part in range(2):
            for low, high, place in (
                (SEL, SEL + last // 2, SEL),
                (SEL + last // 2, SEL + last, SEL + last // 2),
                (last, last + SEL, 0),
                (SEL, 2 * SEL, SEL + last),
            ):
                value = wide_ref[part, low:high, :].astype(BF16)
                work_ref[part, place : place + high - low, :] = value
                snap_ref[beam, part, place : place + high - low, :] = value
                if place in (SEL, SEL + last // 2):
                    yield
            snap_ref[beam, part, last + 2 * SEL :, :] = jnp.zeros(
                (SLOTS * SEL - last - 2 * SEL, CELLS), BF16
            )

    def multiply(step, work_ref, out_ref):
        group = first_group(step)
        beam = lax.div(group, 2)
        weight = ints_ref[beam, 2 * SEL].astype(F32)
        for half in range(2):
            base = exclusive(lax.rem(group, 2), half) * 8
            out = [None, None, None]
            for pair in range(4):
                same, turned = [], []
                for one in range(2):
                    centre = ints_ref[beam, SEL + base + pair * 2 + one]
                    rows = pl.ds(pl.multiple_of(centre * SEL, SEL), DOF)
                    real = work_ref[0, rows, :]
                    imag = work_ref[1, rows, :]
                    same.append(jnp.concatenate([real, imag], 1))
                    turned.append(jnp.concatenate([imag, -real], 1))
                left = jnp.concatenate([same[0], turned[0], same[1], turned[1]], 0)
                right = jnp.concatenate([same[0], same[1], blank], 0)
                gram = lax.dot_general(
                    left, right, TRANSPOSED, preferred_element_type=F32
                )
                packed = jnp.where(
                    lower,
                    jnp.where(lane < DOF, gram[:DOF], gram[2 * DOF : 3 * DOF]),
                    jnp.where(lane < DOF, gram[DOF : 2 * DOF], gram[3 * DOF :]),
                )
                shift = 2 * DOF * pair % LANES
                if shift:
                    packed = pltpu.roll(packed, shift, 1)
                if pair == 0:
                    out[0] = packed
                elif pair == 1:
                    out[0] = jnp.where(lane >= 96, packed, out[0])
                    out[1] = packed
                elif pair == 2:
                    out[1] = jnp.where(lane >= 64, packed, out[1])
                    out[2] = packed
                else:
                    out[2] = jnp.where(lane >= 32, packed, out[2])
                yield
            place = lax.rem(2 * step, 8) + half
            for part in range(3):
                out_ref[place, :, LANES * part : LANES * (part + 1)] = (
                    out[part] * weight
                )

    def run(*works):
        for _ in itertools.zip_longest(*works):
            pass

    def sending(index, carry):
        run(turn(2 * index + 1, odd_ref), multiply(2 * index, even_ref, send_ref))
        run(turn(2 * index + 2, even_ref), multiply(2 * index + 1, odd_ref, send_ref))
        return carry

    run(turn(0, even_ref))
    lax.fori_loop(0, 2, sending, 0)
    run(turn(5, odd_ref), multiply(4, even_ref, keep_ref))
    run(turn(6, even_ref), multiply(5, odd_ref, keep_ref))
    run(turn(7, odd_ref), multiply(6, even_ref, keep_ref))
    run(multiply(7, odd_ref, keep_ref))


def edge_kernel(
    table_ref, low_ref, own_ref, high_ref, ints_ref, floats_ref,
    out_ref, wide_ref,
):
    last = PULSES * SEL
    blank = jnp.zeros((LANES - 3 * OWN_COLS, PULSES), BF16)
    small = lane_ids(8)
    sides = []
    for side in range(2):
        total = None
        for part in range(2):
            columns = jnp.concatenate(
                [low_ref[side, part], own_ref[side, part], high_ref[side, part], blank],
                0,
            )
            product = lax.dot_general(
                table_ref[:, PULSES * part : PULSES * (part + 1)],
                columns,
                TRANSPOSED,
                preferred_element_type=F32,
            )
            total = product if total is None else total + product
        sides.append(total)
    first_part = lax.rem(small, 16) < 8
    turned = jnp.transpose(
        jnp.concatenate(
            [
                ints_ref[...].astype(F32),
                floats_ref[...],
                jnp.zeros((LANES - 16, LANES), F32),
            ],
            0,
        )
    )
    nearest = lax.rem(small, 8)

    def row_of(index, start):
        value = jnp.broadcast_to(turned[index : index + 1, :], (8, LANES))
        return jnp.take_along_axis(value, nearest + start, axis=1)

    for sel in range(SEL):
        index = row_of(sel, 0).astype(jnp.int32)
        cosine = row_of(sel, 8)
        sine = row_of(SEL + sel, 8)

        def chosen(row):
            picked = [
                jnp.take_along_axis(value[row : row + 8], index, axis=1)
                for value in sides
            ]
            return jnp.where(small < 16, picked[0], picked[1])

        values = []
        for row in range(0, PULSES, 8):
            real, imag = chosen(row), chosen(PULSES + row)
            values.append(
                jnp.where(
                    first_part,
                    cosine * real - sine * imag,
                    sine * real + cosine * imag,
                )
            )
        wide_ref[pl.ds(sel, PULSES, stride=SEL), :] = jnp.concatenate(values, 0)
    value = wide_ref[...]
    for part in range(2):
        if part == 1:
            value = pltpu.roll(value, LANES - 8, 1)
        short = value.astype(BF16)
        out_ref[part, SEL : SEL + last, :] = short
        out_ref[part, :SEL, :] = short[last - SEL :]
        out_ref[part, SEL + last : 2 * SEL + last, :] = short[:SEL]
        out_ref[part, last + 2 * SEL :, :] = jnp.zeros(
            (SLOTS * SEL - last - 2 * SEL, LANES), BF16
        )


def spread(value, index):
    return jnp.take_along_axis(
        value, jnp.full(value.shape, index, jnp.int32), axis=1
    )


def solve_kernel(first_ref, second_ref, marks_ref, out_ref, turn_ref):
    lane = lane_ids(DOF)
    row = lax.broadcasted_iota(jnp.int32, (DOF, LANES), 0)
    slot = lax.div(lane, SEL)
    lower = row >= lane
    same = row == lane
    total = first_ref[...] + second_ref[...]
    parts = [total[:, LANES * i : LANES * (i + 1)] for i in range(3)]
    block_a = [None] * BINS
    block_b = [None] * BINS
    for pair in range(4):
        if pair == 0:
            packed = parts[0]
        elif pair == 1:
            packed = jnp.where(
                lane < 32, pltpu.roll(parts[0], 32, 1), pltpu.roll(parts[1], 32, 1)
            )
        elif pair == 2:
            packed = jnp.where(
                lane < 64, pltpu.roll(parts[1], 64, 1), pltpu.roll(parts[2], 64, 1)
            )
        else:
            packed = pltpu.roll(parts[2], 96, 1)
        square = jnp.concatenate([packed, jnp.zeros((LANES - DOF, LANES), F32)], 0)
        turned = jnp.transpose(square)
        for one in range(2):
            item = pair * 2 + one
            here = packed if one == 0 else pltpu.roll(packed, LANES - DOF, 1)
            there = turned[one * DOF : (one + 1) * DOF]
            value_a = jnp.where(lower, here, there)
            value_b = jnp.where(lower, jnp.where(same, 0.0, -there), here)
            if item:
                value_a = pltpu.roll(value_a, SEL * item, 1)
                value_b = pltpu.roll(value_b, SEL * item, 1)
            for part in range(BINS):
                if item == 0:
                    block_a[part] = value_a
                    block_b[part] = value_b
                else:
                    chosen = slot == (item + part) % 8
                    block_a[part] = jnp.where(chosen, value_a, block_a[part])
                    block_b[part] = jnp.where(chosen, value_b, block_b[part])
    for part in range(1, BINS):
        block_a[part] = pltpu.roll(block_a[part], LANES - SEL * part, 1)
        block_b[part] = pltpu.roll(block_b[part], LANES - SEL * part, 1)
    small = lane_ids(8)
    line = lax.broadcasted_iota(jnp.int32, (8, LANES), 0)
    place = lax.rem(small, SEL)
    base = small - place
    diagonal = jnp.zeros((8, LANES), F32)
    masks = []
    for group in range(DOF // 8):
        masks.append(place == line + group % 2 * 8)
        diagonal = diagonal + jnp.where(
            masks[group], block_a[group // 2][8 * group : 8 * group + 8], 0.0
        )
    level = jnp.sum(diagonal, axis=0, keepdims=True)
    level = jnp.broadcast_to(level, (8, LANES))
    for step in (1, 2, 4, 8):
        partner = base + lax.rem(place + step, SEL)
        level = level + jnp.take_along_axis(level, partner, axis=1)
    level = LOADING / DOF * level
    real = [[None] * 4 for _ in range(6)]
    imag = [[None] * 4 for _ in range(6)]
    for group in range(6):
        for part in range(BINS):
            real[group][part] = block_a[part][8 * group : 8 * group + 8]
            imag[group][part] = block_b[part][8 * group : 8 * group + 8]
        real[group][group // 2] = jnp.where(
            masks[group], real[group][group // 2] + level, real[group][group // 2]
        )
        real[group][3] = jnp.ones((8, LANES), F32)
        imag[group][3] = jnp.zeros((8, LANES), F32)
    inverse = [jnp.ones((8, LANES), F32)] * 6
    for k in range(0, DOF, 2):
        group, inner, part = k // 8, k % 8, k // SEL
        columns = []
        for step in range(2):
            index = base + k % SEL + step
            columns.append(
                [
                    [
                        jnp.take_along_axis(half[i][part], index, axis=1)
                        for i in range(6)
                    ]
                    for half in (real, imag)
                ]
            )
        (zero_re, zero_im), (one_re, one_im) = columns

        def line_of(value, offset):
            return jnp.broadcast_to(
                value[inner + offset : inner + offset + 1], (8, LANES)
            )

        side_re, side_im = line_of(one_re[group], 0), line_of(one_im[group], 0)
        below_re, below_im = line_of(zero_re[group], 1), line_of(zero_im[group], 1)
        first = 1.0 / line_of(zero_re[group], 0)
        below_re, below_im = below_re * first, below_im * first
        second = 1.0 / (
            line_of(one_re[group], 1) - below_re * side_re + below_im * side_im
        )
        upper, under = line == inner, line == inner + 1
        inverse[group] = jnp.where(
            upper, first, jnp.where(under, second, inverse[group])
        )
        zero_re[group] = jnp.where(upper, 0.0, zero_re[group])
        zero_im[group] = jnp.where(upper, 0.0, zero_im[group])
        alpha_re = [value * first for value in zero_re]
        alpha_im = [value * first for value in zero_im]
        beta_re = [
            (one_re[i] - alpha_re[i] * side_re + alpha_im[i] * side_im) * second
            for i in range(6)
        ]
        beta_im = [
            (one_im[i] - alpha_re[i] * side_im - alpha_im[i] * side_re) * second
            for i in range(6)
        ]
        beta_re[group] = jnp.where(under, 0.0, beta_re[group])
        beta_im[group] = jnp.where(under, 0.0, beta_im[group])
        for block in (*range(part, BINS), 3):
            row_re = line_of(real[group][block], 0)
            row_im = line_of(imag[group][block], 0)
            next_re = (
                line_of(real[group][block], 1) - below_re * row_re + below_im * row_im
            )
            next_im = (
                line_of(imag[group][block], 1) - below_re * row_im - below_im * row_re
            )
            for i in range(6):
                real[i][block] = (
                    real[i][block]
                    - alpha_re[i] * row_re
                    + alpha_im[i] * row_im
                    - beta_re[i] * next_re
                    + beta_im[i] * next_im
                )
                imag[i][block] = (
                    imag[i][block]
                    - alpha_re[i] * row_im
                    - alpha_im[i] * row_re
                    - beta_re[i] * next_im
                    - beta_im[i] * next_re
                )
    gap = jnp.zeros((SEL, LANES), F32)
    found_re = [real[i][3] * inverse[i] for i in range(6)]
    found_im = [imag[i][3] * inverse[i] for i in range(6)]
    quiet = found_re[0]
    for i in range(1, 6):
        quiet = quiet + found_re[i]
    quiet = jnp.broadcast_to(jnp.sum(quiet, axis=0, keepdims=True), (SEL, LANES))
    turn_ref[...] = jnp.transpose(
        jnp.concatenate([*found_re, quiet, *found_im, gap], 0)
    )
    found = turn_ref[pl.ds(0, 8, stride=SEL), :]
    out_ref[...] = jnp.where(small == 120, marks_ref[...], found)


def power_kernel(
    bins_ref, weights_ref, snap_ref, edge_ref,
    power_ref, first_ref, second_ref,
):
    mine = own_group()
    small = lane_ids(8)
    counts = jnp.zeros((8, LANES), F32)
    for place in range(GROUPS):
        counts = counts + weights_ref[place]
    counts = spread(counts, 120) * BLK
    rows = SLOTS * SEL
    edge = edge_ref[...].reshape(2 * rows, LANES)
    for beam in range(OWN_BEAMS):
        lefts, quiets = [], []
        for group in (2 * beam, 2 * beam + 1):
            scaled = weights_ref[exclusive(mine, group)] * counts[beam : beam + 1, :]
            quiets.append(spread(scaled, 56))
            away = small - bins_ref[group] * SEL
            left = [[], []]
            for tile in range(rows // LANES):
                index = away + LANES * tile
                inside = jnp.logical_and(index >= 0, index < DOF)
                direct = jnp.take_along_axis(
                    scaled, lax.bitwise_and(index, LANES - 1), axis=1
                )
                crossed = jnp.take_along_axis(
                    scaled, lax.bitwise_and(index + 64, LANES - 1), axis=1
                )
                direct = jnp.where(inside, direct, 0.0)
                crossed = jnp.where(inside, crossed, 0.0)
                left[0].append(jnp.concatenate([direct, -crossed], 0).astype(BF16))
                left[1].append(jnp.concatenate([crossed, direct], 0).astype(BF16))
            lefts.append(jnp.concatenate(left[0] + left[1], 1))
        right = jnp.concatenate([snap_ref[beam].reshape(2 * rows, LANES), edge], 1)
        found = jnp.dot(
            jnp.concatenate(lefts, 0), right, preferred_element_type=F32
        )
        found = found * found
        for half in range(2):
            power = found[16 * half : 16 * half + 8] + found[16 * half + 8 : 16 * half + 16]
            inner = power[:, :LANES] / quiets[half]
            outer = power[:, LANES:] / quiets[half]
            low = spread(outer, beam)
            high = spread(outer, 16 + beam)
            below = jnp.where(small == 0, low, pltpu.roll(inner, 1, 1))
            above = jnp.where(
                small == LANES - 1, high, pltpu.roll(inner, LANES - 1, 1)
            )
            power_ref[2 * beam + half] = below + inner + above
    even = lax.rem(lax.axis_index("az"), 2) == 0
    for half in range(2):
        bottom, top = power_ref[half], power_ref[GROUPS - 2 + half]
        first_ref[half] = jnp.where(even, top, bottom)
        second_ref[half] = jnp.where(even, bottom, top)


def smooth_kernel(power_ref, first_ref, second_ref, out_ref):
    even = lax.rem(lax.axis_index("az"), 2) == 0
    first, second = first_ref[...], second_ref[...]
    low = jnp.where(even, second, first)
    high = jnp.where(even, first, second)
    for beam in range(OWN_BEAMS):
        below = low if beam == 0 else power_ref[2 * beam - 2 : 2 * beam]
        above = (
            high if beam == OWN_BEAMS - 1 else power_ref[2 * beam + 2 : 2 * beam + 4]
        )
        here = power_ref[2 * beam : 2 * beam + 2]
        out_ref[2 * beam : 2 * beam + 2] = (below + here + above) / 9.0


def swap(value, turn):
    return lax.ppermute(value, "rng", [(i, i ^ turn) for i in range(32)])


def halo_columns(echoes):
    ring = [(i, (i + 1) % 8) for i in range(8)]
    low = lax.ppermute(echoes, "az", ring)
    high = lax.ppermute(echoes, "az", [(b, a) for a, b in ring])
    return low, high


SMEM = pl.BlockSpec(memory_space=pltpu.SMEM)
VMEM = pl.BlockSpec(memory_space=pltpu.VMEM)


def limit(mebibytes):
    return pltpu.CompilerParams(vmem_limit_bytes=mebibytes * 2**20)


def shape(*dims, dtype=F32):
    return jax.ShapeDtypeStruct(dims, dtype)


def neighbours(count, closed):
    nearest = [(i, i ^ 1) for i in range(count)]
    across = [(i, i + 1) if i % 2 else (i, i - 1) for i in range(count)]
    if closed:
        across = [(a, b % count) for a, b in across]
    else:
        across = [(a, b) for a, b in across if 0 <= b < count]
    return nearest, across


def body(echoes, arc_start, arc_offsets, doppler_bins, steer_angles, train_mask):
    low, high = halo_columns(echoes)
    az = lax.axis_index("az")

    def own(value):
        return lax.dynamic_slice_in_dim(value, az * OWN_BEAMS, OWN_BEAMS, 0)

    ends = [echoes[..., CELLS - 1], echoes[..., 0]]
    ahead = [(i, i + 1) for i in range(31)]
    ends = jnp.stack(
        [
            lax.ppermute(ends[0], "rng", ahead),
            lax.ppermute(ends[1], "rng", [(b, a) for a, b in ahead]),
        ]
    )
    low_ends, high_ends = halo_columns(ends)
    marks = jnp.broadcast_to(train_mask.astype(F32), (OWN_BEAMS, LANES))
    marks = marks + swap(marks, 28)
    first = (own(arc_start) - az * OWN_COLS + ARC // 2) % COLS
    columns = first[:, None] + own(arc_offsets)
    ints = jnp.concatenate([columns, own(doppler_bins), train_mask], 1)
    ints = jnp.pad(ints, ((0, 0), (0, LANES - ints.shape[1])))
    angles = own(steer_angles)
    cosine, sine = jnp.cos(angles), jnp.sin(angles)
    floats = jnp.concatenate([cosine, sine], 1)
    floats = jnp.pad(floats, ((0, 0), (0, LANES - floats.shape[1])))
    centres = jnp.broadcast_to(
        own(doppler_bins).reshape(GROUPS, 8, 1), (GROUPS, 8, LANES)
    )
    transform = pl.pallas_call(
        own_kernel,
        out_shape=(
            shape(OWN_COLS, 2 * PULSES, CELLS),
            shape(2 * PULSES, 2 * PULSES, dtype=BF16),
        ),
        in_specs=[VMEM, VMEM],
        out_specs=(VMEM, VMEM),
        compiler_params=limit(8),
        name="spectra",
    )
    spec, table = transform(jnp.asarray(table_array()), echoes)
    edges = pl.pallas_call(
        edge_kernel,
        out_shape=shape(2, SLOTS * SEL, LANES, dtype=BF16),
        in_specs=[VMEM] * 6,
        out_specs=VMEM,
        scratch_shapes=[pltpu.VMEM((PULSES * SEL, LANES), F32)],
        compiler_params=limit(8),
        name="edges",
    )(table, low_ends, ends, high_ends, ints, floats)
    high, edges, centres = lax.optimization_barrier((high, edges, centres))
    high, table = transform(table, high)
    half = shape(8, DOF, 8 * DOF)
    snaps, keep, send, marks = pl.pallas_call(
        gram_kernel,
        out_shape=(
            shape(OWN_BEAMS, 2, SLOTS * SEL, CELLS, dtype=BF16),
            half,
            half,
            shape(OWN_BEAMS, LANES),
        ),
        in_specs=[SMEM] * 2 + [VMEM] * 5,
        out_specs=(VMEM,) * 4,
        scratch_shapes=[
            pltpu.VMEM((3 * OWN_COLS, 2 * PULSES, CELLS), F32),
            pltpu.VMEM((2, (PULSES + 1) * SEL, CELLS), F32),
            pltpu.VMEM((2, (PULSES + 2) * SEL, CELLS), BF16),
            pltpu.VMEM((2, (PULSES + 2) * SEL, CELLS), BF16),
        ],
        compiler_params=limit(16),
        name="grams",
    )(ints, floats, table, low, spec, high, marks)
    part = keep + swap(send, 1)
    part = part[:2] + swap(part[2:4], 4) + swap(part[4:6], 2) + swap(part[6:], 6)
    part = part[0] + swap(part[1], 8)
    other = swap(part, 28)
    weights = pl.pallas_call(
        solve_kernel,
        out_shape=shape(8, LANES),
        in_specs=[VMEM] * 3,
        out_specs=VMEM,
        scratch_shapes=[pltpu.VMEM((LANES, LANES), F32)],
        compiler_params=limit(8),
        name="solve",
    )(part, other, marks)
    weights = weights[None]
    for turn in (8, 4, 2, 1):
        weights = jnp.concatenate([weights, swap(weights, turn)], 0)
    rim = shape(2, 8, CELLS)
    power, *rims = pl.pallas_call(
        power_kernel,
        out_shape=(shape(GROUPS, 8, CELLS), rim, rim),
        in_specs=[VMEM] * 4,
        out_specs=(VMEM,) * 3,
        compiler_params=limit(12),
        name="power",
    )(centres, weights, snaps, edges)
    rims = [
        lax.ppermute(value, "az", pairs)
        for value, pairs in zip(rims, neighbours(8, True))
    ]
    smoothed = pl.pallas_call(
        smooth_kernel,
        out_shape=shape(GROUPS, 8, CELLS),
        in_specs=[VMEM] * 3,
        out_specs=VMEM,
        compiler_params=limit(8),
        name="smooth",
    )(power, *rims)
    return smoothed.reshape(OWN_BEAMS, DBINS, CELLS)


def solution(mesh):
    return jax.shard_map(
        body,
        mesh=mesh,
        in_specs=(P(None, "az", None, "rng"), P(), P(), P(), P(), P("az", "rng")),
        out_specs=P("az", None, "rng"),
        check_vma=False,
    )
```

```python
import itertools

import jax
import jax.numpy as jnp
import numpy as np
from jax import lax
from jax.experimental import pallas as pl
from jax.experimental.pallas import tpu as pltpu
from jax.sharding import PartitionSpec as P

COLS = 256
ARC = 64
BINS = 3
BEAMS = 64
BLK = 128
PULSES = 32
SEL = 16
DBINS = 16
DOF = BINS * SEL
OWN_COLS = 32
OWN_BEAMS = 8
CELLS = 128
GROUPS = 16
LANES = 128
SLOTS = PULSES + 8
LOADING = 0.1
F32 = jnp.float32
BF16 = jnp.bfloat16
TRANSPOSED = (((1,), (1,)), ((), ()))


def table_array():
    ids = np.arange(PULSES)
    steps = (ids[:, None] * ids[None, :] % PULSES).astype(np.float32)
    angle = np.float32(-2.0 * np.pi / PULSES) * steps
    real, imag = np.cos(angle), np.sin(angle)
    return np.concatenate(
        [np.concatenate([real, -imag], 1), np.concatenate([imag, real], 1)], 0
    ).astype(jnp.bfloat16)


def lane_ids(rows):
    return lax.broadcasted_iota(jnp.int32, (rows, LANES), 1)


def own_group():
    place = lax.axis_index("rng")
    bits = [lax.rem(lax.div(place, 1 << bit), 2) for bit in range(5)]
    along = exclusive(bits[2], bits[4]) * 2 + exclusive(bits[3], bits[4])
    return bits[0] * 8 + bits[1] * 4 + along


def exclusive(left, right):
    return lax.bitwise_xor(left, right)


def spectra(table, ref, pair, out_ref, base):
    blocks = [
        jnp.concatenate([ref[0, 2 * pair + one], ref[1, 2 * pair + one]], 0)
        for one in range(2)
    ]
    both = jnp.dot(table, jnp.concatenate(blocks, 1), preferred_element_type=F32)
    out_ref[base + 2 * pair] = both[:, :CELLS]
    out_ref[base + 2 * pair + 1] = both[:, CELLS:]


def own_kernel(table_ref, own_ref, spec_ref, passed_ref):
    table = table_ref[...]
    passed_ref[...] = table

    def step(index, carry):
        for one in range(4):
            spectra(table, own_ref, 4 * index + one, spec_ref, 0)
        return carry

    lax.fori_loop(0, OWN_COLS // 8, step, 0)


def gram_kernel(
    ints_ref, floats_ref,
    table_ref, low_ref, own_ref, high_ref, marks_ref,
    snap_ref, keep_ref, send_ref, passed_ref,
    spec_ref, wide_ref, even_ref, odd_ref,
):
    mine = own_group()
    table = table_ref[...]
    passed_ref[...] = marks_ref[...]

    for pair in range(OWN_COLS // 2):
        spectra(table, low_ref, pair, spec_ref, 0)
        for column in (2 * pair, 2 * pair + 1):
            spec_ref[OWN_COLS + column] = own_ref[column]
            spec_ref[2 * OWN_COLS + column] = high_ref[column]

    lane = lane_ids(DOF)
    row = lax.broadcasted_iota(jnp.int32, (DOF, LANES), 0)
    lower = row >= lane - jnp.where(lane < DOF, 0, DOF)
    blank = jnp.zeros((LANES - 2 * DOF, 2 * CELLS), BF16)
    last = PULSES * SEL

    def first_group(step):
        return exclusive(exclusive(2 * step, 8), mine)

    def turn(step, work_ref):
        beam = lax.div(first_group(step), 2)
        for sel in range(SEL):
            column = ints_ref[beam, sel]
            real = spec_ref[column, :PULSES]
            imag = spec_ref[column, PULSES:]
            cosine = floats_ref[beam, sel]
            sine = floats_ref[beam, SEL + sel]
            rows = pl.ds(SEL + sel, PULSES, stride=SEL)
            wide_ref[0, rows, :] = cosine * real - sine * imag
            wide_ref[1, rows, :] = sine * real + cosine * imag
            if sel % 4 == 3:
                yield
        for part in range(2):
            for low, high, place in (
                (SEL, SEL + last // 2, SEL),
                (SEL + last // 2, SEL + last, SEL + last // 2),
                (last, last + SEL, 0),
                (SEL, 2 * SEL, SEL + last),
            ):
                value = wide_ref[part, low:high, :].astype(BF16)
                work_ref[part, place : place + high - low, :] = value
                snap_ref[beam, part, place : place + high - low, :] = value
                if place in (SEL, SEL + last // 2):
                    yield
            snap_ref[beam, part, last + 2 * SEL :, :] = jnp.zeros(
                (SLOTS * SEL - last - 2 * SEL, CELLS), BF16
            )

    def multiply(step, work_ref, out_ref):
        group = first_group(step)
        beam = lax.div(group, 2)
        weight = ints_ref[beam, 2 * SEL].astype(F32)
        for half in range(2):
            base = exclusive(lax.rem(group, 2), half) * 8
            out = [None, None, None]
            for pair in range(4):
                same, turned = [], []
                for one in range(2):
                    centre = ints_ref[beam, SEL + base + pair * 2 + one]
                    rows = pl.ds(pl.multiple_of(centre * SEL, SEL), DOF)
                    real = work_ref[0, rows, :]
                    imag = work_ref[1, rows, :]
                    same.append(jnp.concatenate([real, imag], 1))
                    turned.append(jnp.concatenate([imag, -real], 1))
                left = jnp.concatenate([same[0], turned[0], same[1], turned[1]], 0)
                right = jnp.concatenate([same[0], same[1], blank], 0)
                gram = lax.dot_general(
                    left, right, TRANSPOSED, preferred_element_type=F32
                )
                packed = jnp.where(
                    lower,
                    jnp.where(lane < DOF, gram[:DOF], gram[2 * DOF : 3 * DOF]),
                    jnp.where(lane < DOF, gram[DOF : 2 * DOF], gram[3 * DOF :]),
                )
                shift = 2 * DOF * pair % LANES
                if shift:
                    packed = pltpu.roll(packed, shift, 1)
                if pair == 0:
                    out[0] = packed
                elif pair == 1:
                    out[0] = jnp.where(lane >= 96, packed, out[0])
                    out[1] = packed
                elif pair == 2:
                    out[1] = jnp.where(lane >= 64, packed, out[1])
                    out[2] = packed
                else:
                    out[2] = jnp.where(lane >= 32, packed, out[2])
                yield
            place = lax.rem(2 * step, 8) + half
            for part in range(3):
                out_ref[place, :, LANES * part : LANES * (part + 1)] = (
                    out[part] * weight
                )

    def run(*works):
        for _ in itertools.zip_longest(*works):
            pass

    def sending(index, carry):
        run(turn(2 * index + 1, odd_ref), multiply(2 * index, even_ref, send_ref))
        run(turn(2 * index + 2, even_ref), multiply(2 * index + 1, odd_ref, send_ref))
        return carry

    run(turn(0, even_ref))
    lax.fori_loop(0, 2, sending, 0)
    run(turn(5, odd_ref), multiply(4, even_ref, keep_ref))
    run(turn(6, even_ref), multiply(5, odd_ref, keep_ref))
    run(turn(7, odd_ref), multiply(6, even_ref, keep_ref))
    run(multiply(7, odd_ref, keep_ref))


def edge_out_kernel(snap_ref, first_ref, second_ref):
    rows = 8 * 8
    lane = lane_ids(rows)
    ends = [jnp.zeros((rows, LANES), F32) for _ in range(2)]
    for beam in range(OWN_BEAMS):
        for part in range(2):
            for block in range(8):
                low = SEL + rows * block
                value = snap_ref[beam, part, low : low + rows, :].astype(F32)
                target = 16 * block + 8 * part + beam
                here = lane == target
                for end in range(2):
                    shift = (target + end) % LANES
                    moved = pltpu.roll(value, shift, 1) if shift else value
                    ends[end] = jnp.where(here, moved, ends[end])
    even = lax.rem(lax.axis_index("rng"), 2) == 0
    first_ref[...] = jnp.where(even, ends[1], ends[0]).astype(BF16)
    second_ref[...] = jnp.where(even, ends[0], ends[1]).astype(BF16)


def edge_in_kernel(first_ref, second_ref, out_ref):
    rows = 8 * 8
    last = PULSES * SEL
    lane = lane_ids(rows)
    first = first_ref[...].astype(F32)
    second = second_ref[...].astype(F32)

    def rolled(value, shift):
        return pltpu.roll(value, shift % LANES, 1) if shift % LANES else value

    for block in range(8):
        both = jnp.where(
            lane < 16, rolled(first, -16 * block), rolled(second, 16 - 16 * block)
        )
        for part, value in enumerate((both, rolled(both, -8))):
            value = value.astype(BF16)
            out_ref[part, SEL + rows * block : SEL + rows * (block + 1), :] = value
            if block == 0:
                out_ref[part, last + SEL : last + 2 * SEL, :] = value[:SEL]
            if block == 7:
                out_ref[part, :SEL, :] = value[rows - SEL :]
    for part in range(2):
        out_ref[part, last + 2 * SEL :, :] = jnp.zeros(
            (SLOTS * SEL - last - 2 * SEL, CELLS), BF16
        )


def spread(value, index):
    return jnp.take_along_axis(
        value, jnp.full(value.shape, index, jnp.int32), axis=1
    )


def solve_kernel(first_ref, second_ref, marks_ref, out_ref, turn_ref):
    lane = lane_ids(DOF)
    row = lax.broadcasted_iota(jnp.int32, (DOF, LANES), 0)
    slot = lax.div(lane, SEL)
    lower = row >= lane
    same = row == lane
    total = first_ref[...] + second_ref[...]
    parts = [total[:, LANES * i : LANES * (i + 1)] for i in range(3)]
    block_a = [None] * BINS
    block_b = [None] * BINS
    for pair in range(4):
        if pair == 0:
            packed = parts[0]
        elif pair == 1:
            packed = jnp.where(
                lane < 32, pltpu.roll(parts[0], 32, 1), pltpu.roll(parts[1], 32, 1)
            )
        elif pair == 2:
            packed = jnp.where(
                lane < 64, pltpu.roll(parts[1], 64, 1), pltpu.roll(parts[2], 64, 1)
            )
        else:
            packed = pltpu.roll(parts[2], 96, 1)
        square = jnp.concatenate([packed, jnp.zeros((LANES - DOF, LANES), F32)], 0)
        turned = jnp.transpose(square)
        for one in range(2):
            item = pair * 2 + one
            here = packed if one == 0 else pltpu.roll(packed, LANES - DOF, 1)
            there = turned[one * DOF : (one + 1) * DOF]
            value_a = jnp.where(lower, here, there)
            value_b = jnp.where(lower, jnp.where(same, 0.0, -there), here)
            if item:
                value_a = pltpu.roll(value_a, SEL * item, 1)
                value_b = pltpu.roll(value_b, SEL * item, 1)
            for part in range(BINS):
                if item == 0:
                    block_a[part] = value_a
                    block_b[part] = value_b
                else:
                    chosen = slot == (item + part) % 8
                    block_a[part] = jnp.where(chosen, value_a, block_a[part])
                    block_b[part] = jnp.where(chosen, value_b, block_b[part])
    for part in range(1, BINS):
        block_a[part] = pltpu.roll(block_a[part], LANES - SEL * part, 1)
        block_b[part] = pltpu.roll(block_b[part], LANES - SEL * part, 1)
    small = lane_ids(8)
    line = lax.broadcasted_iota(jnp.int32, (8, LANES), 0)
    place = lax.rem(small, SEL)
    base = small - place
    diagonal = jnp.zeros((8, LANES), F32)
    masks = []
    for group in range(DOF // 8):
        masks.append(place == line + group % 2 * 8)
        diagonal = diagonal + jnp.where(
            masks[group], block_a[group // 2][8 * group : 8 * group + 8], 0.0
        )
    level = jnp.sum(diagonal, axis=0, keepdims=True)
    level = jnp.broadcast_to(level, (8, LANES))
    for step in (1, 2, 4, 8):
        partner = base + lax.rem(place + step, SEL)
        level = level + jnp.take_along_axis(level, partner, axis=1)
    level = LOADING / DOF * level
    real = [[None] * 4 for _ in range(6)]
    imag = [[None] * 4 for _ in range(6)]
    for group in range(6):
        for part in range(BINS):
            real[group][part] = block_a[part][8 * group : 8 * group + 8]
            imag[group][part] = block_b[part][8 * group : 8 * group + 8]
        real[group][group // 2] = jnp.where(
            masks[group], real[group][group // 2] + level, real[group][group // 2]
        )
        real[group][3] = jnp.ones((8, LANES), F32)
        imag[group][3] = jnp.zeros((8, LANES), F32)
    inverse = [jnp.ones((8, LANES), F32)] * 6
    for k in range(0, DOF, 2):
        group, inner, part = k // 8, k % 8, k // SEL
        columns = []
        for step in range(2):
            index = base + k % SEL + step
            columns.append(
                [
                    [
                        jnp.take_along_axis(half[i][part], index, axis=1)
                        for i in range(6)
                    ]
                    for half in (real, imag)
                ]
            )
        (zero_re, zero_im), (one_re, one_im) = columns

        def line_of(value, offset):
            return jnp.broadcast_to(
                value[inner + offset : inner + offset + 1], (8, LANES)
            )

        side_re, side_im = line_of(one_re[group], 0), line_of(one_im[group], 0)
        below_re, below_im = line_of(zero_re[group], 1), line_of(zero_im[group], 1)
        first = 1.0 / line_of(zero_re[group], 0)
        below_re, below_im = below_re * first, below_im * first
        second = 1.0 / (
            line_of(one_re[group], 1) - below_re * side_re + below_im * side_im
        )
        upper, under = line == inner, line == inner + 1
        inverse[group] = jnp.where(
            upper, first, jnp.where(under, second, inverse[group])
        )
        zero_re[group] = jnp.where(upper, 0.0, zero_re[group])
        zero_im[group] = jnp.where(upper, 0.0, zero_im[group])
        alpha_re = [value * first for value in zero_re]
        alpha_im = [value * first for value in zero_im]
        beta_re = [
            (one_re[i] - alpha_re[i] * side_re + alpha_im[i] * side_im) * second
            for i in range(6)
        ]
        beta_im = [
            (one_im[i] - alpha_re[i] * side_im - alpha_im[i] * side_re) * second
            for i in range(6)
        ]
        beta_re[group] = jnp.where(under, 0.0, beta_re[group])
        beta_im[group] = jnp.where(under, 0.0, beta_im[group])
        for block in (*range(part, BINS), 3):
            row_re = line_of(real[group][block], 0)
            row_im = line_of(imag[group][block], 0)
            next_re = (
                line_of(real[group][block], 1) - below_re * row_re + below_im * row_im
            )
            next_im = (
                line_of(imag[group][block], 1) - below_re * row_im - below_im * row_re
            )
            for i in range(6):
                real[i][block] = (
                    real[i][block]
                    - alpha_re[i] * row_re
                    + alpha_im[i] * row_im
                    - beta_re[i] * next_re
                    + beta_im[i] * next_im
                )
                imag[i][block] = (
                    imag[i][block]
                    - alpha_re[i] * row_im
                    - alpha_im[i] * row_re
                    - beta_re[i] * next_im
                    - beta_im[i] * next_re
                )
    gap = jnp.zeros((SEL, LANES), F32)
    found_re = [real[i][3] * inverse[i] for i in range(6)]
    found_im = [imag[i][3] * inverse[i] for i in range(6)]
    quiet = found_re[0]
    for i in range(1, 6):
        quiet = quiet + found_re[i]
    quiet = jnp.broadcast_to(jnp.sum(quiet, axis=0, keepdims=True), (SEL, LANES))
    turn_ref[...] = jnp.transpose(
        jnp.concatenate([*found_re, quiet, *found_im, gap], 0)
    )
    found = turn_ref[pl.ds(0, 8, stride=SEL), :]
    out_ref[...] = jnp.where(small == 120, marks_ref[...], found)


def power_kernel(
    bins_ref, weights_ref, snap_ref, edge_ref,
    power_ref, first_ref, second_ref,
):
    mine = own_group()
    even = lax.rem(lax.axis_index("rng"), 2) == 0
    small = lane_ids(8)
    counts = jnp.zeros((8, LANES), F32)
    for place in range(GROUPS):
        counts = counts + weights_ref[place]
    counts = spread(counts, 120) * BLK
    low_lane = jnp.where(even, 16, 0)
    rows = SLOTS * SEL
    edge = edge_ref[...].reshape(2 * rows, LANES)
    for beam in range(OWN_BEAMS):
        lefts, quiets = [], []
        for group in (2 * beam, 2 * beam + 1):
            scaled = weights_ref[exclusive(mine, group)] * counts[beam : beam + 1, :]
            quiets.append(spread(scaled, 56))
            away = small - bins_ref[group] * SEL
            left = [[], []]
            for tile in range(rows // LANES):
                index = away + LANES * tile
                inside = jnp.logical_and(index >= 0, index < DOF)
                direct = jnp.take_along_axis(
                    scaled, lax.bitwise_and(index, LANES - 1), axis=1
                )
                crossed = jnp.take_along_axis(
                    scaled, lax.bitwise_and(index + 64, LANES - 1), axis=1
                )
                direct = jnp.where(inside, direct, 0.0)
                crossed = jnp.where(inside, crossed, 0.0)
                left[0].append(jnp.concatenate([direct, -crossed], 0).astype(BF16))
                left[1].append(jnp.concatenate([crossed, direct], 0).astype(BF16))
            lefts.append(jnp.concatenate(left[0] + left[1], 1))
        right = jnp.concatenate([snap_ref[beam].reshape(2 * rows, LANES), edge], 1)
        found = jnp.dot(
            jnp.concatenate(lefts, 0), right, preferred_element_type=F32
        )
        found = found * found
        for half in range(2):
            power = found[16 * half : 16 * half + 8] + found[16 * half + 8 : 16 * half + 16]
            inner = power[:, :LANES] / quiets[half]
            outer = power[:, LANES:] / quiets[half]
            low = spread(outer, beam + low_lane)
            high = spread(outer, beam + 16 - low_lane)
            below = jnp.where(small == 0, low, pltpu.roll(inner, 1, 1))
            above = jnp.where(
                small == LANES - 1, high, pltpu.roll(inner, LANES - 1, 1)
            )
            power_ref[2 * beam + half] = below + inner + above
    even = lax.rem(lax.axis_index("az"), 2) == 0
    for half in range(2):
        bottom, top = power_ref[half], power_ref[GROUPS - 2 + half]
        first_ref[half] = jnp.where(even, top, bottom)
        second_ref[half] = jnp.where(even, bottom, top)


def smooth_kernel(power_ref, first_ref, second_ref, out_ref):
    even = lax.rem(lax.axis_index("az"), 2) == 0
    first, second = first_ref[...], second_ref[...]
    low = jnp.where(even, second, first)
    high = jnp.where(even, first, second)
    for beam in range(OWN_BEAMS):
        below = low if beam == 0 else power_ref[2 * beam - 2 : 2 * beam]
        above = (
            high if beam == OWN_BEAMS - 1 else power_ref[2 * beam + 2 : 2 * beam + 4]
        )
        here = power_ref[2 * beam : 2 * beam + 2]
        out_ref[2 * beam : 2 * beam + 2] = (below + here + above) / 9.0


def swap(value, turn):
    return lax.ppermute(value, "rng", [(i, i ^ turn) for i in range(32)])


def halo_columns(echoes):
    ring = [(i, (i + 1) % 8) for i in range(8)]
    low = lax.ppermute(echoes, "az", ring)
    high = lax.ppermute(echoes, "az", [(b, a) for a, b in ring])
    return low, high


SMEM = pl.BlockSpec(memory_space=pltpu.SMEM)
VMEM = pl.BlockSpec(memory_space=pltpu.VMEM)


def limit(mebibytes):
    return pltpu.CompilerParams(vmem_limit_bytes=mebibytes * 2**20)


def shape(*dims, dtype=F32):
    return jax.ShapeDtypeStruct(dims, dtype)


def neighbours(count, closed):
    nearest = [(i, i ^ 1) for i in range(count)]
    across = [(i, i + 1) if i % 2 else (i, i - 1) for i in range(count)]
    if closed:
        across = [(a, b % count) for a, b in across]
    else:
        across = [(a, b) for a, b in across if 0 <= b < count]
    return nearest, across


def body(echoes, arc_start, arc_offsets, doppler_bins, steer_angles, train_mask):
    low, high = halo_columns(echoes)
    az = lax.axis_index("az")

    def own(value):
        return lax.dynamic_slice_in_dim(value, az * OWN_BEAMS, OWN_BEAMS, 0)

    marks = jnp.broadcast_to(train_mask.astype(F32), (OWN_BEAMS, LANES))
    marks = marks + swap(marks, 28)
    first = (own(arc_start) - az * OWN_COLS + ARC // 2) % COLS
    ints = jnp.concatenate(
        [first[:, None] + own(arc_offsets), own(doppler_bins), train_mask], 1
    )
    angles = own(steer_angles)
    floats = jnp.concatenate([jnp.cos(angles), jnp.sin(angles)], 1)
    centres = jnp.broadcast_to(
        own(doppler_bins).reshape(GROUPS, 8, 1), (GROUPS, 8, LANES)
    )
    transform = pl.pallas_call(
        own_kernel,
        out_shape=(
            shape(OWN_COLS, 2 * PULSES, CELLS),
            shape(2 * PULSES, 2 * PULSES, dtype=BF16),
        ),
        in_specs=[VMEM, VMEM],
        out_specs=(VMEM, VMEM),
        compiler_params=limit(8),
        name="spectra",
    )
    spec, table = transform(jnp.asarray(table_array()), echoes)
    high, table = transform(table, high)
    half = shape(8, DOF, 8 * DOF)
    snaps, keep, send, marks = pl.pallas_call(
        gram_kernel,
        out_shape=(
            shape(OWN_BEAMS, 2, SLOTS * SEL, CELLS, dtype=BF16),
            half,
            half,
            shape(OWN_BEAMS, LANES),
        ),
        in_specs=[SMEM] * 2 + [VMEM] * 5,
        out_specs=(VMEM,) * 4,
        scratch_shapes=[
            pltpu.VMEM((3 * OWN_COLS, 2 * PULSES, CELLS), F32),
            pltpu.VMEM((2, (PULSES + 1) * SEL, CELLS), F32),
            pltpu.VMEM((2, (PULSES + 2) * SEL, CELLS), BF16),
            pltpu.VMEM((2, (PULSES + 2) * SEL, CELLS), BF16),
        ],
        compiler_params=limit(16),
        name="grams",
    )(ints, floats, table, low, spec, high, marks)
    edge = shape(64, LANES, dtype=BF16)
    edges = pl.pallas_call(
        edge_out_kernel,
        out_shape=(edge, edge),
        in_specs=[VMEM],
        out_specs=(VMEM, VMEM),
        compiler_params=limit(8),
        name="edges_out",
    )(snaps)
    moved, edges = lax.optimization_barrier((swap(send, 1), edges))
    part = keep + moved
    moved = [swap(part[2:4], 4), swap(part[4:6], 2), swap(part[6:], 6)]
    edges = [
        lax.ppermute(value, "rng", pairs)
        for value, pairs in zip(edges, neighbours(32, False))
    ]
    moved, edges[0] = lax.optimization_barrier((moved, edges[0]))
    part = part[:2] + moved[0] + moved[1] + moved[2]
    part = part[0] + swap(part[1], 8)
    other = swap(part, 28)
    weights = pl.pallas_call(
        solve_kernel,
        out_shape=shape(8, LANES),
        in_specs=[VMEM] * 3,
        out_specs=VMEM,
        scratch_shapes=[pltpu.VMEM((LANES, LANES), F32)],
        compiler_params=limit(8),
        name="solve",
    )(part, other, marks)
    weights, edges[1] = lax.optimization_barrier((weights, edges[1]))
    edges = pl.pallas_call(
        edge_in_kernel,
        out_shape=shape(2, SLOTS * SEL, LANES, dtype=BF16),
        in_specs=[VMEM, VMEM],
        out_specs=VMEM,
        compiler_params=limit(8),
        name="edges_in",
    )(*edges)
    weights = weights[None]
    for turn in (8, 4, 2, 1):
        moved = swap(weights, turn)
        if turn == 2:
            moved, edges, centres = lax.optimization_barrier((moved, edges, centres))
        weights = jnp.concatenate([weights, moved], 0)
    rim = shape(2, 8, CELLS)
    power, *rims = pl.pallas_call(
        power_kernel,
        out_shape=(shape(GROUPS, 8, CELLS), rim, rim),
        in_specs=[VMEM] * 4,
        out_specs=(VMEM,) * 3,
        compiler_params=limit(12),
        name="power",
    )(centres, weights, snaps, edges)
    rims = [
        lax.ppermute(value, "az", pairs)
        for value, pairs in zip(rims, neighbours(8, True))
    ]
    smoothed = pl.pallas_call(
        smooth_kernel,
        out_shape=shape(GROUPS, 8, CELLS),
        in_specs=[VMEM] * 3,
        out_specs=VMEM,
        compiler_params=limit(8),
        name="smooth",
    )(power, *rims)
    return smoothed.reshape(OWN_BEAMS, DBINS, CELLS)


def solution(mesh):
    return jax.shard_map(
        body,
        mesh=mesh,
        in_specs=(P(None, "az", None, "rng"), P(), P(), P(), P(), P("az", "rng")),
        out_specs=P("az", None, "rng"),
        check_vma=False,
    )
```

```python
import itertools

import jax
import jax.numpy as jnp
import numpy as np
from jax import lax
from jax.experimental import pallas as pl
from jax.experimental.pallas import tpu as pltpu
from jax.sharding import PartitionSpec as P

COLS = 256
ARC = 64
BINS = 3
BEAMS = 64
BLK = 128
PULSES = 32
SEL = 16
DBINS = 16
DOF = BINS * SEL
OWN_COLS = 32
OWN_BEAMS = 8
CELLS = 128
GROUPS = 16
LANES = 128
SLOTS = PULSES + 8
LOADING = 0.1
F32 = jnp.float32
BF16 = jnp.bfloat16
TRANSPOSED = (((1,), (1,)), ((), ()))


def table_array():
    ids = np.arange(PULSES)
    steps = (ids[:, None] * ids[None, :] % PULSES).astype(np.float32)
    angle = np.float32(-2.0 * np.pi / PULSES) * steps
    real, imag = np.cos(angle), np.sin(angle)
    return np.concatenate(
        [np.concatenate([real, -imag], 1), np.concatenate([imag, real], 1)], 0
    ).astype(jnp.bfloat16)


def lane_ids(rows):
    return lax.broadcasted_iota(jnp.int32, (rows, LANES), 1)


def own_group():
    place = lax.axis_index("rng")
    bits = [lax.rem(lax.div(place, 1 << bit), 2) for bit in range(5)]
    along = exclusive(bits[2], bits[4]) * 2 + exclusive(bits[3], bits[4])
    return bits[0] * 8 + bits[1] * 4 + along


def exclusive(left, right):
    return lax.bitwise_xor(left, right)


def spectra(table, ref, pair, out_ref, base):
    blocks = [
        jnp.concatenate([ref[0, 2 * pair + one], ref[1, 2 * pair + one]], 0)
        for one in range(2)
    ]
    both = jnp.dot(table, jnp.concatenate(blocks, 1), preferred_element_type=F32)
    out_ref[base + 2 * pair] = both[:, :CELLS]
    out_ref[base + 2 * pair + 1] = both[:, CELLS:]


def own_kernel(table_ref, own_ref, spec_ref, passed_ref):
    table = table_ref[...]
    passed_ref[...] = table

    def step(index, carry):
        for one in range(4):
            spectra(table, own_ref, 4 * index + one, spec_ref, 0)
        return carry

    lax.fori_loop(0, OWN_COLS // 8, step, 0)


def first_group(step):
    return exclusive(exclusive(2 * step, 8), own_group())


def send_kernel(
    ints_ref, floats_ref,
    table_ref, low_ref, own_ref, high_ref, marks_ref,
    snap_ref, send_ref, passed_ref, spec_ref,
    wide_ref, even_ref, odd_ref,
):
    table = table_ref[...]
    passed_ref[...] = marks_ref[...]

    for pair in range(OWN_COLS // 2):
        spectra(table, low_ref, pair, spec_ref, 0)
        for column in (2 * pair, 2 * pair + 1):
            spec_ref[OWN_COLS + column] = own_ref[column]
            spec_ref[2 * OWN_COLS + column] = high_ref[column]
    four_beams(
        0, ints_ref, floats_ref, spec_ref, snap_ref, send_ref, wide_ref, even_ref, odd_ref
    )


def keep_kernel(
    ints_ref, floats_ref, spec_ref,
    snap_ref, keep_ref,
    wide_ref, even_ref, odd_ref,
):
    four_beams(
        4, ints_ref, floats_ref, spec_ref, snap_ref, keep_ref, wide_ref, even_ref, odd_ref
    )


def four_beams(
    start, ints_ref, floats_ref, spec_ref, snap_ref, out_ref, wide_ref, even_ref, odd_ref
):
    lane = lane_ids(DOF)
    row = lax.broadcasted_iota(jnp.int32, (DOF, LANES), 0)
    lower = row >= lane - jnp.where(lane < DOF, 0, DOF)
    blank = jnp.zeros((LANES - 2 * DOF, 2 * CELLS), BF16)
    last = PULSES * SEL

    def turn(step, work_ref):
        beam = lax.div(first_group(step), 2)
        for sel in range(SEL):
            column = ints_ref[beam, sel]
            real = spec_ref[column, :PULSES]
            imag = spec_ref[column, PULSES:]
            cosine = floats_ref[beam, sel]
            sine = floats_ref[beam, SEL + sel]
            rows = pl.ds(SEL + sel, PULSES, stride=SEL)
            wide_ref[0, rows, :] = cosine * real - sine * imag
            wide_ref[1, rows, :] = sine * real + cosine * imag
            if sel % 4 == 3:
                yield
        for part in range(2):
            for low, high, place in (
                (SEL, SEL + last // 2, SEL),
                (SEL + last // 2, SEL + last, SEL + last // 2),
                (last, last + SEL, 0),
                (SEL, 2 * SEL, SEL + last),
            ):
                value = wide_ref[part, low:high, :].astype(BF16)
                work_ref[part, place : place + high - low, :] = value
                snap_ref[step - start, part, place : place + high - low, :] = value
                if place in (SEL, SEL + last // 2):
                    yield
            snap_ref[step - start, part, last + 2 * SEL :, :] = jnp.zeros(
                (SLOTS * SEL - last - 2 * SEL, CELLS), BF16
            )

    def multiply(step, work_ref):
        group = first_group(step)
        beam = lax.div(group, 2)
        weight = ints_ref[beam, 2 * SEL].astype(F32)
        for half in range(2):
            base = exclusive(lax.rem(group, 2), half) * 8
            out = [None, None, None]
            for pair in range(4):
                same, turned = [], []
                for one in range(2):
                    centre = ints_ref[beam, SEL + base + pair * 2 + one]
                    rows = pl.ds(pl.multiple_of(centre * SEL, SEL), DOF)
                    real = work_ref[0, rows, :]
                    imag = work_ref[1, rows, :]
                    same.append(jnp.concatenate([real, imag], 1))
                    turned.append(jnp.concatenate([imag, -real], 1))
                left = jnp.concatenate([same[0], turned[0], same[1], turned[1]], 0)
                right = jnp.concatenate([same[0], same[1], blank], 0)
                gram = lax.dot_general(
                    left, right, TRANSPOSED, preferred_element_type=F32
                )
                packed = jnp.where(
                    lower,
                    jnp.where(lane < DOF, gram[:DOF], gram[2 * DOF : 3 * DOF]),
                    jnp.where(lane < DOF, gram[DOF : 2 * DOF], gram[3 * DOF :]),
                )
                shift = 2 * DOF * pair % LANES
                if shift:
                    packed = pltpu.roll(packed, shift, 1)
                if pair == 0:
                    out[0] = packed
                elif pair == 1:
                    out[0] = jnp.where(lane >= 96, packed, out[0])
                    out[1] = packed
                elif pair == 2:
                    out[1] = jnp.where(lane >= 64, packed, out[1])
                    out[2] = packed
                else:
                    out[2] = jnp.where(lane >= 32, packed, out[2])
                yield
            place = 2 * step % 8 + half
            for part in range(3):
                out_ref[place, :, LANES * part : LANES * (part + 1)] = (
                    out[part] * weight
                )

    def run(*works):
        for _ in itertools.zip_longest(*works):
            pass

    works = (even_ref, odd_ref)
    run(turn(start, even_ref))
    for step in range(start, start + 3):
        run(
            turn(step + 1, works[(step + 1) % 2]), multiply(step, works[step % 2])
        )
    run(multiply(start + 3, odd_ref))


def edge_out_kernel(sent_ref, kept_ref, first_ref, second_ref):
    rows = 8 * 8
    lane = lane_ids(rows)
    ends = [jnp.zeros((rows, LANES), F32) for _ in range(2)]
    for step in range(OWN_BEAMS):
        snap_ref = sent_ref if step < 4 else kept_ref
        beam = lax.div(first_group(step), 2)
        for part in range(2):
            for block in range(8):
                low = SEL + rows * block
                value = snap_ref[step % 4, part, low : low + rows, :].astype(F32)
                target = 16 * block + 8 * part + beam
                here = lane == target
                for end in range(2):
                    moved = pltpu.roll(value, lax.rem(target + end, LANES), 1)
                    ends[end] = jnp.where(here, moved, ends[end])
    even = lax.rem(lax.axis_index("rng"), 2) == 0
    first_ref[...] = jnp.where(even, ends[1], ends[0]).astype(BF16)
    second_ref[...] = jnp.where(even, ends[0], ends[1]).astype(BF16)


def edge_in_kernel(first_ref, second_ref, out_ref):
    rows = 8 * 8
    last = PULSES * SEL
    lane = lane_ids(rows)
    first = first_ref[...].astype(F32)
    second = second_ref[...].astype(F32)

    def rolled(value, shift):
        return pltpu.roll(value, shift % LANES, 1) if shift % LANES else value

    for block in range(8):
        both = jnp.where(
            lane < 16, rolled(first, -16 * block), rolled(second, 16 - 16 * block)
        )
        for part, value in enumerate((both, rolled(both, -8))):
            value = value.astype(BF16)
            out_ref[part, SEL + rows * block : SEL + rows * (block + 1), :] = value
            if block == 0:
                out_ref[part, last + SEL : last + 2 * SEL, :] = value[:SEL]
            if block == 7:
                out_ref[part, :SEL, :] = value[rows - SEL :]
    for part in range(2):
        out_ref[part, last + 2 * SEL :, :] = jnp.zeros(
            (SLOTS * SEL - last - 2 * SEL, CELLS), BF16
        )


def spread(value, index):
    return jnp.take_along_axis(
        value, jnp.full(value.shape, index, jnp.int32), axis=1
    )


def solve_kernel(first_ref, second_ref, marks_ref, out_ref, turn_ref):
    lane = lane_ids(DOF)
    row = lax.broadcasted_iota(jnp.int32, (DOF, LANES), 0)
    slot = lax.div(lane, SEL)
    lower = row >= lane
    same = row == lane
    total = first_ref[...] + second_ref[...]
    parts = [total[:, LANES * i : LANES * (i + 1)] for i in range(3)]
    block_a = [None] * BINS
    block_b = [None] * BINS
    for pair in range(4):
        if pair == 0:
            packed = parts[0]
        elif pair == 1:
            packed = jnp.where(
                lane < 32, pltpu.roll(parts[0], 32, 1), pltpu.roll(parts[1], 32, 1)
            )
        elif pair == 2:
            packed = jnp.where(
                lane < 64, pltpu.roll(parts[1], 64, 1), pltpu.roll(parts[2], 64, 1)
            )
        else:
            packed = pltpu.roll(parts[2], 96, 1)
        square = jnp.concatenate([packed, jnp.zeros((LANES - DOF, LANES), F32)], 0)
        turned = jnp.transpose(square)
        for one in range(2):
            item = pair * 2 + one
            here = packed if one == 0 else pltpu.roll(packed, LANES - DOF, 1)
            there = turned[one * DOF : (one + 1) * DOF]
            value_a = jnp.where(lower, here, there)
            value_b = jnp.where(lower, jnp.where(same, 0.0, -there), here)
            if item:
                value_a = pltpu.roll(value_a, SEL * item, 1)
                value_b = pltpu.roll(value_b, SEL * item, 1)
            for part in range(BINS):
                if item == 0:
                    block_a[part] = value_a
                    block_b[part] = value_b
                else:
                    chosen = slot == (item + part) % 8
                    block_a[part] = jnp.where(chosen, value_a, block_a[part])
                    block_b[part] = jnp.where(chosen, value_b, block_b[part])
    for part in range(1, BINS):
        block_a[part] = pltpu.roll(block_a[part], LANES - SEL * part, 1)
        block_b[part] = pltpu.roll(block_b[part], LANES - SEL * part, 1)
    small = lane_ids(8)
    line = lax.broadcasted_iota(jnp.int32, (8, LANES), 0)
    place = lax.rem(small, SEL)
    base = small - place
    diagonal = jnp.zeros((8, LANES), F32)
    masks = []
    for group in range(DOF // 8):
        masks.append(place == line + group % 2 * 8)
        diagonal = diagonal + jnp.where(
            masks[group], block_a[group // 2][8 * group : 8 * group + 8], 0.0
        )
    level = jnp.sum(diagonal, axis=0, keepdims=True)
    level = jnp.broadcast_to(level, (8, LANES))
    for step in (1, 2, 4, 8):
        partner = base + lax.rem(place + step, SEL)
        level = level + jnp.take_along_axis(level, partner, axis=1)
    level = LOADING / DOF * level
    real = [[None] * 4 for _ in range(6)]
    imag = [[None] * 4 for _ in range(6)]
    for group in range(6):
        for part in range(BINS):
            real[group][part] = block_a[part][8 * group : 8 * group + 8]
            imag[group][part] = block_b[part][8 * group : 8 * group + 8]
        real[group][group // 2] = jnp.where(
            masks[group], real[group][group // 2] + level, real[group][group // 2]
        )
        real[group][3] = jnp.ones((8, LANES), F32)
        imag[group][3] = jnp.zeros((8, LANES), F32)
    inverse = [jnp.ones((8, LANES), F32)] * 6
    for k in range(0, DOF, 2):
        group, inner, part = k // 8, k % 8, k // SEL
        columns = []
        for step in range(2):
            index = base + k % SEL + step
            columns.append(
                [
                    [
                        jnp.take_along_axis(half[i][part], index, axis=1)
                        for i in range(6)
                    ]
                    for half in (real, imag)
                ]
            )
        (zero_re, zero_im), (one_re, one_im) = columns

        def line_of(value, offset):
            return jnp.broadcast_to(
                value[inner + offset : inner + offset + 1], (8, LANES)
            )

        side_re, side_im = line_of(one_re[group], 0), line_of(one_im[group], 0)
        below_re, below_im = line_of(zero_re[group], 1), line_of(zero_im[group], 1)
        first = 1.0 / line_of(zero_re[group], 0)
        below_re, below_im = below_re * first, below_im * first
        second = 1.0 / (
            line_of(one_re[group], 1) - below_re * side_re + below_im * side_im
        )
        upper, under = line == inner, line == inner + 1
        inverse[group] = jnp.where(
            upper, first, jnp.where(under, second, inverse[group])
        )
        zero_re[group] = jnp.where(upper, 0.0, zero_re[group])
        zero_im[group] = jnp.where(upper, 0.0, zero_im[group])
        alpha_re = [value * first for value in zero_re]
        alpha_im = [value * first for value in zero_im]
        beta_re = [
            (one_re[i] - alpha_re[i] * side_re + alpha_im[i] * side_im) * second
            for i in range(6)
        ]
        beta_im = [
            (one_im[i] - alpha_re[i] * side_im - alpha_im[i] * side_re) * second
            for i in range(6)
        ]
        beta_re[group] = jnp.where(under, 0.0, beta_re[group])
        beta_im[group] = jnp.where(under, 0.0, beta_im[group])
        for block in (*range(part, BINS), 3):
            row_re = line_of(real[group][block], 0)
            row_im = line_of(imag[group][block], 0)
            next_re = (
                line_of(real[group][block], 1) - below_re * row_re + below_im * row_im
            )
            next_im = (
                line_of(imag[group][block], 1) - below_re * row_im - below_im * row_re
            )
            for i in range(6):
                real[i][block] = (
                    real[i][block]
                    - alpha_re[i] * row_re
                    + alpha_im[i] * row_im
                    - beta_re[i] * next_re
                    + beta_im[i] * next_im
                )
                imag[i][block] = (
                    imag[i][block]
                    - alpha_re[i] * row_im
                    - alpha_im[i] * row_re
                    - beta_re[i] * next_im
                    - beta_im[i] * next_re
                )
    gap = jnp.zeros((SEL, LANES), F32)
    found_re = [real[i][3] * inverse[i] for i in range(6)]
    found_im = [imag[i][3] * inverse[i] for i in range(6)]
    quiet = found_re[0]
    for i in range(1, 6):
        quiet = quiet + found_re[i]
    quiet = jnp.broadcast_to(jnp.sum(quiet, axis=0, keepdims=True), (SEL, LANES))
    turn_ref[...] = jnp.transpose(
        jnp.concatenate([*found_re, quiet, *found_im, gap], 0)
    )
    found = turn_ref[pl.ds(0, 8, stride=SEL), :]
    out_ref[...] = jnp.where(small == 120, marks_ref[...], found)


def power_kernel(
    bins_ref, weights_ref, sent_ref, kept_ref, edge_ref,
    power_ref, first_ref, second_ref,
    count_ref,
):
    mine = own_group()
    even = lax.rem(lax.axis_index("rng"), 2) == 0
    small = lane_ids(8)
    counts = jnp.zeros((8, LANES), F32)
    for place in range(GROUPS):
        counts = counts + weights_ref[place]
    count_ref[...] = spread(counts, 120) * BLK
    low_lane = jnp.where(even, 16, 0)
    rows = SLOTS * SEL
    edge = edge_ref[...].reshape(2 * rows, LANES)
    for step in range(OWN_BEAMS):
        snap_ref = sent_ref if step < 4 else kept_ref
        beam = lax.div(first_group(step), 2)
        count = jnp.broadcast_to(count_ref[pl.ds(beam, 1), :], (8, LANES))
        lefts, quiets = [], []
        for group in (2 * beam, 2 * beam + 1):
            scaled = weights_ref[exclusive(mine, group)] * count
            quiets.append(spread(scaled, 56))
            away = small - bins_ref[group] * SEL
            left = [[], []]
            for tile in range(rows // LANES):
                index = away + LANES * tile
                inside = jnp.logical_and(index >= 0, index < DOF)
                direct = jnp.take_along_axis(
                    scaled, lax.bitwise_and(index, LANES - 1), axis=1
                )
                crossed = jnp.take_along_axis(
                    scaled, lax.bitwise_and(index + 64, LANES - 1), axis=1
                )
                direct = jnp.where(inside, direct, 0.0)
                crossed = jnp.where(inside, crossed, 0.0)
                left[0].append(jnp.concatenate([direct, -crossed], 0).astype(BF16))
                left[1].append(jnp.concatenate([crossed, direct], 0).astype(BF16))
            lefts.append(jnp.concatenate(left[0] + left[1], 1))
        right = jnp.concatenate([snap_ref[step % 4].reshape(2 * rows, LANES), edge], 1)
        found = jnp.dot(
            jnp.concatenate(lefts, 0), right, preferred_element_type=F32
        )
        found = found * found
        for half in range(2):
            power = found[16 * half : 16 * half + 8] + found[16 * half + 8 : 16 * half + 16]
            inner = power[:, :LANES] / quiets[half]
            outer = power[:, LANES:] / quiets[half]
            low = spread(outer, beam + low_lane)
            high = spread(outer, beam + 16 - low_lane)
            below = jnp.where(small == 0, low, pltpu.roll(inner, 1, 1))
            above = jnp.where(
                small == LANES - 1, high, pltpu.roll(inner, LANES - 1, 1)
            )
            power_ref[2 * beam + half] = below + inner + above
    even = lax.rem(lax.axis_index("az"), 2) == 0
    for half in range(2):
        bottom, top = power_ref[half], power_ref[GROUPS - 2 + half]
        first_ref[half] = jnp.where(even, top, bottom)
        second_ref[half] = jnp.where(even, bottom, top)


def smooth_kernel(power_ref, first_ref, second_ref, out_ref):
    even = lax.rem(lax.axis_index("az"), 2) == 0
    first, second = first_ref[...], second_ref[...]
    low = jnp.where(even, second, first)
    high = jnp.where(even, first, second)
    for beam in range(OWN_BEAMS):
        below = low if beam == 0 else power_ref[2 * beam - 2 : 2 * beam]
        above = (
            high if beam == OWN_BEAMS - 1 else power_ref[2 * beam + 2 : 2 * beam + 4]
        )
        here = power_ref[2 * beam : 2 * beam + 2]
        out_ref[2 * beam : 2 * beam + 2] = (below + here + above) / 9.0


def swap(value, turn):
    return lax.ppermute(value, "rng", [(i, i ^ turn) for i in range(32)])


def halo_columns(echoes):
    ring = [(i, (i + 1) % 8) for i in range(8)]
    low = lax.ppermute(echoes, "az", ring)
    high = lax.ppermute(echoes, "az", [(b, a) for a, b in ring])
    return low, high


SMEM = pl.BlockSpec(memory_space=pltpu.SMEM)
VMEM = pl.BlockSpec(memory_space=pltpu.VMEM)


def limit(mebibytes):
    return pltpu.CompilerParams(vmem_limit_bytes=mebibytes * 2**20)


def shape(*dims, dtype=F32):
    return jax.ShapeDtypeStruct(dims, dtype)


def neighbours(count, closed):
    nearest = [(i, i ^ 1) for i in range(count)]
    across = [(i, i + 1) if i % 2 else (i, i - 1) for i in range(count)]
    if closed:
        across = [(a, b % count) for a, b in across]
    else:
        across = [(a, b) for a, b in across if 0 <= b < count]
    return nearest, across


def body(echoes, arc_start, arc_offsets, doppler_bins, steer_angles, train_mask):
    low, high = halo_columns(echoes)
    az = lax.axis_index("az")

    def own(value):
        return lax.dynamic_slice_in_dim(value, az * OWN_BEAMS, OWN_BEAMS, 0)

    marks = jnp.broadcast_to(train_mask.astype(F32), (OWN_BEAMS, LANES))
    marks = marks + swap(marks, 28)
    first = (own(arc_start) - az * OWN_COLS + ARC // 2) % COLS
    ints = jnp.concatenate(
        [first[:, None] + own(arc_offsets), own(doppler_bins), train_mask], 1
    )
    angles = own(steer_angles)
    floats = jnp.concatenate([jnp.cos(angles), jnp.sin(angles)], 1)
    centres = jnp.broadcast_to(
        own(doppler_bins).reshape(GROUPS, 8, 1), (GROUPS, 8, LANES)
    )
    transform = pl.pallas_call(
        own_kernel,
        out_shape=(
            shape(OWN_COLS, 2 * PULSES, CELLS),
            shape(2 * PULSES, 2 * PULSES, dtype=BF16),
        ),
        in_specs=[VMEM, VMEM],
        out_specs=(VMEM, VMEM),
        compiler_params=limit(8),
        name="spectra",
    )
    spec, table = transform(jnp.asarray(table_array()), echoes)
    high, table = transform(table, high)
    half = shape(8, DOF, 8 * DOF)
    some = shape(OWN_BEAMS // 2, 2, SLOTS * SEL, CELLS, dtype=BF16)
    scratch = [
        pltpu.VMEM((2, (PULSES + 1) * SEL, CELLS), F32),
        pltpu.VMEM((2, (PULSES + 2) * SEL, CELLS), BF16),
        pltpu.VMEM((2, (PULSES + 2) * SEL, CELLS), BF16),
    ]
    sent, send, marks, spectrum = pl.pallas_call(
        send_kernel,
        out_shape=(
            some,
            half,
            shape(OWN_BEAMS, LANES),
            shape(3 * OWN_COLS, 2 * PULSES, CELLS),
        ),
        in_specs=[SMEM] * 2 + [VMEM] * 5,
        out_specs=(VMEM,) * 4,
        scratch_shapes=scratch,
        compiler_params=limit(16),
        name="grams_sent",
    )(ints, floats, table, low, spec, high, marks)
    moved = swap(send, 1)
    kept, keep = pl.pallas_call(
        keep_kernel,
        out_shape=(some, half),
        in_specs=[SMEM] * 2 + [VMEM],
        out_specs=(VMEM,) * 2,
        scratch_shapes=scratch,
        compiler_params=limit(16),
        name="grams_kept",
    )(ints, floats, spectrum)
    moved, keep, kept = lax.optimization_barrier((moved, keep, kept))
    part = keep + moved
    part, kept = lax.optimization_barrier((part, kept))
    edge = shape(64, LANES, dtype=BF16)
    edges = pl.pallas_call(
        edge_out_kernel,
        out_shape=(edge, edge),
        in_specs=[VMEM, VMEM],
        out_specs=(VMEM, VMEM),
        compiler_params=limit(8),
        name="edges_out",
    )(sent, kept)
    moved = [swap(part[2:4], 4), swap(part[4:6], 2), swap(part[6:], 6)]
    edges = [
        lax.ppermute(value, "rng", pairs)
        for value, pairs in zip(edges, neighbours(32, False))
    ]
    moved, edges[0] = lax.optimization_barrier((moved, edges[0]))
    part = part[:2] + moved[0] + moved[1] + moved[2]
    part = part[0] + swap(part[1], 8)
    other = swap(part, 28)
    weights = pl.pallas_call(
        solve_kernel,
        out_shape=shape(8, LANES),
        in_specs=[VMEM] * 3,
        out_specs=VMEM,
        scratch_shapes=[pltpu.VMEM((LANES, LANES), F32)],
        compiler_params=limit(8),
        name="solve",
    )(part, other, marks)
    weights, edges[1] = lax.optimization_barrier((weights, edges[1]))
    edges = pl.pallas_call(
        edge_in_kernel,
        out_shape=shape(2, SLOTS * SEL, LANES, dtype=BF16),
        in_specs=[VMEM, VMEM],
        out_specs=VMEM,
        compiler_params=limit(8),
        name="edges_in",
    )(*edges)
    weights = weights[None]
    for turn in (8, 4, 2, 1):
        moved = swap(weights, turn)
        if turn == 2:
            moved, edges, centres = lax.optimization_barrier((moved, edges, centres))
        weights = jnp.concatenate([weights, moved], 0)
    rim = shape(2, 8, CELLS)
    power, *rims = pl.pallas_call(
        power_kernel,
        out_shape=(shape(GROUPS, 8, CELLS), rim, rim),
        in_specs=[VMEM] * 5,
        out_specs=(VMEM,) * 3,
        scratch_shapes=[pltpu.VMEM((8, LANES), F32)],
        compiler_params=limit(12),
        name="power",
    )(centres, weights, sent, kept, edges)
    rims = [
        lax.ppermute(value, "az", pairs)
        for value, pairs in zip(rims, neighbours(8, True))
    ]
    smoothed = pl.pallas_call(
        smooth_kernel,
        out_shape=shape(GROUPS, 8, CELLS),
        in_specs=[VMEM] * 3,
        out_specs=VMEM,
        compiler_params=limit(8),
        name="smooth",
    )(power, *rims)
    return smoothed.reshape(OWN_BEAMS, DBINS, CELLS)


def solution(mesh):
    return jax.shard_map(
        body,
        mesh=mesh,
        in_specs=(P(None, "az", None, "rng"), P(), P(), P(), P(), P("az", "rng")),
        out_specs=P("az", None, "rng"),
        check_vma=False,
    )
```

```python
import itertools

import jax
import jax.numpy as jnp
import numpy as np
from jax import lax
from jax.experimental import pallas as pl
from jax.experimental.pallas import tpu as pltpu
from jax.sharding import PartitionSpec as P

COLS = 256
ARC = 64
BINS = 3
BEAMS = 64
BLK = 128
PULSES = 32
SEL = 16
DBINS = 16
DOF = BINS * SEL
OWN_COLS = 32
OWN_BEAMS = 8
CELLS = 128
GROUPS = 16
LANES = 128
SLOTS = PULSES + 8
LOADING = 0.1
F32 = jnp.float32
BF16 = jnp.bfloat16
TRANSPOSED = (((1,), (1,)), ((), ()))


def table_array():
    ids = np.arange(PULSES)
    steps = (ids[:, None] * ids[None, :] % PULSES).astype(np.float32)
    angle = np.float32(-2.0 * np.pi / PULSES) * steps
    real, imag = np.cos(angle), np.sin(angle)
    return np.concatenate(
        [np.concatenate([real, -imag], 1), np.concatenate([imag, real], 1)], 0
    ).astype(jnp.bfloat16)


def lane_ids(rows):
    return lax.broadcasted_iota(jnp.int32, (rows, LANES), 1)


def own_group():
    place = lax.axis_index("rng")
    bits = [lax.rem(lax.div(place, 1 << bit), 2) for bit in range(5)]
    along = exclusive(bits[2], bits[4]) * 2 + exclusive(bits[3], bits[4])
    return bits[0] * 8 + bits[1] * 4 + along


def exclusive(left, right):
    return lax.bitwise_xor(left, right)


def spectra(table, ref, pair, out_ref, base):
    blocks = [
        jnp.concatenate([ref[0, 2 * pair + one], ref[1, 2 * pair + one]], 0)
        for one in range(2)
    ]
    both = jnp.dot(table, jnp.concatenate(blocks, 1), preferred_element_type=F32)
    out_ref[base + 2 * pair] = both[:, :CELLS]
    out_ref[base + 2 * pair + 1] = both[:, CELLS:]


def own_kernel(table_ref, own_ref, spec_ref, passed_ref):
    table = table_ref[...]
    passed_ref[...] = table

    def step(index, carry):
        for one in range(4):
            spectra(table, own_ref, 4 * index + one, spec_ref, 0)
        return carry

    lax.fori_loop(0, OWN_COLS // 8, step, 0)


def first_group(step):
    return exclusive(exclusive(2 * step, 8), own_group())


def send_kernel(
    ints_ref, floats_ref,
    table_ref, low_ref, own_ref, high_ref, marks_ref,
    snap_ref, send_ref, passed_ref, spec_ref,
    wide_ref, even_ref, odd_ref,
):
    table = table_ref[...]
    passed_ref[...] = marks_ref[...]

    for pair in range(OWN_COLS // 2):
        spectra(table, low_ref, pair, spec_ref, 0)
        for column in (2 * pair, 2 * pair + 1):
            spec_ref[OWN_COLS + column] = own_ref[column]
            spec_ref[2 * OWN_COLS + column] = high_ref[column]
    four_beams(
        0, ints_ref, floats_ref, spec_ref, snap_ref, send_ref, wide_ref, even_ref, odd_ref
    )


def keep_kernel(
    ints_ref, floats_ref, spec_ref,
    snap_ref, keep_ref,
    wide_ref, even_ref, odd_ref,
):
    four_beams(
        4, ints_ref, floats_ref, spec_ref, snap_ref, keep_ref, wide_ref, even_ref, odd_ref
    )


def four_beams(
    start, ints_ref, floats_ref, spec_ref, snap_ref, out_ref, wide_ref, even_ref, odd_ref
):
    lane = lane_ids(DOF)
    row = lax.broadcasted_iota(jnp.int32, (DOF, LANES), 0)
    lower = row >= lane - jnp.where(lane < DOF, 0, DOF)
    blank = jnp.zeros((LANES - 2 * DOF, 2 * CELLS), BF16)
    last = PULSES * SEL

    def turn(step, work_ref):
        beam = lax.div(first_group(step), 2)
        for sel in range(SEL):
            column = ints_ref[beam, sel]
            real = spec_ref[column, :PULSES]
            imag = spec_ref[column, PULSES:]
            cosine = floats_ref[beam, sel]
            sine = floats_ref[beam, SEL + sel]
            rows = pl.ds(SEL + sel, PULSES, stride=SEL)
            wide_ref[0, rows, :] = cosine * real - sine * imag
            wide_ref[1, rows, :] = sine * real + cosine * imag
            if sel % 4 == 3:
                yield
        for part in range(2):
            for low, high, place in (
                (SEL, SEL + last // 2, SEL),
                (SEL + last // 2, SEL + last, SEL + last // 2),
                (last, last + SEL, 0),
                (SEL, 2 * SEL, SEL + last),
            ):
                value = wide_ref[part, low:high, :].astype(BF16)
                work_ref[part, place : place + high - low, :] = value
                snap_ref[step - start, part, place : place + high - low, :] = value
                if place in (SEL, SEL + last // 2):
                    yield
            snap_ref[step - start, part, last + 2 * SEL :, :] = jnp.zeros(
                (SLOTS * SEL - last - 2 * SEL, CELLS), BF16
            )

    def multiply(step, work_ref):
        group = first_group(step)
        beam = lax.div(group, 2)
        weight = ints_ref[beam, 2 * SEL].astype(F32)
        for half in range(2):
            base = exclusive(lax.rem(group, 2), half) * 8
            out = [None, None, None]
            for pair in range(4):
                same, turned = [], []
                for one in range(2):
                    centre = ints_ref[beam, SEL + base + pair * 2 + one]
                    rows = pl.ds(pl.multiple_of(centre * SEL, SEL), DOF)
                    real = work_ref[0, rows, :]
                    imag = work_ref[1, rows, :]
                    same.append(jnp.concatenate([real, imag], 1))
                    turned.append(jnp.concatenate([imag, -real], 1))
                left = jnp.concatenate([same[0], turned[0], same[1], turned[1]], 0)
                right = jnp.concatenate([same[0], same[1], blank], 0)
                gram = lax.dot_general(
                    left, right, TRANSPOSED, preferred_element_type=F32
                )
                packed = jnp.where(
                    lower,
                    jnp.where(lane < DOF, gram[:DOF], gram[2 * DOF : 3 * DOF]),
                    jnp.where(lane < DOF, gram[DOF : 2 * DOF], gram[3 * DOF :]),
                )
                shift = 2 * DOF * pair % LANES
                if shift:
                    packed = pltpu.roll(packed, shift, 1)
                if pair == 0:
                    out[0] = packed
                elif pair == 1:
                    out[0] = jnp.where(lane >= 96, packed, out[0])
                    out[1] = packed
                elif pair == 2:
                    out[1] = jnp.where(lane >= 64, packed, out[1])
                    out[2] = packed
                else:
                    out[2] = jnp.where(lane >= 32, packed, out[2])
                yield
            place = 2 * step % 8 + half
            for part in range(3):
                out_ref[place, :, LANES * part : LANES * (part + 1)] = (
                    out[part] * weight
                )

    def run(*works):
        for _ in itertools.zip_longest(*works):
            pass

    works = (even_ref, odd_ref)
    run(turn(start, even_ref))
    for step in range(start, start + 3):
        run(
            turn(step + 1, works[(step + 1) % 2]), multiply(step, works[step % 2])
        )
    run(multiply(start + 3, odd_ref))


def edge_out_kernel(sent_ref, kept_ref, first_ref, second_ref):
    rows = 8 * 8
    lane = lane_ids(rows)
    ends = [jnp.zeros((rows, LANES), F32) for _ in range(2)]
    for step in range(OWN_BEAMS):
        snap_ref = sent_ref if step < 4 else kept_ref
        beam = lax.div(first_group(step), 2)
        for part in range(2):
            for block in range(8):
                low = SEL + rows * block
                value = snap_ref[step % 4, part, low : low + rows, :].astype(F32)
                target = 16 * block + 8 * part + beam
                here = lane == target
                for end in range(2):
                    moved = pltpu.roll(value, lax.rem(target + end, LANES), 1)
                    ends[end] = jnp.where(here, moved, ends[end])
    even = lax.rem(lax.axis_index("rng"), 2) == 0
    first_ref[...] = jnp.where(even, ends[1], ends[0]).astype(BF16)
    second_ref[...] = jnp.where(even, ends[0], ends[1]).astype(BF16)


def edge_in_kernel(first_ref, second_ref, out_ref):
    rows = 8 * 8
    last = PULSES * SEL
    lane = lane_ids(rows)
    first = first_ref[...].astype(F32)
    second = second_ref[...].astype(F32)

    def rolled(value, shift):
        return pltpu.roll(value, shift % LANES, 1) if shift % LANES else value

    for block in range(8):
        both = jnp.where(
            lane < 16, rolled(first, -16 * block), rolled(second, 16 - 16 * block)
        )
        for part, value in enumerate((both, rolled(both, -8))):
            value = value.astype(BF16)
            out_ref[part, SEL + rows * block : SEL + rows * (block + 1), :] = value
            if block == 0:
                out_ref[part, last + SEL : last + 2 * SEL, :] = value[:SEL]
            if block == 7:
                out_ref[part, :SEL, :] = value[rows - SEL :]
    for part in range(2):
        out_ref[part, last + 2 * SEL :, :] = jnp.zeros(
            (SLOTS * SEL - last - 2 * SEL, CELLS), BF16
        )


def spread(value, index):
    return jnp.take_along_axis(
        value, jnp.full(value.shape, index, jnp.int32), axis=1
    )


def solve_kernel(first_ref, second_ref, marks_ref, out_ref, turn_ref):
    lane = lane_ids(DOF)
    row = lax.broadcasted_iota(jnp.int32, (DOF, LANES), 0)
    slot = lax.div(lane, SEL)
    lower = row >= lane
    same = row == lane
    total = first_ref[...] + second_ref[...]
    parts = [total[:, LANES * i : LANES * (i + 1)] for i in range(3)]
    block_a = [None] * BINS
    block_b = [None] * BINS
    for pair in range(4):
        if pair == 0:
            packed = parts[0]
        elif pair == 1:
            packed = jnp.where(
                lane < 32, pltpu.roll(parts[0], 32, 1), pltpu.roll(parts[1], 32, 1)
            )
        elif pair == 2:
            packed = jnp.where(
                lane < 64, pltpu.roll(parts[1], 64, 1), pltpu.roll(parts[2], 64, 1)
            )
        else:
            packed = pltpu.roll(parts[2], 96, 1)
        square = jnp.concatenate([packed, jnp.zeros((LANES - DOF, LANES), F32)], 0)
        turned = jnp.transpose(square)
        for one in range(2):
            item = pair * 2 + one
            here = packed if one == 0 else pltpu.roll(packed, LANES - DOF, 1)
            there = turned[one * DOF : (one + 1) * DOF]
            value_a = jnp.where(lower, here, there)
            value_b = jnp.where(lower, jnp.where(same, 0.0, -there), here)
            if item:
                value_a = pltpu.roll(value_a, SEL * item, 1)
                value_b = pltpu.roll(value_b, SEL * item, 1)
            for part in range(BINS):
                if item == 0:
                    block_a[part] = value_a
                    block_b[part] = value_b
                else:
                    chosen = slot == (item + part) % 8
                    block_a[part] = jnp.where(chosen, value_a, block_a[part])
                    block_b[part] = jnp.where(chosen, value_b, block_b[part])
    for part in range(1, BINS):
        block_a[part] = pltpu.roll(block_a[part], LANES - SEL * part, 1)
        block_b[part] = pltpu.roll(block_b[part], LANES - SEL * part, 1)
    small = lane_ids(8)
    line = lax.broadcasted_iota(jnp.int32, (8, LANES), 0)
    place = lax.rem(small, SEL)
    base = small - place
    diagonal = jnp.zeros((8, LANES), F32)
    masks = []
    for group in range(DOF // 8):
        masks.append(place == line + group % 2 * 8)
        diagonal = diagonal + jnp.where(
            masks[group], block_a[group // 2][8 * group : 8 * group + 8], 0.0
        )
    level = jnp.sum(diagonal, axis=0, keepdims=True)
    level = jnp.broadcast_to(level, (8, LANES))
    for step in (1, 2, 4, 8):
        partner = base + lax.rem(place + step, SEL)
        level = level + jnp.take_along_axis(level, partner, axis=1)
    level = LOADING / DOF * level
    real = [[None] * 4 for _ in range(6)]
    imag = [[None] * 4 for _ in range(6)]
    for group in range(6):
        for part in range(BINS):
            real[group][part] = block_a[part][8 * group : 8 * group + 8]
            imag[group][part] = block_b[part][8 * group : 8 * group + 8]
        real[group][group // 2] = jnp.where(
            masks[group], real[group][group // 2] + level, real[group][group // 2]
        )
        real[group][3] = jnp.ones((8, LANES), F32)
        imag[group][3] = jnp.zeros((8, LANES), F32)
    inverse = [jnp.ones((8, LANES), F32)] * 6
    for k in range(0, DOF, 2):
        group, inner, part = k // 8, k % 8, k // SEL
        columns = []
        for step in range(2):
            index = base + k % SEL + step
            columns.append(
                [
                    [
                        jnp.take_along_axis(half[i][part], index, axis=1)
                        for i in range(6)
                    ]
                    for half in (real, imag)
                ]
            )
        (zero_re, zero_im), (one_re, one_im) = columns

        def line_of(value, offset):
            return jnp.broadcast_to(
                value[inner + offset : inner + offset + 1], (8, LANES)
            )

        side_re, side_im = line_of(one_re[group], 0), line_of(one_im[group], 0)
        below_re, below_im = line_of(zero_re[group], 1), line_of(zero_im[group], 1)
        first = 1.0 / line_of(zero_re[group], 0)
        below_re, below_im = below_re * first, below_im * first
        second = 1.0 / (
            line_of(one_re[group], 1) - below_re * side_re + below_im * side_im
        )
        upper, under = line == inner, line == inner + 1
        inverse[group] = jnp.where(
            upper, first, jnp.where(under, second, inverse[group])
        )
        zero_re[group] = jnp.where(upper, 0.0, zero_re[group])
        zero_im[group] = jnp.where(upper, 0.0, zero_im[group])
        alpha_re = [value * first for value in zero_re]
        alpha_im = [value * first for value in zero_im]
        beta_re = [
            (one_re[i] - alpha_re[i] * side_re + alpha_im[i] * side_im) * second
            for i in range(6)
        ]
        beta_im = [
            (one_im[i] - alpha_re[i] * side_im - alpha_im[i] * side_re) * second
            for i in range(6)
        ]
        beta_re[group] = jnp.where(under, 0.0, beta_re[group])
        beta_im[group] = jnp.where(under, 0.0, beta_im[group])
        for block in (*range(part, BINS), 3):
            row_re = line_of(real[group][block], 0)
            row_im = line_of(imag[group][block], 0)
            next_re = (
                line_of(real[group][block], 1) - below_re * row_re + below_im * row_im
            )
            next_im = (
                line_of(imag[group][block], 1) - below_re * row_im - below_im * row_re
            )
            for i in range(6):
                real[i][block] = (
                    real[i][block]
                    - alpha_re[i] * row_re
                    + alpha_im[i] * row_im
                    - beta_re[i] * next_re
                    + beta_im[i] * next_im
                )
                imag[i][block] = (
                    imag[i][block]
                    - alpha_re[i] * row_im
                    - alpha_im[i] * row_re
                    - beta_re[i] * next_im
                    - beta_im[i] * next_re
                )
    gap = jnp.zeros((SEL, LANES), F32)
    found_re = [real[i][3] * inverse[i] for i in range(6)]
    found_im = [imag[i][3] * inverse[i] for i in range(6)]
    quiet = found_re[0]
    for i in range(1, 6):
        quiet = quiet + found_re[i]
    quiet = jnp.broadcast_to(jnp.sum(quiet, axis=0, keepdims=True), (SEL, LANES))
    turn_ref[...] = jnp.transpose(
        jnp.concatenate([*found_re, quiet, *found_im, gap], 0)
    )
    found = turn_ref[pl.ds(0, 8, stride=SEL), :]
    out_ref[...] = jnp.where(small == 120, marks_ref[...], found)


def power_kernel(
    bins_ref, weights_ref, sent_ref, kept_ref, edge_ref,
    power_ref, first_ref, second_ref,
    count_ref,
):
    mine = own_group()
    even = lax.rem(lax.axis_index("rng"), 2) == 0
    small = lane_ids(8)
    counts = jnp.zeros((8, LANES), F32)
    for place in range(GROUPS):
        counts = counts + weights_ref[place]
    count_ref[...] = spread(counts, 120) * BLK
    low_lane = jnp.where(even, 16, 0)
    rows = SLOTS * SEL
    edge = edge_ref[...].reshape(2 * rows, LANES)
    for step in range(OWN_BEAMS):
        snap_ref = sent_ref if step < 4 else kept_ref
        beam = lax.div(first_group(step), 2)
        count = jnp.broadcast_to(count_ref[pl.ds(beam, 1), :], (8, LANES))
        lefts, quiets = [], []
        for group in (2 * beam, 2 * beam + 1):
            scaled = weights_ref[exclusive(mine, group)] * count
            quiets.append(spread(scaled, 56))
            away = small - bins_ref[group] * SEL
            left = [[], []]
            for tile in range(rows // LANES):
                index = away + LANES * tile
                inside = jnp.logical_and(index >= 0, index < DOF)
                direct = jnp.take_along_axis(
                    scaled, lax.bitwise_and(index, LANES - 1), axis=1
                )
                crossed = jnp.take_along_axis(
                    scaled, lax.bitwise_and(index + 64, LANES - 1), axis=1
                )
                direct = jnp.where(inside, direct, 0.0)
                crossed = jnp.where(inside, crossed, 0.0)
                left[0].append(jnp.concatenate([direct, -crossed], 0).astype(BF16))
                left[1].append(jnp.concatenate([crossed, direct], 0).astype(BF16))
            lefts.append(jnp.concatenate(left[0] + left[1], 1))
        right = jnp.concatenate([snap_ref[step % 4].reshape(2 * rows, LANES), edge], 1)
        found = jnp.dot(
            jnp.concatenate(lefts, 0), right, preferred_element_type=F32
        )
        found = found * found
        for half in range(2):
            power = found[16 * half : 16 * half + 8] + found[16 * half + 8 : 16 * half + 16]
            inner = power[:, :LANES] / quiets[half]
            outer = power[:, LANES:] / quiets[half]
            low = spread(outer, beam + low_lane)
            high = spread(outer, beam + 16 - low_lane)
            below = jnp.where(small == 0, low, pltpu.roll(inner, 1, 1))
            above = jnp.where(
                small == LANES - 1, high, pltpu.roll(inner, LANES - 1, 1)
            )
            power_ref[2 * beam + half] = below + inner + above
    even = lax.rem(lax.axis_index("az"), 2) == 0
    for half in range(2):
        bottom, top = power_ref[half], power_ref[GROUPS - 2 + half]
        first_ref[half] = jnp.where(even, top, bottom)
        second_ref[half] = jnp.where(even, bottom, top)


def smooth_kernel(power_ref, first_ref, second_ref, out_ref):
    even = lax.rem(lax.axis_index("az"), 2) == 0
    first, second = first_ref[...], second_ref[...]
    low = jnp.where(even, second, first)
    high = jnp.where(even, first, second)
    for beam in range(OWN_BEAMS):
        below = low if beam == 0 else power_ref[2 * beam - 2 : 2 * beam]
        above = (
            high if beam == OWN_BEAMS - 1 else power_ref[2 * beam + 2 : 2 * beam + 4]
        )
        here = power_ref[2 * beam : 2 * beam + 2]
        out_ref[2 * beam : 2 * beam + 2] = (below + here + above) / 9.0


def swap(value, turn):
    return lax.ppermute(value, "rng", [(i, i ^ turn) for i in range(32)])


def halo_columns(echoes):
    ring = [(i, (i + 1) % 8) for i in range(8)]
    low = lax.ppermute(echoes, "az", ring)
    high = lax.ppermute(echoes, "az", [(b, a) for a, b in ring])
    return low, high


SMEM = pl.BlockSpec(memory_space=pltpu.SMEM)
VMEM = pl.BlockSpec(memory_space=pltpu.VMEM)


def limit(mebibytes):
    return pltpu.CompilerParams(vmem_limit_bytes=mebibytes * 2**20)


def shape(*dims, dtype=F32):
    return jax.ShapeDtypeStruct(dims, dtype)


def neighbours(count, closed):
    nearest = [(i, i ^ 1) for i in range(count)]
    across = [(i, i + 1) if i % 2 else (i, i - 1) for i in range(count)]
    if closed:
        across = [(a, b % count) for a, b in across]
    else:
        across = [(a, b) for a, b in across if 0 <= b < count]
    return nearest, across


def body(echoes, arc_start, arc_offsets, doppler_bins, steer_angles, train_mask):
    low, high = halo_columns(echoes)
    az = lax.axis_index("az")

    def own(value):
        return lax.dynamic_slice_in_dim(value, az * OWN_BEAMS, OWN_BEAMS, 0)

    marks = jnp.broadcast_to(train_mask.astype(F32), (OWN_BEAMS, LANES))
    marks = marks + swap(marks, 28)
    first = (own(arc_start) - az * OWN_COLS + ARC // 2) % COLS
    ints = jnp.concatenate(
        [first[:, None] + own(arc_offsets), own(doppler_bins), train_mask], 1
    )
    angles = own(steer_angles)
    floats = jnp.concatenate([jnp.cos(angles), jnp.sin(angles)], 1)
    centres = jnp.broadcast_to(
        own(doppler_bins).reshape(GROUPS, 8, 1), (GROUPS, 8, LANES)
    )
    transform = pl.pallas_call(
        own_kernel,
        out_shape=(
            shape(OWN_COLS, 2 * PULSES, CELLS),
            shape(2 * PULSES, 2 * PULSES, dtype=BF16),
        ),
        in_specs=[VMEM, VMEM],
        out_specs=(VMEM, VMEM),
        compiler_params=limit(8),
        name="spectra",
    )
    spec, table = transform(jnp.asarray(table_array()), echoes)
    high, table = transform(table, high)
    half = shape(8, DOF, 8 * DOF)
    some = shape(OWN_BEAMS // 2, 2, SLOTS * SEL, CELLS, dtype=BF16)
    scratch = [
        pltpu.VMEM((2, (PULSES + 1) * SEL, CELLS), F32),
        pltpu.VMEM((2, (PULSES + 2) * SEL, CELLS), BF16),
        pltpu.VMEM((2, (PULSES + 2) * SEL, CELLS), BF16),
    ]
    sent, send, marks, spectrum = pl.pallas_call(
        send_kernel,
        out_shape=(
            some,
            half,
            shape(OWN_BEAMS, LANES),
            shape(3 * OWN_COLS, 2 * PULSES, CELLS),
        ),
        in_specs=[SMEM] * 2 + [VMEM] * 5,
        out_specs=(VMEM,) * 4,
        scratch_shapes=scratch,
        compiler_params=limit(16),
        name="grams_sent",
    )(ints, floats, table, low, spec, high, marks)
    moved = swap(send, 1)
    kept, keep = pl.pallas_call(
        keep_kernel,
        out_shape=(some, half),
        in_specs=[SMEM] * 2 + [VMEM],
        out_specs=(VMEM,) * 2,
        scratch_shapes=scratch,
        compiler_params=limit(16),
        name="grams_kept",
    )(ints, floats, spectrum)
    moved, keep, kept = lax.optimization_barrier((moved, keep, kept))
    part = keep + moved
    part, kept = lax.optimization_barrier((part, kept))
    edge = shape(64, LANES, dtype=BF16)
    edges = pl.pallas_call(
        edge_out_kernel,
        out_shape=(edge, edge),
        in_specs=[VMEM, VMEM],
        out_specs=(VMEM, VMEM),
        compiler_params=limit(8),
        name="edges_out",
    )(sent, kept)
    moved = [swap(part[2:4], 4), swap(part[4:6], 2), swap(part[6:], 6)]
    nearest, across = neighbours(32, False)
    edges = [lax.ppermute(edges[0], "rng", nearest), edges[1]]
    moved, edges[0] = lax.optimization_barrier((moved, edges[0]))
    part = part[:2] + moved[0] + moved[1] + moved[2]
    part = part[0] + swap(part[1], 8)
    other = swap(part, 28)
    weights = pl.pallas_call(
        solve_kernel,
        out_shape=shape(8, LANES),
        in_specs=[VMEM] * 3,
        out_specs=VMEM,
        scratch_shapes=[pltpu.VMEM((LANES, LANES), F32)],
        compiler_params=limit(8),
        name="solve",
    )(part, other, marks)
    weights, edges[1] = lax.optimization_barrier((weights, edges[1]))
    edges[1] = lax.ppermute(edges[1], "rng", across)
    edges = pl.pallas_call(
        edge_in_kernel,
        out_shape=shape(2, SLOTS * SEL, LANES, dtype=BF16),
        in_specs=[VMEM, VMEM],
        out_specs=VMEM,
        compiler_params=limit(8),
        name="edges_in",
    )(*edges)
    weights = weights[None]
    for turn in (8, 4, 2, 1):
        moved = swap(weights, turn)
        if turn == 2:
            moved, edges, centres = lax.optimization_barrier((moved, edges, centres))
        weights = jnp.concatenate([weights, moved], 0)
    rim = shape(2, 8, CELLS)
    power, *rims = pl.pallas_call(
        power_kernel,
        out_shape=(shape(GROUPS, 8, CELLS), rim, rim),
        in_specs=[VMEM] * 5,
        out_specs=(VMEM,) * 3,
        scratch_shapes=[pltpu.VMEM((8, LANES), F32)],
        compiler_params=limit(12),
        name="power",
    )(centres, weights, sent, kept, edges)
    rims = [
        lax.ppermute(value, "az", pairs)
        for value, pairs in zip(rims, neighbours(8, True))
    ]
    smoothed = pl.pallas_call(
        smooth_kernel,
        out_shape=shape(GROUPS, 8, CELLS),
        in_specs=[VMEM] * 3,
        out_specs=VMEM,
        compiler_params=limit(8),
        name="smooth",
    )(power, *rims)
    return smoothed.reshape(OWN_BEAMS, DBINS, CELLS)


def solution(mesh):
    return jax.shard_map(
        body,
        mesh=mesh,
        in_specs=(P(None, "az", None, "rng"), P(), P(), P(), P(), P("az", "rng")),
        out_specs=P("az", None, "rng"),
        check_vma=False,
    )
```

```python
import itertools

import jax
import jax.numpy as jnp
import numpy as np
from jax import lax
from jax.experimental import pallas as pl
from jax.experimental.pallas import tpu as pltpu
from jax.sharding import PartitionSpec as P

COLS = 256
ARC = 64
BINS = 3
BEAMS = 64
BLK = 128
PULSES = 32
SEL = 16
DBINS = 16
DOF = BINS * SEL
OWN_COLS = 32
OWN_BEAMS = 8
CELLS = 128
GROUPS = 16
LANES = 128
SLOTS = PULSES + 8
LOADING = 0.1
F32 = jnp.float32
BF16 = jnp.bfloat16
TRANSPOSED = (((1,), (1,)), ((), ()))


def table_array():
    ids = np.arange(PULSES)
    steps = (ids[:, None] * ids[None, :] % PULSES).astype(np.float32)
    angle = np.float32(-2.0 * np.pi / PULSES) * steps
    real, imag = np.cos(angle), np.sin(angle)
    return np.concatenate(
        [np.concatenate([real, -imag], 1), np.concatenate([imag, real], 1)], 0
    ).astype(jnp.bfloat16)


def lane_ids(rows):
    return lax.broadcasted_iota(jnp.int32, (rows, LANES), 1)


def own_group():
    place = lax.axis_index("rng")
    bits = [lax.rem(lax.div(place, 1 << bit), 2) for bit in range(5)]
    along = exclusive(bits[2], bits[4]) * 2 + exclusive(bits[3], bits[4])
    return bits[0] * 8 + bits[1] * 4 + along


def exclusive(left, right):
    return lax.bitwise_xor(left, right)


def spectra(table, ref, pair, out_ref, base):
    blocks = [
        jnp.concatenate([ref[0, 2 * pair + one], ref[1, 2 * pair + one]], 0)
        for one in range(2)
    ]
    both = jnp.dot(table, jnp.concatenate(blocks, 1), preferred_element_type=F32)
    out_ref[base + 2 * pair] = both[:, :CELLS]
    out_ref[base + 2 * pair + 1] = both[:, CELLS:]


def own_kernel(table_ref, own_ref, spec_ref, passed_ref):
    table = table_ref[...]
    passed_ref[...] = table

    def step(index, carry):
        for one in range(4):
            spectra(table, own_ref, 4 * index + one, spec_ref, 0)
        return carry

    lax.fori_loop(0, OWN_COLS // 8, step, 0)


def first_group(step):
    return exclusive(exclusive(2 * step, 8), own_group())


def send_kernel(
    ints_ref, floats_ref,
    table_ref, low_ref, own_ref, high_ref, marks_ref,
    snap_ref, send_ref, passed_ref, spec_ref,
    wide_ref, even_ref, odd_ref,
):
    table = table_ref[...]
    passed_ref[...] = marks_ref[...]

    for pair in range(OWN_COLS // 2):
        spectra(table, low_ref, pair, spec_ref, 0)
        for column in (2 * pair, 2 * pair + 1):
            spec_ref[OWN_COLS + column] = own_ref[column]
            spec_ref[2 * OWN_COLS + column] = high_ref[column]
    four_beams(
        0, ints_ref, floats_ref, spec_ref, snap_ref, send_ref, wide_ref, even_ref, odd_ref
    )


def keep_kernel(
    ints_ref, floats_ref, spec_ref,
    snap_ref, keep_ref,
    wide_ref, even_ref, odd_ref,
):
    four_beams(
        4, ints_ref, floats_ref, spec_ref, snap_ref, keep_ref, wide_ref, even_ref, odd_ref
    )


def four_beams(
    start, ints_ref, floats_ref, spec_ref, snap_ref, out_ref, wide_ref, even_ref, odd_ref
):
    lane = lane_ids(DOF)
    row = lax.broadcasted_iota(jnp.int32, (DOF, LANES), 0)
    lower = row >= lane - jnp.where(lane < DOF, 0, DOF)
    blank = jnp.zeros((LANES - 2 * DOF, 2 * CELLS), BF16)
    last = PULSES * SEL

    def turn(step, work_ref):
        beam = lax.div(first_group(step), 2)
        for sel in range(SEL):
            column = ints_ref[beam, sel]
            real = spec_ref[column, :PULSES]
            imag = spec_ref[column, PULSES:]
            cosine = floats_ref[beam, sel]
            sine = floats_ref[beam, SEL + sel]
            rows = pl.ds(SEL + sel, PULSES, stride=SEL)
            wide_ref[0, rows, :] = cosine * real - sine * imag
            wide_ref[1, rows, :] = sine * real + cosine * imag
            if sel % 4 == 3:
                yield
        for part in range(2):
            for low, high, place in (
                (SEL, SEL + last // 2, SEL),
                (SEL + last // 2, SEL + last, SEL + last // 2),
                (last, last + SEL, 0),
                (SEL, 2 * SEL, SEL + last),
            ):
                value = wide_ref[part, low:high, :].astype(BF16)
                work_ref[part, place : place + high - low, :] = value
                snap_ref[step - start, part, place : place + high - low, :] = value
                if place in (SEL, SEL + last // 2):
                    yield
            snap_ref[step - start, part, last + 2 * SEL :, :] = jnp.zeros(
                (SLOTS * SEL - last - 2 * SEL, CELLS), BF16
            )

    def multiply(step, work_ref):
        group = first_group(step)
        beam = lax.div(group, 2)
        weight = ints_ref[beam, 2 * SEL].astype(F32)
        for half in range(2):
            base = exclusive(lax.rem(group, 2), half) * 8
            out = [None, None, None]
            for pair in range(4):
                same, turned = [], []
                for one in range(2):
                    centre = ints_ref[beam, SEL + base + pair * 2 + one]
                    rows = pl.ds(pl.multiple_of(centre * SEL, SEL), DOF)
                    real = work_ref[0, rows, :]
                    imag = work_ref[1, rows, :]
                    same.append(jnp.concatenate([real, imag], 1))
                    turned.append(jnp.concatenate([imag, -real], 1))
                left = jnp.concatenate([same[0], turned[0], same[1], turned[1]], 0)
                right = jnp.concatenate([same[0], same[1], blank], 0)
                gram = lax.dot_general(
                    left, right, TRANSPOSED, preferred_element_type=F32
                )
                packed = jnp.where(
                    lower,
                    jnp.where(lane < DOF, gram[:DOF], gram[2 * DOF : 3 * DOF]),
                    jnp.where(lane < DOF, gram[DOF : 2 * DOF], gram[3 * DOF :]),
                )
                shift = 2 * DOF * pair % LANES
                if shift:
                    packed = pltpu.roll(packed, shift, 1)
                if pair == 0:
                    out[0] = packed
                elif pair == 1:
                    out[0] = jnp.where(lane >= 96, packed, out[0])
                    out[1] = packed
                elif pair == 2:
                    out[1] = jnp.where(lane >= 64, packed, out[1])
                    out[2] = packed
                else:
                    out[2] = jnp.where(lane >= 32, packed, out[2])
                yield
            place = 2 * step % 8 + half
            for part in range(3):
                out_ref[place, :, LANES * part : LANES * (part + 1)] = (
                    out[part] * weight
                )

    def run(*works):
        for _ in itertools.zip_longest(*works):
            pass

    works = (even_ref, odd_ref)
    run(turn(start, even_ref))
    for step in range(start, start + 3):
        run(
            turn(step + 1, works[(step + 1) % 2]), multiply(step, works[step % 2])
        )
    run(multiply(start + 3, odd_ref))


def edge_out_kernel(sent_ref, kept_ref, first_ref, second_ref):
    rows = 8 * 8
    lane = lane_ids(rows)
    ends = [jnp.zeros((rows, LANES), F32) for _ in range(2)]
    for step in range(OWN_BEAMS):
        snap_ref = sent_ref if step < 4 else kept_ref
        beam = lax.div(first_group(step), 2)
        for part in range(2):
            for block in range(8):
                low = SEL + rows * block
                value = snap_ref[step % 4, part, low : low + rows, :].astype(F32)
                target = 16 * block + 8 * part + beam
                here = lane == target
                for end in range(2):
                    moved = pltpu.roll(value, lax.rem(target + end, LANES), 1)
                    ends[end] = jnp.where(here, moved, ends[end])
    even = lax.rem(lax.axis_index("rng"), 2) == 0
    first_ref[...] = jnp.where(even, ends[1], ends[0]).astype(BF16)
    second_ref[...] = jnp.where(even, ends[0], ends[1]).astype(BF16)


def edge_in_kernel(first_ref, second_ref, out_ref):
    rows = 8 * 8
    last = PULSES * SEL
    lane = lane_ids(rows)
    first = first_ref[...].astype(F32)
    second = second_ref[...].astype(F32)

    def rolled(value, shift):
        return pltpu.roll(value, shift % LANES, 1) if shift % LANES else value

    for block in range(8):
        both = jnp.where(
            lane < 16, rolled(first, -16 * block), rolled(second, 16 - 16 * block)
        )
        for part, value in enumerate((both, rolled(both, -8))):
            value = value.astype(BF16)
            out_ref[part, SEL + rows * block : SEL + rows * (block + 1), :] = value
            if block == 0:
                out_ref[part, last + SEL : last + 2 * SEL, :] = value[:SEL]
            if block == 7:
                out_ref[part, :SEL, :] = value[rows - SEL :]
    for part in range(2):
        out_ref[part, last + 2 * SEL :, :] = jnp.zeros(
            (SLOTS * SEL - last - 2 * SEL, CELLS), BF16
        )


def spread(value, index):
    return jnp.take_along_axis(
        value, jnp.full(value.shape, index, jnp.int32), axis=1
    )


def solve_kernel(first_ref, second_ref, marks_ref, out_ref, turn_ref):
    lane = lane_ids(DOF)
    row = lax.broadcasted_iota(jnp.int32, (DOF, LANES), 0)
    slot = lax.div(lane, SEL)
    lower = row >= lane
    same = row == lane
    total = first_ref[...] + second_ref[...]
    parts = [total[:, LANES * i : LANES * (i + 1)] for i in range(3)]
    block_a = [None] * BINS
    block_b = [None] * BINS
    for pair in range(4):
        if pair == 0:
            packed = parts[0]
        elif pair == 1:
            packed = jnp.where(
                lane < 32, pltpu.roll(parts[0], 32, 1), pltpu.roll(parts[1], 32, 1)
            )
        elif pair == 2:
            packed = jnp.where(
                lane < 64, pltpu.roll(parts[1], 64, 1), pltpu.roll(parts[2], 64, 1)
            )
        else:
            packed = pltpu.roll(parts[2], 96, 1)
        square = jnp.concatenate([packed, jnp.zeros((LANES - DOF, LANES), F32)], 0)
        turned = jnp.transpose(square)
        for one in range(2):
            item = pair * 2 + one
            here = packed if one == 0 else pltpu.roll(packed, LANES - DOF, 1)
            there = turned[one * DOF : (one + 1) * DOF]
            value_a = jnp.where(lower, here, there)
            value_b = jnp.where(lower, jnp.where(same, 0.0, -there), here)
            if item:
                value_a = pltpu.roll(value_a, SEL * item, 1)
                value_b = pltpu.roll(value_b, SEL * item, 1)
            for part in range(BINS):
                if item == 0:
                    block_a[part] = value_a
                    block_b[part] = value_b
                else:
                    chosen = slot == (item + part) % 8
                    block_a[part] = jnp.where(chosen, value_a, block_a[part])
                    block_b[part] = jnp.where(chosen, value_b, block_b[part])
    for part in range(1, BINS):
        block_a[part] = pltpu.roll(block_a[part], LANES - SEL * part, 1)
        block_b[part] = pltpu.roll(block_b[part], LANES - SEL * part, 1)
    small = lane_ids(8)
    line = lax.broadcasted_iota(jnp.int32, (8, LANES), 0)
    place = lax.rem(small, SEL)
    base = small - place
    diagonal = jnp.zeros((8, LANES), F32)
    masks = []
    for group in range(DOF // 8):
        masks.append(place == line + group % 2 * 8)
        diagonal = diagonal + jnp.where(
            masks[group], block_a[group // 2][8 * group : 8 * group + 8], 0.0
        )
    level = jnp.sum(diagonal, axis=0, keepdims=True)
    level = jnp.broadcast_to(level, (8, LANES))
    for step in (1, 2, 4, 8):
        partner = base + lax.rem(place + step, SEL)
        level = level + jnp.take_along_axis(level, partner, axis=1)
    level = LOADING / DOF * level
    real = [[None] * 4 for _ in range(6)]
    imag = [[None] * 4 for _ in range(6)]
    for group in range(6):
        for part in range(BINS):
            real[group][part] = block_a[part][8 * group : 8 * group + 8]
            imag[group][part] = block_b[part][8 * group : 8 * group + 8]
        real[group][group // 2] = jnp.where(
            masks[group], real[group][group // 2] + level, real[group][group // 2]
        )
        real[group][3] = jnp.ones((8, LANES), F32)
        imag[group][3] = jnp.zeros((8, LANES), F32)
    inverse = [jnp.ones((8, LANES), F32)] * 6
    for k in range(0, DOF, 2):
        group, inner, part = k // 8, k % 8, k // SEL
        columns = []
        for step in range(2):
            index = base + k % SEL + step
            columns.append(
                [
                    [
                        jnp.take_along_axis(half[i][part], index, axis=1)
                        for i in range(6)
                    ]
                    for half in (real, imag)
                ]
            )
        (zero_re, zero_im), (one_re, one_im) = columns

        def line_of(value, offset):
            return jnp.broadcast_to(
                value[inner + offset : inner + offset + 1], (8, LANES)
            )

        side_re, side_im = line_of(one_re[group], 0), line_of(one_im[group], 0)
        below_re, below_im = line_of(zero_re[group], 1), line_of(zero_im[group], 1)
        first = 1.0 / line_of(zero_re[group], 0)
        below_re, below_im = below_re * first, below_im * first
        second = 1.0 / (
            line_of(one_re[group], 1) - below_re * side_re + below_im * side_im
        )
        upper, under = line == inner, line == inner + 1
        inverse[group] = jnp.where(
            upper, first, jnp.where(under, second, inverse[group])
        )
        zero_re[group] = jnp.where(upper, 0.0, zero_re[group])
        zero_im[group] = jnp.where(upper, 0.0, zero_im[group])
        alpha_re = [value * first for value in zero_re]
        alpha_im = [value * first for value in zero_im]
        beta_re = [
            (one_re[i] - alpha_re[i] * side_re + alpha_im[i] * side_im) * second
            for i in range(6)
        ]
        beta_im = [
            (one_im[i] - alpha_re[i] * side_im - alpha_im[i] * side_re) * second
            for i in range(6)
        ]
        beta_re[group] = jnp.where(under, 0.0, beta_re[group])
        beta_im[group] = jnp.where(under, 0.0, beta_im[group])
        for block in (*range(part, BINS), 3):
            row_re = line_of(real[group][block], 0)
            row_im = line_of(imag[group][block], 0)
            next_re = (
                line_of(real[group][block], 1) - below_re * row_re + below_im * row_im
            )
            next_im = (
                line_of(imag[group][block], 1) - below_re * row_im - below_im * row_re
            )
            for i in range(6):
                real[i][block] = (
                    real[i][block]
                    - alpha_re[i] * row_re
                    + alpha_im[i] * row_im
                    - beta_re[i] * next_re
                    + beta_im[i] * next_im
                )
                imag[i][block] = (
                    imag[i][block]
                    - alpha_re[i] * row_im
                    - alpha_im[i] * row_re
                    - beta_re[i] * next_im
                    - beta_im[i] * next_re
                )
    gap = jnp.zeros((SEL, LANES), F32)
    found_re = [real[i][3] * inverse[i] for i in range(6)]
    found_im = [imag[i][3] * inverse[i] for i in range(6)]
    quiet = found_re[0]
    for i in range(1, 6):
        quiet = quiet + found_re[i]
    quiet = jnp.broadcast_to(jnp.sum(quiet, axis=0, keepdims=True), (SEL, LANES))
    turn_ref[...] = jnp.transpose(
        jnp.concatenate([*found_re, quiet, *found_im, gap], 0)
    )
    found = turn_ref[pl.ds(0, 8, stride=SEL), :]
    out_ref[...] = jnp.where(small == 120, marks_ref[...], found)


def power_kernel(
    bins_ref, weights_ref, sent_ref, kept_ref, edge_ref,
    power_ref, first_ref, second_ref,
    count_ref,
):
    mine = own_group()
    even = lax.rem(lax.axis_index("rng"), 2) == 0
    small = lane_ids(8)
    counts = jnp.zeros((8, LANES), F32)
    for place in range(GROUPS):
        counts = counts + weights_ref[place]
    count_ref[...] = spread(counts, 120) * BLK
    low_lane = jnp.where(even, 16, 0)
    rows = SLOTS * SEL
    edge = edge_ref[...].reshape(2 * rows, LANES)
    for step in range(OWN_BEAMS):
        snap_ref = sent_ref if step < 4 else kept_ref
        beam = lax.div(first_group(step), 2)
        count = jnp.broadcast_to(count_ref[pl.ds(beam, 1), :], (8, LANES))
        lefts, quiets = [], []
        for group in (2 * beam, 2 * beam + 1):
            scaled = weights_ref[exclusive(mine, group)] * count
            quiets.append(spread(scaled, 56))
            away = small - bins_ref[group] * SEL
            left = [[], []]
            for tile in range(rows // LANES):
                index = away + LANES * tile
                inside = jnp.logical_and(index >= 0, index < DOF)
                direct = jnp.take_along_axis(
                    scaled, lax.bitwise_and(index, LANES - 1), axis=1
                )
                crossed = jnp.take_along_axis(
                    scaled, lax.bitwise_and(index + 64, LANES - 1), axis=1
                )
                direct = jnp.where(inside, direct, 0.0)
                crossed = jnp.where(inside, crossed, 0.0)
                left[0].append(jnp.concatenate([direct, -crossed], 0).astype(BF16))
                left[1].append(jnp.concatenate([crossed, direct], 0).astype(BF16))
            lefts.append(jnp.concatenate(left[0] + left[1], 1))
        right = jnp.concatenate([snap_ref[step % 4].reshape(2 * rows, LANES), edge], 1)
        found = jnp.dot(
            jnp.concatenate(lefts, 0), right, preferred_element_type=F32
        )
        found = found * found
        for half in range(2):
            power = found[16 * half : 16 * half + 8] + found[16 * half + 8 : 16 * half + 16]
            inner = power[:, :LANES] / quiets[half]
            outer = power[:, LANES:] / quiets[half]
            low = spread(outer, beam + low_lane)
            high = spread(outer, beam + 16 - low_lane)
            below = jnp.where(small == 0, low, pltpu.roll(inner, 1, 1))
            above = jnp.where(
                small == LANES - 1, high, pltpu.roll(inner, LANES - 1, 1)
            )
            power_ref[2 * beam + half] = below + inner + above
    even = lax.rem(lax.axis_index("az"), 2) == 0
    for half in range(2):
        bottom, top = power_ref[half], power_ref[GROUPS - 2 + half]
        first_ref[half] = jnp.where(even, top, bottom)
        second_ref[half] = jnp.where(even, bottom, top)


def smooth_kernel(power_ref, first_ref, second_ref, out_ref):
    even = lax.rem(lax.axis_index("az"), 2) == 0
    first, second = first_ref[...], second_ref[...]
    low = jnp.where(even, second, first)
    high = jnp.where(even, first, second)
    for beam in range(OWN_BEAMS):
        below = low if beam == 0 else power_ref[2 * beam - 2 : 2 * beam]
        above = (
            high if beam == OWN_BEAMS - 1 else power_ref[2 * beam + 2 : 2 * beam + 4]
        )
        here = power_ref[2 * beam : 2 * beam + 2]
        out_ref[2 * beam : 2 * beam + 2] = (below + here + above) / 9.0


def swap(value, turn):
    return lax.ppermute(value, "rng", [(i, i ^ turn) for i in range(32)])


def halo_columns(echoes):
    ring = [(i, (i + 1) % 8) for i in range(8)]
    low = lax.ppermute(echoes, "az", ring)
    high = lax.ppermute(echoes, "az", [(b, a) for a, b in ring])
    return low, high


SMEM = pl.BlockSpec(memory_space=pltpu.SMEM)
VMEM = pl.BlockSpec(memory_space=pltpu.VMEM)


def limit(mebibytes):
    return pltpu.CompilerParams(vmem_limit_bytes=mebibytes * 2**20)


def shape(*dims, dtype=F32):
    return jax.ShapeDtypeStruct(dims, dtype)


def neighbours(count, closed):
    nearest = [(i, i ^ 1) for i in range(count)]
    across = [(i, i + 1) if i % 2 else (i, i - 1) for i in range(count)]
    if closed:
        across = [(a, b % count) for a, b in across]
    else:
        across = [(a, b) for a, b in across if 0 <= b < count]
    return nearest, across


def body(echoes, arc_start, arc_offsets, doppler_bins, steer_angles, train_mask):
    low, high = halo_columns(echoes)
    az = lax.axis_index("az")

    def own(value):
        return lax.dynamic_slice_in_dim(value, az * OWN_BEAMS, OWN_BEAMS, 0)

    marks = jnp.broadcast_to(train_mask.astype(F32), (OWN_BEAMS, LANES))
    marks = marks + swap(marks, 28)
    first = (own(arc_start) - az * OWN_COLS + ARC // 2) % COLS
    ints = jnp.concatenate(
        [first[:, None] + own(arc_offsets), own(doppler_bins), train_mask], 1
    )
    angles = own(steer_angles)
    floats = jnp.concatenate([jnp.cos(angles), jnp.sin(angles)], 1)
    centres = jnp.broadcast_to(
        own(doppler_bins).reshape(GROUPS, 8, 1), (GROUPS, 8, LANES)
    )
    transform = pl.pallas_call(
        own_kernel,
        out_shape=(
            shape(OWN_COLS, 2 * PULSES, CELLS),
            shape(2 * PULSES, 2 * PULSES, dtype=BF16),
        ),
        in_specs=[VMEM, VMEM],
        out_specs=(VMEM, VMEM),
        compiler_params=limit(8),
        name="spectra",
    )
    spec, table = transform(jnp.asarray(table_array()), echoes)
    high, table = transform(table, high)
    half = shape(8, DOF, 8 * DOF)
    some = shape(OWN_BEAMS // 2, 2, SLOTS * SEL, CELLS, dtype=BF16)
    scratch = [
        pltpu.VMEM((2, (PULSES + 1) * SEL, CELLS), F32),
        pltpu.VMEM((2, (PULSES + 2) * SEL, CELLS), BF16),
        pltpu.VMEM((2, (PULSES + 2) * SEL, CELLS), BF16),
    ]
    sent, send, marks, spectrum = pl.pallas_call(
        send_kernel,
        out_shape=(
            some,
            half,
            shape(OWN_BEAMS, LANES),
            shape(3 * OWN_COLS, 2 * PULSES, CELLS),
        ),
        in_specs=[SMEM] * 2 + [VMEM] * 5,
        out_specs=(VMEM,) * 4,
        scratch_shapes=scratch,
        compiler_params=limit(16),
        name="grams_sent",
    )(ints, floats, table, low, spec, high, marks)
    moved = swap(send, 1)
    kept, keep = pl.pallas_call(
        keep_kernel,
        out_shape=(some, half),
        in_specs=[SMEM] * 2 + [VMEM],
        out_specs=(VMEM,) * 2,
        scratch_shapes=scratch,
        compiler_params=limit(16),
        name="grams_kept",
    )(ints, floats, spectrum)
    moved, keep, kept = lax.optimization_barrier((moved, keep, kept))
    part = keep + moved
    part, kept = lax.optimization_barrier((part, kept))
    edge = shape(64, LANES, dtype=BF16)
    edges = pl.pallas_call(
        edge_out_kernel,
        out_shape=(edge, edge),
        in_specs=[VMEM, VMEM],
        out_specs=(VMEM, VMEM),
        compiler_params=limit(8),
        name="edges_out",
    )(sent, kept)
    moved = [swap(part[4:6], 2), swap(part[6:], 6), swap(part[2:4], 4)]
    edges = [
        lax.ppermute(value, "rng", pairs)
        for value, pairs in zip(edges, neighbours(32, False))
    ]
    moved, edges[0] = lax.optimization_barrier((moved, edges[0]))
    part = part[:2] + moved[0] + moved[1] + moved[2]
    part = part[0] + swap(part[1], 8)
    other = swap(part, 28)
    weights = pl.pallas_call(
        solve_kernel,
        out_shape=shape(8, LANES),
        in_specs=[VMEM] * 3,
        out_specs=VMEM,
        scratch_shapes=[pltpu.VMEM((LANES, LANES), F32)],
        compiler_params=limit(8),
        name="solve",
    )(part, other, marks)
    weights, edges[1] = lax.optimization_barrier((weights, edges[1]))
    edges = pl.pallas_call(
        edge_in_kernel,
        out_shape=shape(2, SLOTS * SEL, LANES, dtype=BF16),
        in_specs=[VMEM, VMEM],
        out_specs=VMEM,
        compiler_params=limit(8),
        name="edges_in",
    )(*edges)
    weights = weights[None]
    for turn in (8, 4, 2, 1):
        moved = swap(weights, turn)
        if turn == 2:
            moved, edges, centres = lax.optimization_barrier((moved, edges, centres))
        weights = jnp.concatenate([weights, moved], 0)
    rim = shape(2, 8, CELLS)
    power, *rims = pl.pallas_call(
        power_kernel,
        out_shape=(shape(GROUPS, 8, CELLS), rim, rim),
        in_specs=[VMEM] * 5,
        out_specs=(VMEM,) * 3,
        scratch_shapes=[pltpu.VMEM((8, LANES), F32)],
        compiler_params=limit(12),
        name="power",
    )(centres, weights, sent, kept, edges)
    rims = [
        lax.ppermute(value, "az", pairs)
        for value, pairs in zip(rims, neighbours(8, True))
    ]
    smoothed = pl.pallas_call(
        smooth_kernel,
        out_shape=shape(GROUPS, 8, CELLS),
        in_specs=[VMEM] * 3,
        out_specs=VMEM,
        compiler_params=limit(8),
        name="smooth",
    )(power, *rims)
    return smoothed.reshape(OWN_BEAMS, DBINS, CELLS)


def solution(mesh):
    return jax.shard_map(
        body,
        mesh=mesh,
        in_specs=(P(None, "az", None, "rng"), P(), P(), P(), P(), P("az", "rng")),
        out_specs=P("az", None, "rng"),
        check_vma=False,
    )
```

```python
import itertools

import jax
import jax.numpy as jnp
import numpy as np
from jax import lax
from jax.experimental import pallas as pl
from jax.experimental.pallas import tpu as pltpu
from jax.sharding import PartitionSpec as P

COLS = 256
ARC = 64
BINS = 3
BEAMS = 64
BLK = 128
PULSES = 32
SEL = 16
DBINS = 16
DOF = BINS * SEL
OWN_COLS = 32
OWN_BEAMS = 8
CELLS = 128
GROUPS = 16
LANES = 128
SLOTS = PULSES + 8
LOADING = 0.1
F32 = jnp.float32
BF16 = jnp.bfloat16
TRANSPOSED = (((1,), (1,)), ((), ()))


def table_array():
    ids = np.arange(PULSES)
    steps = (ids[:, None] * ids[None, :] % PULSES).astype(np.float32)
    angle = np.float32(-2.0 * np.pi / PULSES) * steps
    real, imag = np.cos(angle), np.sin(angle)
    return np.concatenate(
        [np.concatenate([real, -imag], 1), np.concatenate([imag, real], 1)], 0
    ).astype(jnp.bfloat16)


def lane_ids(rows):
    return lax.broadcasted_iota(jnp.int32, (rows, LANES), 1)


def own_group():
    place = lax.axis_index("rng")
    bits = [lax.rem(lax.div(place, 1 << bit), 2) for bit in range(5)]
    along = exclusive(bits[2], bits[4]) * 2 + exclusive(bits[3], bits[4])
    return bits[0] * 8 + bits[1] * 4 + along


def exclusive(left, right):
    return lax.bitwise_xor(left, right)


def spectra(table, ref, pair, out_ref, base):
    blocks = [
        jnp.concatenate([ref[0, 2 * pair + one], ref[1, 2 * pair + one]], 0)
        for one in range(2)
    ]
    both = jnp.dot(table, jnp.concatenate(blocks, 1), preferred_element_type=F32)
    out_ref[base + 2 * pair] = both[:, :CELLS]
    out_ref[base + 2 * pair + 1] = both[:, CELLS:]


def own_kernel(table_ref, own_ref, spec_ref, passed_ref):
    table = table_ref[...]
    passed_ref[...] = table

    def step(index, carry):
        for one in range(4):
            spectra(table, own_ref, 4 * index + one, spec_ref, 0)
        return carry

    lax.fori_loop(0, OWN_COLS // 8, step, 0)


def first_group(step):
    return exclusive(exclusive(2 * step, 8), own_group())


def send_kernel(
    ints_ref, floats_ref,
    table_ref, low_ref, own_ref, high_ref, marks_ref,
    snap_ref, send_ref, passed_ref, spec_ref,
    wide_ref, even_ref, odd_ref,
):
    table = table_ref[...]
    passed_ref[...] = marks_ref[...]

    for pair in range(OWN_COLS // 2):
        spectra(table, low_ref, pair, spec_ref, 0)
        for column in (2 * pair, 2 * pair + 1):
            spec_ref[OWN_COLS + column] = own_ref[column]
            spec_ref[2 * OWN_COLS + column] = high_ref[column]
    four_beams(
        0, ints_ref, floats_ref, spec_ref, snap_ref, send_ref, wide_ref, even_ref, odd_ref
    )


def keep_kernel(
    ints_ref, floats_ref, spec_ref,
    snap_ref, keep_ref,
    wide_ref, even_ref, odd_ref,
):
    four_beams(
        4, ints_ref, floats_ref, spec_ref, snap_ref, keep_ref, wide_ref, even_ref, odd_ref
    )


def four_beams(
    start, ints_ref, floats_ref, spec_ref, snap_ref, out_ref, wide_ref, even_ref, odd_ref
):
    lane = lane_ids(DOF)
    row = lax.broadcasted_iota(jnp.int32, (DOF, LANES), 0)
    lower = row >= lane - jnp.where(lane < DOF, 0, DOF)
    blank = jnp.zeros((LANES - 2 * DOF, 2 * CELLS), BF16)
    last = PULSES * SEL

    def turn(step, work_ref):
        beam = lax.div(first_group(step), 2)
        for sel in range(SEL):
            column = ints_ref[beam, sel]
            real = spec_ref[column, :PULSES]
            imag = spec_ref[column, PULSES:]
            cosine = floats_ref[beam, sel]
            sine = floats_ref[beam, SEL + sel]
            rows = pl.ds(SEL + sel, PULSES, stride=SEL)
            wide_ref[0, rows, :] = cosine * real - sine * imag
            wide_ref[1, rows, :] = sine * real + cosine * imag
            if sel % 4 == 3:
                yield
        for part in range(2):
            for low, high, place in (
                (SEL, SEL + last // 2, SEL),
                (SEL + last // 2, SEL + last, SEL + last // 2),
                (last, last + SEL, 0),
                (SEL, 2 * SEL, SEL + last),
            ):
                value = wide_ref[part, low:high, :].astype(BF16)
                work_ref[part, place : place + high - low, :] = value
                snap_ref[step - start, part, place : place + high - low, :] = value
                if place in (SEL, SEL + last // 2):
                    yield
            snap_ref[step - start, part, last + 2 * SEL :, :] = jnp.zeros(
                (SLOTS * SEL - last - 2 * SEL, CELLS), BF16
            )

    def multiply(step, work_ref):
        group = first_group(step)
        beam = lax.div(group, 2)
        weight = ints_ref[beam, 2 * SEL].astype(F32)
        for half in range(2):
            base = exclusive(lax.rem(group, 2), half) * 8
            out = [None, None, None]
            for pair in range(4):
                same, turned = [], []
                for one in range(2):
                    centre = ints_ref[beam, SEL + base + pair * 2 + one]
                    rows = pl.ds(pl.multiple_of(centre * SEL, SEL), DOF)
                    real = work_ref[0, rows, :]
                    imag = work_ref[1, rows, :]
                    same.append(jnp.concatenate([real, imag], 1))
                    turned.append(jnp.concatenate([imag, -real], 1))
                left = jnp.concatenate([same[0], turned[0], same[1], turned[1]], 0)
                right = jnp.concatenate([same[0], same[1], blank], 0)
                gram = lax.dot_general(
                    left, right, TRANSPOSED, preferred_element_type=F32
                )
                packed = jnp.where(
                    lower,
                    jnp.where(lane < DOF, gram[:DOF], gram[2 * DOF : 3 * DOF]),
                    jnp.where(lane < DOF, gram[DOF : 2 * DOF], gram[3 * DOF :]),
                )
                shift = 2 * DOF * pair % LANES
                if shift:
                    packed = pltpu.roll(packed, shift, 1)
                if pair == 0:
                    out[0] = packed
                elif pair == 1:
                    out[0] = jnp.where(lane >= 96, packed, out[0])
                    out[1] = packed
                elif pair == 2:
                    out[1] = jnp.where(lane >= 64, packed, out[1])
                    out[2] = packed
                else:
                    out[2] = jnp.where(lane >= 32, packed, out[2])
                yield
            place = 2 * step % 8 + half
            for part in range(3):
                out_ref[place, :, LANES * part : LANES * (part + 1)] = (
                    out[part] * weight
                )

    def run(*works):
        for _ in itertools.zip_longest(*works):
            pass

    works = (even_ref, odd_ref)
    run(turn(start, even_ref))
    for step in range(start, start + 3):
        run(
            turn(step + 1, works[(step + 1) % 2]), multiply(step, works[step % 2])
        )
    run(multiply(start + 3, odd_ref))


def edge_out_kernel(sent_ref, kept_ref, first_ref, second_ref):
    rows = 8 * 8
    lane = lane_ids(rows)
    ends = [jnp.zeros((rows, LANES), F32) for _ in range(2)]
    for step in range(OWN_BEAMS):
        snap_ref = sent_ref if step < 4 else kept_ref
        beam = lax.div(first_group(step), 2)
        for part in range(2):
            for block in range(8):
                low = SEL + rows * block
                value = snap_ref[step % 4, part, low : low + rows, :].astype(F32)
                target = 16 * block + 8 * part + beam
                here = lane == target
                for end in range(2):
                    moved = pltpu.roll(value, lax.rem(target + end, LANES), 1)
                    ends[end] = jnp.where(here, moved, ends[end])
    even = lax.rem(lax.axis_index("rng"), 2) == 0
    first_ref[...] = jnp.where(even, ends[1], ends[0]).astype(BF16)
    second_ref[...] = jnp.where(even, ends[0], ends[1]).astype(BF16)


def edge_in_kernel(first_ref, second_ref, out_ref):
    rows = 8 * 8
    last = PULSES * SEL
    lane = lane_ids(rows)
    first = first_ref[...].astype(F32)
    second = second_ref[...].astype(F32)

    def rolled(value, shift):
        return pltpu.roll(value, shift % LANES, 1) if shift % LANES else value

    for block in range(8):
        both = jnp.where(
            lane < 16, rolled(first, -16 * block), rolled(second, 16 - 16 * block)
        )
        for part, value in enumerate((both, rolled(both, -8))):
            value = value.astype(BF16)
            out_ref[part, SEL + rows * block : SEL + rows * (block + 1), :] = value
            if block == 0:
                out_ref[part, last + SEL : last + 2 * SEL, :] = value[:SEL]
            if block == 7:
                out_ref[part, :SEL, :] = value[rows - SEL :]
    for part in range(2):
        out_ref[part, last + 2 * SEL :, :] = jnp.zeros(
            (SLOTS * SEL - last - 2 * SEL, CELLS), BF16
        )


def spread(value, index):
    return jnp.take_along_axis(
        value, jnp.full(value.shape, index, jnp.int32), axis=1
    )


def solve_kernel(first_ref, second_ref, marks_ref, out_ref, turn_ref):
    lane = lane_ids(DOF)
    row = lax.broadcasted_iota(jnp.int32, (DOF, LANES), 0)
    slot = lax.div(lane, SEL)
    lower = row >= lane
    same = row == lane
    total = first_ref[...] + second_ref[...]
    parts = [total[:, LANES * i : LANES * (i + 1)] for i in range(3)]
    block_a = [None] * BINS
    block_b = [None] * BINS
    for pair in range(4):
        if pair == 0:
            packed = parts[0]
        elif pair == 1:
            packed = jnp.where(
                lane < 32, pltpu.roll(parts[0], 32, 1), pltpu.roll(parts[1], 32, 1)
            )
        elif pair == 2:
            packed = jnp.where(
                lane < 64, pltpu.roll(parts[1], 64, 1), pltpu.roll(parts[2], 64, 1)
            )
        else:
            packed = pltpu.roll(parts[2], 96, 1)
        square = jnp.concatenate([packed, jnp.zeros((LANES - DOF, LANES), F32)], 0)
        turned = jnp.transpose(square)
        for one in range(2):
            item = pair * 2 + one
            here = packed if one == 0 else pltpu.roll(packed, LANES - DOF, 1)
            there = turned[one * DOF : (one + 1) * DOF]
            value_a = jnp.where(lower, here, there)
            value_b = jnp.where(lower, jnp.where(same, 0.0, -there), here)
            if item:
                value_a = pltpu.roll(value_a, SEL * item, 1)
                value_b = pltpu.roll(value_b, SEL * item, 1)
            for part in range(BINS):
                if item == 0:
                    block_a[part] = value_a
                    block_b[part] = value_b
                else:
                    chosen = slot == (item + part) % 8
                    block_a[part] = jnp.where(chosen, value_a, block_a[part])
                    block_b[part] = jnp.where(chosen, value_b, block_b[part])
    for part in range(1, BINS):
        block_a[part] = pltpu.roll(block_a[part], LANES - SEL * part, 1)
        block_b[part] = pltpu.roll(block_b[part], LANES - SEL * part, 1)
    small = lane_ids(8)
    line = lax.broadcasted_iota(jnp.int32, (8, LANES), 0)
    place = lax.rem(small, SEL)
    base = small - place
    diagonal = jnp.zeros((8, LANES), F32)
    masks = []
    for group in range(DOF // 8):
        masks.append(place == line + group % 2 * 8)
        diagonal = diagonal + jnp.where(
            masks[group], block_a[group // 2][8 * group : 8 * group + 8], 0.0
        )
    level = jnp.sum(diagonal, axis=0, keepdims=True)
    level = jnp.broadcast_to(level, (8, LANES))
    for step in (1, 2, 4, 8):
        partner = base + lax.rem(place + step, SEL)
        level = level + jnp.take_along_axis(level, partner, axis=1)
    level = LOADING / DOF * level
    real = [[None] * 4 for _ in range(6)]
    imag = [[None] * 4 for _ in range(6)]
    for group in range(6):
        for part in range(BINS):
            real[group][part] = block_a[part][8 * group : 8 * group + 8]
            imag[group][part] = block_b[part][8 * group : 8 * group + 8]
        real[group][group // 2] = jnp.where(
            masks[group], real[group][group // 2] + level, real[group][group // 2]
        )
        real[group][3] = jnp.ones((8, LANES), F32)
        imag[group][3] = jnp.zeros((8, LANES), F32)
    inverse = [jnp.ones((8, LANES), F32)] * 6
    for k in range(0, DOF, 2):
        group, inner, part = k // 8, k % 8, k // SEL
        columns = []
        for step in range(2):
            index = base + k % SEL + step
            columns.append(
                [
                    [
                        jnp.take_along_axis(half[i][part], index, axis=1)
                        for i in range(6)
                    ]
                    for half in (real, imag)
                ]
            )
        (zero_re, zero_im), (one_re, one_im) = columns

        def line_of(value, offset):
            return jnp.broadcast_to(
                value[inner + offset : inner + offset + 1], (8, LANES)
            )

        side_re, side_im = line_of(one_re[group], 0), line_of(one_im[group], 0)
        below_re, below_im = line_of(zero_re[group], 1), line_of(zero_im[group], 1)
        first = 1.0 / line_of(zero_re[group], 0)
        below_re, below_im = below_re * first, below_im * first
        second = 1.0 / (
            line_of(one_re[group], 1) - below_re * side_re + below_im * side_im
        )
        upper, under = line == inner, line == inner + 1
        inverse[group] = jnp.where(
            upper, first, jnp.where(under, second, inverse[group])
        )
        zero_re[group] = jnp.where(upper, 0.0, zero_re[group])
        zero_im[group] = jnp.where(upper, 0.0, zero_im[group])
        alpha_re = [value * first for value in zero_re]
        alpha_im = [value * first for value in zero_im]
        beta_re = [
            (one_re[i] - alpha_re[i] * side_re + alpha_im[i] * side_im) * second
            for i in range(6)
        ]
        beta_im = [
            (one_im[i] - alpha_re[i] * side_im - alpha_im[i] * side_re) * second
            for i in range(6)
        ]
        beta_re[group] = jnp.where(under, 0.0, beta_re[group])
        beta_im[group] = jnp.where(under, 0.0, beta_im[group])
        for block in (*range(part, BINS), 3):
            row_re = line_of(real[group][block], 0)
            row_im = line_of(imag[group][block], 0)
            next_re = (
                line_of(real[group][block], 1) - below_re * row_re + below_im * row_im
            )
            next_im = (
                line_of(imag[group][block], 1) - below_re * row_im - below_im * row_re
            )
            for i in range(6):
                real[i][block] = (
                    real[i][block]
                    - alpha_re[i] * row_re
                    + alpha_im[i] * row_im
                    - beta_re[i] * next_re
                    + beta_im[i] * next_im
                )
                imag[i][block] = (
                    imag[i][block]
                    - alpha_re[i] * row_im
                    - alpha_im[i] * row_re
                    - beta_re[i] * next_im
                    - beta_im[i] * next_re
                )
    gap = jnp.zeros((SEL, LANES), F32)
    found_re = [real[i][3] * inverse[i] for i in range(6)]
    found_im = [imag[i][3] * inverse[i] for i in range(6)]
    quiet = found_re[0]
    for i in range(1, 6):
        quiet = quiet + found_re[i]
    quiet = jnp.broadcast_to(jnp.sum(quiet, axis=0, keepdims=True), (SEL, LANES))
    turn_ref[...] = jnp.transpose(
        jnp.concatenate([*found_re, quiet, *found_im, gap], 0)
    )
    found = turn_ref[pl.ds(0, 8, stride=SEL), :]
    out_ref[...] = jnp.where(small == 120, marks_ref[...], found)


def power_kernel(
    bins_ref, weights_ref, sent_ref, kept_ref, edge_ref,
    power_ref, first_ref, second_ref,
    count_ref,
):
    mine = own_group()
    even = lax.rem(lax.axis_index("rng"), 2) == 0
    small = lane_ids(8)
    counts = jnp.zeros((8, LANES), F32)
    for place in range(GROUPS):
        counts = counts + weights_ref[place]
    count_ref[...] = spread(counts, 120) * BLK
    low_lane = jnp.where(even, 16, 0)
    rows = SLOTS * SEL
    edge = edge_ref[...].reshape(2 * rows, LANES)
    for step in range(OWN_BEAMS):
        snap_ref = sent_ref if step < 4 else kept_ref
        beam = lax.div(first_group(step), 2)
        count = jnp.broadcast_to(count_ref[pl.ds(beam, 1), :], (8, LANES))
        lefts, quiets = [], []
        for group in (2 * beam, 2 * beam + 1):
            scaled = weights_ref[exclusive(mine, group)] * count
            quiets.append(spread(scaled, 56))
            away = small - bins_ref[group] * SEL
            left = [[], []]
            for tile in range(rows // LANES):
                index = away + LANES * tile
                inside = jnp.logical_and(index >= 0, index < DOF)
                direct = jnp.take_along_axis(
                    scaled, lax.bitwise_and(index, LANES - 1), axis=1
                )
                crossed = jnp.take_along_axis(
                    scaled, lax.bitwise_and(index + 64, LANES - 1), axis=1
                )
                direct = jnp.where(inside, direct, 0.0)
                crossed = jnp.where(inside, crossed, 0.0)
                left[0].append(jnp.concatenate([direct, -crossed], 0).astype(BF16))
                left[1].append(jnp.concatenate([crossed, direct], 0).astype(BF16))
            lefts.append(jnp.concatenate(left[0] + left[1], 1))
        right = jnp.concatenate([snap_ref[step % 4].reshape(2 * rows, LANES), edge], 1)
        found = jnp.dot(
            jnp.concatenate(lefts, 0), right, preferred_element_type=F32
        )
        found = found * found
        for half in range(2):
            power = found[16 * half : 16 * half + 8] + found[16 * half + 8 : 16 * half + 16]
            inner = power[:, :LANES] / quiets[half]
            outer = power[:, LANES:] / quiets[half]
            low = spread(outer, beam + low_lane)
            high = spread(outer, beam + 16 - low_lane)
            below = jnp.where(small == 0, low, pltpu.roll(inner, 1, 1))
            above = jnp.where(
                small == LANES - 1, high, pltpu.roll(inner, LANES - 1, 1)
            )
            power_ref[2 * beam + half] = below + inner + above
    even = lax.rem(lax.axis_index("az"), 2) == 0
    for half in range(2):
        bottom, top = power_ref[half], power_ref[GROUPS - 2 + half]
        first_ref[half] = jnp.where(even, top, bottom)
        second_ref[half] = jnp.where(even, bottom, top)


def smooth_kernel(power_ref, first_ref, second_ref, out_ref):
    even = lax.rem(lax.axis_index("az"), 2) == 0
    first, second = first_ref[...], second_ref[...]
    low = jnp.where(even, second, first)
    high = jnp.where(even, first, second)
    for beam in range(OWN_BEAMS):
        below = low if beam == 0 else power_ref[2 * beam - 2 : 2 * beam]
        above = (
            high if beam == OWN_BEAMS - 1 else power_ref[2 * beam + 2 : 2 * beam + 4]
        )
        here = power_ref[2 * beam : 2 * beam + 2]
        out_ref[2 * beam : 2 * beam + 2] = (below + here + above) / 9.0


def swap(value, turn):
    return lax.ppermute(value, "rng", [(i, i ^ turn) for i in range(32)])


def halo_columns(echoes):
    ring = [(i, (i + 1) % 8) for i in range(8)]
    low = lax.ppermute(echoes, "az", ring)
    high = lax.ppermute(echoes, "az", [(b, a) for a, b in ring])
    return low, high


SMEM = pl.BlockSpec(memory_space=pltpu.SMEM)
VMEM = pl.BlockSpec(memory_space=pltpu.VMEM)


def limit(mebibytes):
    return pltpu.CompilerParams(vmem_limit_bytes=mebibytes * 2**20)


def shape(*dims, dtype=F32):
    return jax.ShapeDtypeStruct(dims, dtype)


def neighbours(count, closed):
    nearest = [(i, i ^ 1) for i in range(count)]
    across = [(i, i + 1) if i % 2 else (i, i - 1) for i in range(count)]
    if closed:
        across = [(a, b % count) for a, b in across]
    else:
        across = [(a, b) for a, b in across if 0 <= b < count]
    return nearest, across


def body(echoes, arc_start, arc_offsets, doppler_bins, steer_angles, train_mask):
    low, high = halo_columns(echoes)
    az = lax.axis_index("az")

    def own(value):
        return lax.dynamic_slice_in_dim(value, az * OWN_BEAMS, OWN_BEAMS, 0)

    marks = jnp.broadcast_to(train_mask.astype(F32), (OWN_BEAMS, LANES))
    marks = marks + swap(marks, 28)
    first = (own(arc_start) - az * OWN_COLS + ARC // 2) % COLS
    ints = jnp.concatenate(
        [first[:, None] + own(arc_offsets), own(doppler_bins), train_mask], 1
    )
    angles = own(steer_angles)
    floats = jnp.concatenate([jnp.cos(angles), jnp.sin(angles)], 1)
    centres = jnp.broadcast_to(
        own(doppler_bins).reshape(GROUPS, 8, 1), (GROUPS, 8, LANES)
    )
    transform = pl.pallas_call(
        own_kernel,
        out_shape=(
            shape(OWN_COLS, 2 * PULSES, CELLS),
            shape(2 * PULSES, 2 * PULSES, dtype=BF16),
        ),
        in_specs=[VMEM, VMEM],
        out_specs=(VMEM, VMEM),
        compiler_params=limit(8),
        name="spectra",
    )
    spec, table = transform(jnp.asarray(table_array()), echoes)
    high, table = transform(table, high)
    half = shape(8, DOF, 8 * DOF)
    some = shape(OWN_BEAMS // 2, 2, SLOTS * SEL, CELLS, dtype=BF16)
    scratch = [
        pltpu.VMEM((2, (PULSES + 1) * SEL, CELLS), F32),
        pltpu.VMEM((2, (PULSES + 2) * SEL, CELLS), BF16),
        pltpu.VMEM((2, (PULSES + 2) * SEL, CELLS), BF16),
    ]
    sent, send, marks, spectrum = pl.pallas_call(
        send_kernel,
        out_shape=(
            some,
            half,
            shape(OWN_BEAMS, LANES),
            shape(3 * OWN_COLS, 2 * PULSES, CELLS),
        ),
        in_specs=[SMEM] * 2 + [VMEM] * 5,
        out_specs=(VMEM,) * 4,
        scratch_shapes=scratch,
        compiler_params=limit(16),
        name="grams_sent",
    )(ints, floats, table, low, spec, high, marks)
    moved = swap(send, 1)
    kept, keep = pl.pallas_call(
        keep_kernel,
        out_shape=(some, half),
        in_specs=[SMEM] * 2 + [VMEM],
        out_specs=(VMEM,) * 2,
        scratch_shapes=scratch,
        compiler_params=limit(16),
        name="grams_kept",
    )(ints, floats, spectrum)
    moved, keep, kept = lax.optimization_barrier((moved, keep, kept))
    part = keep + moved
    part, kept = lax.optimization_barrier((part, kept))
    edge = shape(64, LANES, dtype=BF16)
    edges = pl.pallas_call(
        edge_out_kernel,
        out_shape=(edge, edge),
        in_specs=[VMEM, VMEM],
        out_specs=(VMEM, VMEM),
        compiler_params=limit(8),
        name="edges_out",
    )(sent, kept)
    moved = [swap(part[2:4], 4), swap(part[4:6], 2), swap(part[6:], 6)]
    edges = [
        lax.ppermute(value, "rng", pairs)
        for value, pairs in zip(edges, neighbours(32, False))
    ]
    moved, edges[0] = lax.optimization_barrier((moved, edges[0]))
    part = part[:2] + moved[0] + moved[1] + moved[2]
    part = part[0] + swap(part[1], 8)
    other = swap(part, 28)
    weights = pl.pallas_call(
        solve_kernel,
        out_shape=shape(8, LANES),
        in_specs=[VMEM] * 3,
        out_specs=VMEM,
        scratch_shapes=[pltpu.VMEM((LANES, LANES), F32)],
        compiler_params=limit(8),
        name="solve",
    )(part, other, marks)
    weights, edges[1] = lax.optimization_barrier((weights, edges[1]))
    edges = pl.pallas_call(
        edge_in_kernel,
        out_shape=shape(2, SLOTS * SEL, LANES, dtype=BF16),
        in_specs=[VMEM, VMEM],
        out_specs=VMEM,
        compiler_params=limit(8),
        name="edges_in",
    )(*edges)
    weights = weights[None]
    for turn in (8, 4, 2, 1):
        moved = swap(weights, turn)
        if turn == 2:
            moved, edges, centres = lax.optimization_barrier((moved, edges, centres))
        weights = jnp.concatenate([weights, moved], 0)
    rim = shape(2, 8, CELLS)
    power, *rims = pl.pallas_call(
        power_kernel,
        out_shape=(shape(GROUPS, 8, CELLS), rim, rim),
        in_specs=[VMEM] * 5,
        out_specs=(VMEM,) * 3,
        scratch_shapes=[pltpu.VMEM((8, LANES), F32)],
        compiler_params=limit(12),
        name="power",
    )(centres, weights, sent, kept, edges)
    nearest, across = neighbours(8, True)
    second = lax.ppermute(rims[1], "az", across)
    second, first = lax.optimization_barrier(
        (second, lax.ppermute(rims[0], "az", nearest))
    )
    smoothed = pl.pallas_call(
        smooth_kernel,
        out_shape=shape(GROUPS, 8, CELLS),
        in_specs=[VMEM] * 3,
        out_specs=VMEM,
        compiler_params=limit(8),
        name="smooth",
    )(power, first, second)
    return smoothed.reshape(OWN_BEAMS, DBINS, CELLS)


def solution(mesh):
    return jax.shard_map(
        body,
        mesh=mesh,
        in_specs=(P(None, "az", None, "rng"), P(), P(), P(), P(), P("az", "rng")),
        out_specs=P("az", None, "rng"),
        check_vma=False,
    )
```

```python
import itertools

import jax
import jax.numpy as jnp
import numpy as np
from jax import lax
from jax.experimental import pallas as pl
from jax.experimental.pallas import tpu as pltpu
from jax.sharding import PartitionSpec as P

COLS = 256
ARC = 64
BINS = 3
BEAMS = 64
BLK = 128
PULSES = 32
SEL = 16
DBINS = 16
DOF = BINS * SEL
OWN_COLS = 32
OWN_BEAMS = 8
CELLS = 128
GROUPS = 16
LANES = 128
SLOTS = PULSES + 8
LOADING = 0.1
F32 = jnp.float32
BF16 = jnp.bfloat16
TRANSPOSED = (((1,), (1,)), ((), ()))


def table_array():
    ids = np.arange(PULSES)
    steps = (ids[:, None] * ids[None, :] % PULSES).astype(np.float32)
    angle = np.float32(-2.0 * np.pi / PULSES) * steps
    real, imag = np.cos(angle), np.sin(angle)
    return np.concatenate(
        [np.concatenate([real, -imag], 1), np.concatenate([imag, real], 1)], 0
    ).astype(jnp.bfloat16)


def lane_ids(rows):
    return lax.broadcasted_iota(jnp.int32, (rows, LANES), 1)


def own_group():
    place = lax.axis_index("rng")
    bits = [lax.rem(lax.div(place, 1 << bit), 2) for bit in range(5)]
    along = exclusive(bits[2], bits[4]) * 2 + exclusive(bits[3], bits[4])
    return bits[0] * 8 + bits[1] * 4 + along


def exclusive(left, right):
    return lax.bitwise_xor(left, right)


def spectra(table, ref, pair, out_ref, base):
    blocks = [
        jnp.concatenate([ref[0, 2 * pair + one], ref[1, 2 * pair + one]], 0)
        for one in range(2)
    ]
    both = jnp.dot(table, jnp.concatenate(blocks, 1), preferred_element_type=F32)
    out_ref[base + 2 * pair] = both[:, :CELLS]
    out_ref[base + 2 * pair + 1] = both[:, CELLS:]


def own_kernel(table_ref, own_ref, spec_ref, passed_ref):
    table = table_ref[...]
    passed_ref[...] = table

    def step(index, carry):
        for one in range(4):
            spectra(table, own_ref, 4 * index + one, spec_ref, 0)
        return carry

    lax.fori_loop(0, OWN_COLS // 8, step, 0)


def first_group(step):
    return exclusive(exclusive(2 * step, 8), own_group())


def send_kernel(
    ints_ref, floats_ref,
    table_ref, low_ref, own_ref, high_ref, marks_ref,
    snap_ref, send_ref, passed_ref, spec_ref,
    wide_ref, even_ref, odd_ref,
):
    table = table_ref[...]
    passed_ref[...] = marks_ref[...]

    for pair in range(OWN_COLS // 2):
        spectra(table, low_ref, pair, spec_ref, 0)
        for column in (2 * pair, 2 * pair + 1):
            spec_ref[OWN_COLS + column] = own_ref[column]
            spec_ref[2 * OWN_COLS + column] = high_ref[column]
    four_beams(
        0, ints_ref, floats_ref, spec_ref, snap_ref, send_ref, wide_ref, even_ref, odd_ref
    )


def keep_kernel(
    ints_ref, floats_ref, spec_ref,
    snap_ref, keep_ref,
    wide_ref, even_ref, odd_ref,
):
    four_beams(
        4, ints_ref, floats_ref, spec_ref, snap_ref, keep_ref, wide_ref, even_ref, odd_ref
    )


def four_beams(
    start, ints_ref, floats_ref, spec_ref, snap_ref, out_ref, wide_ref, even_ref, odd_ref
):
    lane = lane_ids(DOF)
    row = lax.broadcasted_iota(jnp.int32, (DOF, LANES), 0)
    lower = row >= lane - jnp.where(lane < DOF, 0, DOF)
    blank = jnp.zeros((LANES - 2 * DOF, 2 * CELLS), BF16)
    last = PULSES * SEL

    def turn(step, work_ref):
        beam = lax.div(first_group(step), 2)
        for sel in range(SEL):
            column = ints_ref[beam, sel]
            real = spec_ref[column, :PULSES]
            imag = spec_ref[column, PULSES:]
            cosine = floats_ref[beam, sel]
            sine = floats_ref[beam, SEL + sel]
            rows = pl.ds(SEL + sel, PULSES, stride=SEL)
            wide_ref[0, rows, :] = cosine * real - sine * imag
            wide_ref[1, rows, :] = sine * real + cosine * imag
            if sel % 4 == 3:
                yield
        for part in range(2):
            for low, high, place in (
                (SEL, SEL + last // 2, SEL),
                (SEL + last // 2, SEL + last, SEL + last // 2),
                (last, last + SEL, 0),
                (SEL, 2 * SEL, SEL + last),
            ):
                value = wide_ref[part, low:high, :].astype(BF16)
                work_ref[part, place : place + high - low, :] = value
                snap_ref[step - start, part, place : place + high - low, :] = value
                if place in (SEL, SEL + last // 2):
                    yield
            snap_ref[step - start, part, last + 2 * SEL :, :] = jnp.zeros(
                (SLOTS * SEL - last - 2 * SEL, CELLS), BF16
            )

    def multiply(step, work_ref):
        group = first_group(step)
        beam = lax.div(group, 2)
        weight = ints_ref[beam, 2 * SEL].astype(F32)
        for half in range(2):
            base = exclusive(lax.rem(group, 2), half) * 8
            out = [None, None, None]
            for pair in range(4):
                same, turned = [], []
                for one in range(2):
                    centre = ints_ref[beam, SEL + base + pair * 2 + one]
                    rows = pl.ds(pl.multiple_of(centre * SEL, SEL), DOF)
                    real = work_ref[0, rows, :]
                    imag = work_ref[1, rows, :]
                    same.append(jnp.concatenate([real, imag], 1))
                    turned.append(jnp.concatenate([imag, -real], 1))
                left = jnp.concatenate([same[0], turned[0], same[1], turned[1]], 0)
                right = jnp.concatenate([same[0], same[1], blank], 0)
                gram = lax.dot_general(
                    left, right, TRANSPOSED, preferred_element_type=F32
                )
                packed = jnp.where(
                    lower,
                    jnp.where(lane < DOF, gram[:DOF], gram[2 * DOF : 3 * DOF]),
                    jnp.where(lane < DOF, gram[DOF : 2 * DOF], gram[3 * DOF :]),
                )
                shift = 2 * DOF * pair % LANES
                if shift:
                    packed = pltpu.roll(packed, shift, 1)
                if pair == 0:
                    out[0] = packed
                elif pair == 1:
                    out[0] = jnp.where(lane >= 96, packed, out[0])
                    out[1] = packed
                elif pair == 2:
                    out[1] = jnp.where(lane >= 64, packed, out[1])
                    out[2] = packed
                else:
                    out[2] = jnp.where(lane >= 32, packed, out[2])
                yield
            place = 2 * step % 8 + half
            for part in range(3):
                out_ref[place, :, LANES * part : LANES * (part + 1)] = (
                    out[part] * weight
                )

    def run(*works):
        for _ in itertools.zip_longest(*works):
            pass

    works = (even_ref, odd_ref)
    run(turn(start, even_ref))
    for step in range(start, start + 3):
        run(
            turn(step + 1, works[(step + 1) % 2]), multiply(step, works[step % 2])
        )
    run(multiply(start + 3, odd_ref))


def edge_out_kernel(sent_ref, kept_ref, first_ref, second_ref):
    rows = 8 * 8
    lane = lane_ids(rows)
    ends = [jnp.zeros((rows, LANES), F32) for _ in range(2)]
    for step in range(OWN_BEAMS):
        snap_ref = sent_ref if step < 4 else kept_ref
        beam = lax.div(first_group(step), 2)
        for part in range(2):
            for block in range(8):
                low = SEL + rows * block
                value = snap_ref[step % 4, part, low : low + rows, :].astype(F32)
                target = 16 * block + 8 * part + beam
                here = lane == target
                for end in range(2):
                    moved = pltpu.roll(value, lax.rem(target + end, LANES), 1)
                    ends[end] = jnp.where(here, moved, ends[end])
    even = lax.rem(lax.axis_index("rng"), 2) == 0
    first_ref[...] = jnp.where(even, ends[1], ends[0]).astype(BF16)
    second_ref[...] = jnp.where(even, ends[0], ends[1]).astype(BF16)


def edge_in_kernel(first_ref, second_ref, out_ref):
    rows = 8 * 8
    last = PULSES * SEL
    lane = lane_ids(rows)
    first = first_ref[...].astype(F32)
    second = second_ref[...].astype(F32)

    def rolled(value, shift):
        return pltpu.roll(value, shift % LANES, 1) if shift % LANES else value

    for block in range(8):
        both = jnp.where(
            lane < 16, rolled(first, -16 * block), rolled(second, 16 - 16 * block)
        )
        for part, value in enumerate((both, rolled(both, -8))):
            value = value.astype(BF16)
            out_ref[part, SEL + rows * block : SEL + rows * (block + 1), :] = value
            if block == 0:
                out_ref[part, last + SEL : last + 2 * SEL, :] = value[:SEL]
            if block == 7:
                out_ref[part, :SEL, :] = value[rows - SEL :]
    for part in range(2):
        out_ref[part, last + 2 * SEL :, :] = jnp.zeros(
            (SLOTS * SEL - last - 2 * SEL, CELLS), BF16
        )


def spread(value, index):
    return jnp.take_along_axis(
        value, jnp.full(value.shape, index, jnp.int32), axis=1
    )


def solve_kernel(first_ref, second_ref, marks_ref, out_ref, turn_ref):
    lane = lane_ids(DOF)
    row = lax.broadcasted_iota(jnp.int32, (DOF, LANES), 0)
    slot = lax.div(lane, SEL)
    lower = row >= lane
    same = row == lane
    total = first_ref[...] + second_ref[...]
    parts = [total[:, LANES * i : LANES * (i + 1)] for i in range(3)]
    block_a = [None] * BINS
    block_b = [None] * BINS
    for pair in range(4):
        if pair == 0:
            packed = parts[0]
        elif pair == 1:
            packed = jnp.where(
                lane < 32, pltpu.roll(parts[0], 32, 1), pltpu.roll(parts[1], 32, 1)
            )
        elif pair == 2:
            packed = jnp.where(
                lane < 64, pltpu.roll(parts[1], 64, 1), pltpu.roll(parts[2], 64, 1)
            )
        else:
            packed = pltpu.roll(parts[2], 96, 1)
        square = jnp.concatenate([packed, jnp.zeros((LANES - DOF, LANES), F32)], 0)
        turned = jnp.transpose(square)
        for one in range(2):
            item = pair * 2 + one
            here = packed if one == 0 else pltpu.roll(packed, LANES - DOF, 1)
            there = turned[one * DOF : (one + 1) * DOF]
            value_a = jnp.where(lower, here, there)
            value_b = jnp.where(lower, jnp.where(same, 0.0, -there), here)
            if item:
                value_a = pltpu.roll(value_a, SEL * item, 1)
                value_b = pltpu.roll(value_b, SEL * item, 1)
            for part in range(BINS):
                if item == 0:
                    block_a[part] = value_a
                    block_b[part] = value_b
                else:
                    chosen = slot == (item + part) % 8
                    block_a[part] = jnp.where(chosen, value_a, block_a[part])
                    block_b[part] = jnp.where(chosen, value_b, block_b[part])
    for part in range(1, BINS):
        block_a[part] = pltpu.roll(block_a[part], LANES - SEL * part, 1)
        block_b[part] = pltpu.roll(block_b[part], LANES - SEL * part, 1)
    small = lane_ids(8)
    line = lax.broadcasted_iota(jnp.int32, (8, LANES), 0)
    place = lax.rem(small, SEL)
    base = small - place
    diagonal = jnp.zeros((8, LANES), F32)
    masks = []
    for group in range(DOF // 8):
        masks.append(place == line + group % 2 * 8)
        diagonal = diagonal + jnp.where(
            masks[group], block_a[group // 2][8 * group : 8 * group + 8], 0.0
        )
    level = jnp.sum(diagonal, axis=0, keepdims=True)
    level = jnp.broadcast_to(level, (8, LANES))
    for step in (1, 2, 4, 8):
        partner = base + lax.rem(place + step, SEL)
        level = level + jnp.take_along_axis(level, partner, axis=1)
    level = LOADING / DOF * level
    real = [[None] * 4 for _ in range(6)]
    imag = [[None] * 4 for _ in range(6)]
    for group in range(6):
        for part in range(BINS):
            real[group][part] = block_a[part][8 * group : 8 * group + 8]
            imag[group][part] = block_b[part][8 * group : 8 * group + 8]
        real[group][group // 2] = jnp.where(
            masks[group], real[group][group // 2] + level, real[group][group // 2]
        )
        real[group][3] = jnp.ones((8, LANES), F32)
        imag[group][3] = jnp.zeros((8, LANES), F32)
    inverse = [jnp.ones((8, LANES), F32)] * 6
    for k in range(0, DOF, 2):
        group, inner, part = k // 8, k % 8, k // SEL
        columns = []
        for step in range(2):
            index = base + k % SEL + step
            columns.append(
                [
                    [
                        jnp.take_along_axis(half[i][part], index, axis=1)
                        for i in range(6)
                    ]
                    for half in (real, imag)
                ]
            )
        (zero_re, zero_im), (one_re, one_im) = columns

        def line_of(value, offset):
            return jnp.broadcast_to(
                value[inner + offset : inner + offset + 1], (8, LANES)
            )

        side_re, side_im = line_of(one_re[group], 0), line_of(one_im[group], 0)
        below_re, below_im = line_of(zero_re[group], 1), line_of(zero_im[group], 1)
        first = 1.0 / line_of(zero_re[group], 0)
        below_re, below_im = below_re * first, below_im * first
        second = 1.0 / (
            line_of(one_re[group], 1) - below_re * side_re + below_im * side_im
        )
        upper, under = line == inner, line == inner + 1
        inverse[group] = jnp.where(
            upper, first, jnp.where(under, second, inverse[group])
        )
        zero_re[group] = jnp.where(upper, 0.0, zero_re[group])
        zero_im[group] = jnp.where(upper, 0.0, zero_im[group])
        alpha_re = [value * first for value in zero_re]
        alpha_im = [value * first for value in zero_im]
        beta_re = [
            (one_re[i] - alpha_re[i] * side_re + alpha_im[i] * side_im) * second
            for i in range(6)
        ]
        beta_im = [
            (one_im[i] - alpha_re[i] * side_im - alpha_im[i] * side_re) * second
            for i in range(6)
        ]
        beta_re[group] = jnp.where(under, 0.0, beta_re[group])
        beta_im[group] = jnp.where(under, 0.0, beta_im[group])
        for block in (*range(part, BINS), 3):
            row_re = line_of(real[group][block], 0)
            row_im = line_of(imag[group][block], 0)
            next_re = (
                line_of(real[group][block], 1) - below_re * row_re + below_im * row_im
            )
            next_im = (
                line_of(imag[group][block], 1) - below_re * row_im - below_im * row_re
            )
            for i in range(6):
                real[i][block] = (
                    real[i][block]
                    - alpha_re[i] * row_re
                    + alpha_im[i] * row_im
                    - beta_re[i] * next_re
                    + beta_im[i] * next_im
                )
                imag[i][block] = (
                    imag[i][block]
                    - alpha_re[i] * row_im
                    - alpha_im[i] * row_re
                    - beta_re[i] * next_im
                    - beta_im[i] * next_re
                )
    gap = jnp.zeros((SEL, LANES), F32)
    found_re = [real[i][3] * inverse[i] for i in range(6)]
    found_im = [imag[i][3] * inverse[i] for i in range(6)]
    quiet = found_re[0]
    for i in range(1, 6):
        quiet = quiet + found_re[i]
    quiet = jnp.broadcast_to(jnp.sum(quiet, axis=0, keepdims=True), (SEL, LANES))
    turn_ref[...] = jnp.transpose(
        jnp.concatenate([*found_re, quiet, *found_im, gap], 0)
    )
    found = turn_ref[pl.ds(0, 8, stride=SEL), :]
    out_ref[...] = jnp.where(small == 120, marks_ref[...], found)


def power_kernel(
    bins_ref, weights_ref, sent_ref, kept_ref, edge_ref,
    power_ref, first_ref, second_ref,
    count_ref,
):
    mine = own_group()
    even = lax.rem(lax.axis_index("rng"), 2) == 0
    small = lane_ids(8)
    counts = jnp.zeros((8, LANES), F32)
    for place in range(GROUPS):
        counts = counts + weights_ref[place]
    count_ref[...] = spread(counts, 120) * BLK
    low_lane = jnp.where(even, 16, 0)
    rows = SLOTS * SEL
    edge = edge_ref[...].reshape(2 * rows, LANES)
    for step in range(OWN_BEAMS):
        snap_ref = sent_ref if step < 4 else kept_ref
        beam = lax.div(first_group(step), 2)
        count = jnp.broadcast_to(count_ref[pl.ds(beam, 1), :], (8, LANES))
        lefts, quiets = [], []
        for group in (2 * beam, 2 * beam + 1):
            scaled = weights_ref[exclusive(mine, group)] * count
            quiets.append(spread(scaled, 56))
            away = small - bins_ref[group] * SEL
            left = [[], []]
            for tile in range(rows // LANES):
                index = away + LANES * tile
                inside = jnp.logical_and(index >= 0, index < DOF)
                direct = jnp.take_along_axis(
                    scaled, lax.bitwise_and(index, LANES - 1), axis=1
                )
                crossed = jnp.take_along_axis(
                    scaled, lax.bitwise_and(index + 64, LANES - 1), axis=1
                )
                direct = jnp.where(inside, direct, 0.0)
                crossed = jnp.where(inside, crossed, 0.0)
                left[0].append(jnp.concatenate([direct, -crossed], 0).astype(BF16))
                left[1].append(jnp.concatenate([crossed, direct], 0).astype(BF16))
            lefts.append(jnp.concatenate(left[0] + left[1], 1))
        right = jnp.concatenate([snap_ref[step % 4].reshape(2 * rows, LANES), edge], 1)
        found = jnp.dot(
            jnp.concatenate(lefts, 0), right, preferred_element_type=F32
        )
        found = found * found
        for half in range(2):
            power = found[16 * half : 16 * half + 8] + found[16 * half + 8 : 16 * half + 16]
            inner = power[:, :LANES] / quiets[half]
            outer = power[:, LANES:] / quiets[half]
            low = spread(outer, beam + low_lane)
            high = spread(outer, beam + 16 - low_lane)
            below = jnp.where(small == 0, low, pltpu.roll(inner, 1, 1))
            above = jnp.where(
                small == LANES - 1, high, pltpu.roll(inner, LANES - 1, 1)
            )
            power_ref[2 * beam + half] = below + inner + above
    even = lax.rem(lax.axis_index("az"), 2) == 0
    for half in range(2):
        bottom, top = power_ref[half], power_ref[GROUPS - 2 + half]
        first_ref[half] = jnp.where(even, top, bottom)
        second_ref[half] = jnp.where(even, bottom, top)


def smooth_kernel(power_ref, first_ref, second_ref, out_ref):
    even = lax.rem(lax.axis_index("az"), 2) == 0
    first, second = first_ref[...], second_ref[...]
    low = jnp.where(even, second, first)
    high = jnp.where(even, first, second)
    for beam in range(OWN_BEAMS):
        below = low if beam == 0 else power_ref[2 * beam - 2 : 2 * beam]
        above = (
            high if beam == OWN_BEAMS - 1 else power_ref[2 * beam + 2 : 2 * beam + 4]
        )
        here = power_ref[2 * beam : 2 * beam + 2]
        out_ref[2 * beam : 2 * beam + 2] = (below + here + above) / 9.0


def swap(value, turn):
    return lax.ppermute(value, "rng", [(i, i ^ turn) for i in range(32)])


def halo_columns(echoes):
    ring = [(i, (i + 1) % 8) for i in range(8)]
    low = lax.ppermute(echoes, "az", ring)
    high = lax.ppermute(echoes, "az", [(b, a) for a, b in ring])
    return low, high


SMEM = pl.BlockSpec(memory_space=pltpu.SMEM)
VMEM = pl.BlockSpec(memory_space=pltpu.VMEM)


def limit(mebibytes):
    return pltpu.CompilerParams(vmem_limit_bytes=mebibytes * 2**20)


def shape(*dims, dtype=F32):
    return jax.ShapeDtypeStruct(dims, dtype)


def neighbours(count, closed):
    nearest = [(i, i ^ 1) for i in range(count)]
    across = [(i, i + 1) if i % 2 else (i, i - 1) for i in range(count)]
    if closed:
        across = [(a, b % count) for a, b in across]
    else:
        across = [(a, b) for a, b in across if 0 <= b < count]
    return nearest, across


def body(echoes, arc_start, arc_offsets, doppler_bins, steer_angles, train_mask):
    low, high = halo_columns(echoes)
    az = lax.axis_index("az")

    def own(value):
        return lax.dynamic_slice_in_dim(value, az * OWN_BEAMS, OWN_BEAMS, 0)

    marks = jnp.broadcast_to(train_mask.astype(F32), (OWN_BEAMS, LANES))
    marks = marks + swap(marks, 28)
    first = (own(arc_start) - az * OWN_COLS + ARC // 2) % COLS
    ints = jnp.concatenate(
        [first[:, None] + own(arc_offsets), own(doppler_bins), train_mask], 1
    )
    angles = own(steer_angles)
    floats = jnp.concatenate([jnp.cos(angles), jnp.sin(angles)], 1)
    centres = jnp.broadcast_to(
        own(doppler_bins).reshape(GROUPS, 8, 1), (GROUPS, 8, LANES)
    )
    transform = pl.pallas_call(
        own_kernel,
        out_shape=(
            shape(OWN_COLS, 2 * PULSES, CELLS),
            shape(2 * PULSES, 2 * PULSES, dtype=BF16),
        ),
        in_specs=[VMEM, VMEM],
        out_specs=(VMEM, VMEM),
        compiler_params=limit(8),
        name="spectra",
    )
    spec, table = transform(jnp.asarray(table_array()), echoes)
    high, table = transform(table, high)
    half = shape(8, DOF, 8 * DOF)
    some = shape(OWN_BEAMS // 2, 2, SLOTS * SEL, CELLS, dtype=BF16)
    scratch = [
        pltpu.VMEM((2, (PULSES + 1) * SEL, CELLS), F32),
        pltpu.VMEM((2, (PULSES + 2) * SEL, CELLS), BF16),
        pltpu.VMEM((2, (PULSES + 2) * SEL, CELLS), BF16),
    ]
    sent, send, marks, spectrum = pl.pallas_call(
        send_kernel,
        out_shape=(
            some,
            half,
            shape(OWN_BEAMS, LANES),
            shape(3 * OWN_COLS, 2 * PULSES, CELLS),
        ),
        in_specs=[SMEM] * 2 + [VMEM] * 5,
        out_specs=(VMEM,) * 4,
        scratch_shapes=scratch,
        compiler_params=limit(16),
        name="grams_sent",
    )(ints, floats, table, low, spec, high, marks)
    moved = swap(send, 1)
    kept, keep = pl.pallas_call(
        keep_kernel,
        out_shape=(some, half),
        in_specs=[SMEM] * 2 + [VMEM],
        out_specs=(VMEM,) * 2,
        scratch_shapes=scratch,
        compiler_params=limit(16),
        name="grams_kept",
    )(ints, floats, spectrum)
    moved, keep, kept = lax.optimization_barrier((moved, keep, kept))
    part = keep + moved
    part, kept = lax.optimization_barrier((part, kept))
    edge = shape(64, LANES, dtype=BF16)
    edges = pl.pallas_call(
        edge_out_kernel,
        out_shape=(edge, edge),
        in_specs=[VMEM, VMEM],
        out_specs=(VMEM, VMEM),
        compiler_params=limit(8),
        name="edges_out",
    )(sent, kept)
    moved = [swap(part[4:6], 2), swap(part[6:], 6), swap(part[2:4], 4)]
    edges = [
        lax.ppermute(value, "rng", pairs)
        for value, pairs in zip(edges, neighbours(32, False))
    ]
    moved, edges[0] = lax.optimization_barrier((moved, edges[0]))
    part = part[:2] + moved[0] + moved[1] + moved[2]
    part = part[0] + swap(part[1], 8)
    other = swap(part, 28)
    weights = pl.pallas_call(
        solve_kernel,
        out_shape=shape(8, LANES),
        in_specs=[VMEM] * 3,
        out_specs=VMEM,
        scratch_shapes=[pltpu.VMEM((LANES, LANES), F32)],
        compiler_params=limit(8),
        name="solve",
    )(part, other, marks)
    weights, edges[1] = lax.optimization_barrier((weights, edges[1]))
    edges = pl.pallas_call(
        edge_in_kernel,
        out_shape=shape(2, SLOTS * SEL, LANES, dtype=BF16),
        in_specs=[VMEM, VMEM],
        out_specs=VMEM,
        compiler_params=limit(8),
        name="edges_in",
    )(*edges)
    weights = weights[None]
    for turn in (8, 4, 2, 1):
        moved = swap(weights, turn)
        if turn == 2:
            moved, edges, centres = lax.optimization_barrier((moved, edges, centres))
        weights = jnp.concatenate([weights, moved], 0)
    rim = shape(2, 8, CELLS)
    power, *rims = pl.pallas_call(
        power_kernel,
        out_shape=(shape(GROUPS, 8, CELLS), rim, rim),
        in_specs=[VMEM] * 5,
        out_specs=(VMEM,) * 3,
        scratch_shapes=[pltpu.VMEM((8, LANES), F32)],
        compiler_params=limit(12),
        name="power",
    )(centres, weights, sent, kept, edges)
    nearest, across = neighbours(8, True)
    second = lax.ppermute(rims[1], "az", across)
    second, first = lax.optimization_barrier(
        (second, lax.ppermute(rims[0], "az", nearest))
    )
    smoothed = pl.pallas_call(
        smooth_kernel,
        out_shape=shape(GROUPS, 8, CELLS),
        in_specs=[VMEM] * 3,
        out_specs=VMEM,
        compiler_params=limit(8),
        name="smooth",
    )(power, first, second)
    return smoothed.reshape(OWN_BEAMS, DBINS, CELLS)


def solution(mesh):
    return jax.shard_map(
        body,
        mesh=mesh,
        in_specs=(P(None, "az", None, "rng"), P(), P(), P(), P(), P("az", "rng")),
        out_specs=P("az", None, "rng"),
        check_vma=False,
    )
```
